32 devices in a mesh: gx: 8 (over z, x), gy: 4 (over y, core).
Axes of the slice: x: 2, y: 2, z: 4, core: 2. Of those that a mesh axis runs over, the one named last changes fastest.
Arguments:
- model_image: float32 [128, 64, 128], P('gx', 'gy'), may hold values from -6 to 6
- data_residual: float32 [128, 64, 2048], P('gx', 'gy'), may hold values from -6 to 6
- direction: float32 [128, 64, 128], P('gx', 'gy'), may hold values from -6 to 6
- old_gradient: float32 [128, 64, 128], P('gx', 'gy'), may hold values from -18 to 18
- aperture: int32 [128, 64, 16], P('gx', 'gy'), may hold values from 0 to 288
- travel_times: int32 [128, 64, 16, 128], P('gx', 'gy'), may hold values from 0 to 2047, as said below
- amplitude: float32 [128, 64, 16], P('gx', 'gy'), may hold values from 0.02 to 0.2
- trace_counts: int32 [128, 64], P('gx', 'gy'), may hold values from 1 to 24
Outputs:
- new_image: float32 [128, 64, 128], P('gx', 'gy')
- new_residual: float32 [128, 64, 2048], P('gx', 'gy')
- new_direction: float32 [128, 64, 128], P('gx', 'gy')
The draws below stay inside these ranges and needn't reach their ends.
Inputs may be any that keep to these rules, and one draw needn't show every extreme that they name: `travel_times`: along each aperture entry the time sample index never decreases with depth.
All inputs are finite; a program needn't handle non-finite values.
Results may differ from the reference program's by a relative error of at most 0.0003.
Values sent between devices are 32-bit elements; how exact they have to be, the bound alone decides.
No kernel may reach another device: no remote copies, remote signals or barrier semaphores. Data moves between devices by JAX's collectives and lax.ppermute only.
A program may use at most 64 MiB of HBM per device.

```python
import jax
import jax.numpy as jnp
from jax import lax

DEPTHS = 128
SAMPLES = 2048
ENTRIES = 16
RADIUS = 8
GRID_X = 128
GRID_Y = 64


def draw_travel_times(key, part):
    key = jax.random.fold_in(key, 11)
    key_start, key_steps = jax.random.split(key)
    start = jax.random.randint(key_start, (GRID_X, GRID_Y, ENTRIES, 1), 0, SAMPLES // 3 + 1)
    step_top = max(3, 3 * SAMPLES // (2 * DEPTHS))
    steps = jax.random.randint(key_steps, (GRID_X, GRID_Y, ENTRIES, DEPTHS), 1, step_top)
    entry = jnp.arange(ENTRIES, dtype=jnp.int32)[None, None, :, None]
    depth = jnp.arange(DEPTHS, dtype=jnp.int32)[None, None, None, :]
    steps = jnp.where(depth == 0, 0, steps)
    start = jnp.where(entry == 0, 0, start)
    times = jnp.minimum(start + jnp.cumsum(steps, axis=3), SAMPLES - 1)
    times = jnp.where((entry == ENTRIES - 1) & (depth == DEPTHS - 1), SAMPLES - 1, times)
    return times.astype(jnp.int32)


def with_ends(drawn, stream_key, low, high):
    shape = drawn.shape
    index_at = [jax.random.randint(jax.random.fold_in(stream_key, axis), (), 0, shape[axis]) for axis in range(len(shape))]
    drawn = drawn.at[tuple(index_at)].set(low)
    longest = shape.index(max(shape))
    index_at[longest] = (index_at[longest] + 1) % shape[longest]
    return drawn.at[tuple(index_at)].set(high)


def level_of(rng, dims, pieces, least, high):
    factor_of = 1.0
    for axis_at, parts in pieces:
        steps = jax.random.uniform(jax.random.fold_in(jax.random.fold_in(rng, 6), axis_at), (parts,), jnp.float32, least / len(pieces), high / len(pieces))
        factor_of = factor_of * jnp.repeat(jnp.exp(steps), dims[axis_at] // parts).reshape((-1,) + (1,) * (len(dims) - 1 - axis_at))
    return factor_of


def normal_values(own_key, extent, scale, limit, pieces=(), kind=jnp.bfloat16):
    gain = level_of(own_key, extent, pieces, -0.22, 0.18) if pieces else 1.0
    result = jax.random.normal(own_key, extent, jnp.float32) * scale * gain
    return jnp.minimum(jnp.maximum(result, -limit), limit).astype(kind)


def setup_inputs(seed: int = 0) -> dict:
    keys = jax.random.split(jax.random.key(seed), 9)
    return {
        "model_image": normal_values(keys[0], (GRID_X, GRID_Y, DEPTHS), 1.0, 6.0, ((0, 8), (1, 4)), jnp.float32),
        "data_residual": normal_values(keys[1], (GRID_X, GRID_Y, SAMPLES), 1.0, 6.0, ((0, 8), (1, 4)), jnp.float32),
        "direction": normal_values(keys[2], (GRID_X, GRID_Y, DEPTHS), 1.0, 6.0, ((0, 8), (1, 4)), jnp.float32),
        "old_gradient": normal_values(keys[3], (GRID_X, GRID_Y, DEPTHS), 3.0, 18.0, ((0, 8), (1, 4)), jnp.float32),
        "aperture": with_ends(jax.random.randint(keys[4], (GRID_X, GRID_Y, ENTRIES), 0, (2 * RADIUS + 1) * (2 * RADIUS + 1)), jax.random.fold_in(keys[4], 1), 0, ((2 * RADIUS + 1) * (2 * RADIUS + 1)) - 1).astype(jnp.int32),
        "travel_times": draw_travel_times(jax.random.fold_in(keys[8], 71), 0),
        "amplitude": jnp.clip(0.02 + 0.18 * jax.random.uniform(keys[6], (GRID_X, GRID_Y, ENTRIES), jnp.float32) ** level_of(keys[6], (GRID_X, GRID_Y, ENTRIES), ((0, 8), (1, 4)), -0.2, 0.2), 0.02, 0.2),
        "trace_counts": with_ends(jax.random.randint(keys[7], (GRID_X, GRID_Y), 1, 25), jax.random.fold_in(keys[7], 1), 1, 24).astype(jnp.int32),
    }


def row_indices(offs_row):
    side = 2 * RADIUS + 1
    off_x = offs_row // side
    off_y = offs_row % side
    cols_y = jnp.arange(GRID_Y, dtype=jnp.int32)[:, None]
    return (off_x * (GRID_Y + 2 * RADIUS) + cols_y + off_y).astype(jnp.int32)


def demigrate(image, aperture, travel_times, weight):
    padded = jnp.pad(image, ((RADIUS, RADIUS), (RADIUS, RADIUS), (0, 0)))
    starts = jnp.arange(GRID_X, dtype=jnp.int32)

    def one_row(item):
        offs_row, tt_row, w_row, start = item
        window = lax.dynamic_slice_in_dim(padded, start, 2 * RADIUS + 1, 0).reshape(-1, DEPTHS)
        gathered = window[row_indices(offs_row)] * w_row[:, :, None]
        flat_index = (jnp.arange(GRID_Y, dtype=jnp.int32) * SAMPLES)[:, None, None] + tt_row
        traces = jnp.zeros((GRID_Y * SAMPLES,), jnp.float32).at[flat_index.reshape(-1)].add(gathered.reshape(-1))
        return traces.reshape(GRID_Y, SAMPLES)

    return lax.map(one_row, (aperture, travel_times, weight, starts))


def migrate(residual, aperture, travel_times, weight):
    padded = jnp.zeros((GRID_X + 2 * RADIUS, GRID_Y + 2 * RADIUS, DEPTHS), jnp.float32)
    starts = jnp.arange(GRID_X, dtype=jnp.int32)

    def one_row(carry, item):
        res_row, offs_row, tt_row, w_row, start = item
        sampled = jnp.take_along_axis(res_row, tt_row.reshape(GRID_Y, -1), axis=1)
        sampled = sampled.reshape(GRID_Y, ENTRIES, DEPTHS) * w_row[:, :, None]
        window = jnp.zeros(((2 * RADIUS + 1) * (GRID_Y + 2 * RADIUS), DEPTHS), jnp.float32)
        window = window.at[row_indices(offs_row).reshape(-1)].add(sampled.reshape(-1, DEPTHS))
        window = window.reshape(2 * RADIUS + 1, GRID_Y + 2 * RADIUS, DEPTHS)
        zero = jnp.zeros((), jnp.int32)
        current = lax.dynamic_slice(carry, (start, zero, zero), window.shape)
        return lax.dynamic_update_slice(carry, current + window, (start, zero, zero)), None

    padded, unused = lax.scan(one_row, padded, (residual, aperture, travel_times, weight, starts))
    return padded[RADIUS:RADIUS + GRID_X, RADIUS:RADIUS + GRID_Y]


def reference(model_image, data_residual, direction, old_gradient, aperture, travel_times, amplitude, trace_counts):
    weight = amplitude * trace_counts.astype(jnp.float32)[:, :, None]
    gamma = jnp.sum(old_gradient * old_gradient)
    image_data = demigrate(direction, aperture, travel_times, weight)
    curvature = jnp.sum(image_data * image_data)
    alpha = gamma / curvature
    new_image = model_image + alpha * direction
    new_residual = data_residual - alpha * image_data
    gradient = migrate(new_residual, aperture, travel_times, weight)
    gamma_new = jnp.sum(gradient * gradient)
    new_direction = gradient + (gamma_new / gamma) * direction
    return new_image, new_residual, new_direction
```

```python
import functools

import jax
import jax.numpy as jnp
from jax import lax
from jax.experimental import pallas as pl
from jax.experimental.pallas import tpu as pltpu
from jax.sharding import PartitionSpec as P

RADIUS = 8
SIDE = 2 * RADIUS + 1
LANES = 128
SUB = 8
F32 = jnp.float32
BF16 = jnp.bfloat16
VMEM_LIMIT = 48 * 1024 * 1024


def params(**extra):
    return pltpu.CompilerParams(vmem_limit_bytes=VMEM_LIMIT, **extra)


def to_rows(traces):
    bins_x, bins_y, samples = traces.shape
    parts = traces.reshape(bins_x, bins_y // SUB, SUB, samples // LANES, LANES)
    return parts.transpose(0, 1, 3, 2, 4).reshape(-1, LANES)


def from_rows(rows, shape):
    bins_x, bins_y, samples = shape
    parts = rows.reshape(bins_x, bins_y // SUB, samples // LANES, SUB, LANES)
    return parts.transpose(0, 1, 3, 2, 4).reshape(shape)


def trace_row(b, highs):
    return (b // SUB) * (SUB * highs) + b % SUB


def sample_row(res_ref, times_ref, wt_ref, vals, bins_y, entries, highs):
    for b in range(bins_y):
        times = times_ref[b]
        high = times // LANES
        low = times % LANES
        acc = jnp.zeros(times.shape, F32)
        first = trace_row(b, highs)
        for h in range(highs):
            row = res_ref[pl.ds(first + SUB * h, 1), :]
            table = jnp.broadcast_to(row, times.shape)
            got = jnp.take_along_axis(table, low, axis=1, mode="promise_in_bounds")
            acc = jnp.where(high == h, got, acc)
        vals[pl.ds(b * entries, entries), :] = acc * wt_ref[0][:, b : b + 1]


def spread_row(vals, place_ref, s_ref, row, wide_y, span):
    value = vals[...]
    upper = value.astype(BF16)
    lower = (value - upper.astype(F32)).astype(BF16)
    both = jnp.concatenate([upper, lower], axis=1)
    place = place_ref[0]
    step = 32
    for m in range(0, span, step):
        iota = lax.broadcasted_iota(jnp.int32, (step, place.shape[1]), 0) + m
        table = jnp.where(iota == place, 1.0, 0.0).astype(BF16)
        part = jnp.dot(table, both, preferred_element_type=F32)
        at = pl.ds(pl.multiple_of(row * wide_y + m, SUB), step)
        s_ref[at, :] += part[:, :LANES] + part[:, LANES:]


def first_kernel(geo, row0, res_ref, times_ref, wt_ref, place_ref, prev_ref, s_ref, vals):
    bins_y, entries, highs, wide_y = geo
    step = pl.program_id(0)

    @pl.when(step == 0)
    def _():
        s_ref[...] = prev_ref[...]

    sample_row(res_ref, times_ref, wt_ref, vals, bins_y, entries, highs)
    spread_row(vals, place_ref, s_ref, step + row0, wide_y, SIDE * wide_y)


def main_kernel(
    geo,
    unroll,
    col_ref,
    weight_ref,
    times_ref,
    wt_ref,
    place_ref,
    mid_ref,
    left_ref,
    right_ref,
    s1_ref,
    data_ref,
    curv_ref,
    out_left,
    out_mid,
    out_right,
    image,
    s_ref,
    vals,
    work,
):
    bins_y, entries, highs, wide_y = geo
    step = pl.program_id(0)
    wide_x = mid_ref.shape[0]

    @pl.when(step == 0)
    def _():
        s_ref[...] = jnp.zeros_like(s_ref)
        curv_ref[...] = jnp.zeros_like(curv_ref)
        for x in range(wide_x):
            image[pl.ds(x * wide_y, RADIUS), :] = left_ref[x]
            image[pl.ds(x * wide_y + RADIUS, bins_y), :] = mid_ref[x]
            image[pl.ds(x * wide_y + RADIUS + bins_y, RADIUS), :] = right_ref[x]

    half = LANES // 2
    iota_lo = lax.broadcasted_iota(jnp.int32, (half, LANES), 0).astype(F32).astype(BF16)
    iota_hi = lax.broadcasted_iota(jnp.int32, (2 * highs, LANES), 0).astype(F32).astype(BF16)
    zero = jnp.zeros((), BF16)
    one = jnp.ones((), BF16)

    def one_bin(b, slot):
        for e in range(entries):
            column = col_ref[0, b, e]
            work[slot, 0, pl.ds(e, 1), :] = image[pl.ds(column, 1), :] * weight_ref[0, b, e]
        value = work[slot, 0]
        upper = value.astype(BF16).astype(F32)
        work[slot, 0] = upper
        work[slot, 1] = value - upper
        times = times_ref[b]
        work[slot, 2] = (times % half).astype(F32)
        work[slot, 3] = (times // LANES + ((times // half) % 2) * highs).astype(F32)
        lefts = []
        rights = []
        for e in range(entries):

            def wide(k, rows):
                row = work[slot, k, pl.ds(e, 1), :]
                return jnp.broadcast_to(
                    jnp.broadcast_to(row, (16, LANES)).astype(BF16)[None], (rows // 16, 16, LANES)
                ).reshape(rows, LANES)

            hit = wide(3, 2 * highs) == iota_hi
            lefts.append(
                jnp.concatenate(
                    [
                        jnp.where(hit, wide(0, 2 * highs), zero),
                        jnp.where(hit, wide(1, 2 * highs), zero),
                    ],
                    axis=0,
                )
            )
            rights.append(jnp.where(wide(2, half) == iota_lo, one, zero))
        out = lax.dot_general(
            jnp.concatenate(lefts, axis=1),
            jnp.concatenate(rights, axis=1),
            (((1,), (1,)), ((), ())),
            preferred_element_type=F32,
        )
        out = out[: 2 * highs] + out[2 * highs :]
        trace = jnp.concatenate([out[:highs], out[highs:]], axis=1)
        data_ref[pl.ds(trace_row(b, highs), highs, stride=SUB), :] = trace
        return trace * trace

    def some_bins(k, total):
        for u in range(unroll):
            total = total + one_bin(k * unroll + u, u)
        return total

    total = lax.fori_loop(0, bins_y // unroll, some_bins, jnp.zeros((highs, LANES), F32))
    curv_ref[...] += total
    sample_row(data_ref, times_ref, wt_ref, vals, bins_y, entries, highs)
    spread_row(vals, place_ref, s_ref, step, wide_y, SIDE * wide_y)

    @pl.when(step == pl.num_programs(0) - 1)
    def _():
        for k, ref in enumerate((s1_ref, s_ref)):
            for x in range(wide_x):
                out_left[k, x] = ref[pl.ds(x * wide_y, RADIUS), :]
                out_mid[k, x] = ref[pl.ds(x * wide_y + RADIUS, bins_y), :]
                out_right[k, x] = ref[pl.ds(x * wide_y + RADIUS + bins_y, RADIUS), :]


def fold_y_kernel(mid_ref, low_ref, high_ref, out_head, out_mid, out_tail):
    wide_x, bins_y = mid_ref.shape[1], mid_ref.shape[2]
    bins_x = wide_x - 2 * RADIUS
    for k in range(2):
        for x in range(wide_x):
            if x < RADIUS:
                ref, at = out_head, x
            elif x < RADIUS + bins_x:
                ref, at = out_mid, x - RADIUS
            else:
                ref, at = out_tail, x - RADIUS - bins_x
            ref[k, at, pl.ds(0, RADIUS), :] = mid_ref[k, x, pl.ds(0, RADIUS), :] + low_ref[k, x]
            high = pl.ds(bins_y - RADIUS, RADIUS)
            ref[k, at, high, :] = mid_ref[k, x, high, :] + high_ref[k, x]


def fold_x_kernel(mid_ref, low_ref, high_ref, grad_ref, curv_ref, out_ref, stats_ref):
    bins_x = mid_ref.shape[1]
    sums = [jnp.zeros((1, LANES), F32) for _ in range(5)]
    for x in range(bins_x):
        pair = []
        for k in range(2):
            cells = mid_ref[k, x]
            if x < RADIUS:
                cells = cells + low_ref[k, x]
            else:
                cells = cells + high_ref[k, x - RADIUS]
            out_ref[k, x] = cells
            pair.append(cells)
        old = grad_ref[x]
        terms = (old * old, None, pair[0] * pair[0], pair[0] * pair[1], pair[1] * pair[1])
        for n, term in enumerate(terms):
            if term is not None:
                sums[n] = sums[n] + jnp.sum(term, axis=0, keepdims=True)
    sums[1] = jnp.sum(curv_ref[...], axis=0, keepdims=True)
    lane = lax.broadcasted_iota(jnp.int32, (1, LANES), 1)
    stats = jnp.zeros((1, LANES), F32)
    for n, term in enumerate(sums):
        stats = jnp.where(lane == n, jnp.sum(term, axis=1, keepdims=True), stats)
    stats_ref[...] = stats


def last_kernel(
    stats_ref, res_ref, data_ref, model_ref, dir_ref, grad_ref, new_image, new_residual, new_dir
):
    stats = jnp.sum(stats_ref[...], axis=0, keepdims=True)
    lane = lax.broadcasted_iota(jnp.int32, stats.shape, 1)

    def pick(n):
        return jnp.sum(jnp.where(lane == n, stats, 0.0), axis=1, keepdims=True)

    gamma, curvature, one_one, one_two, two_two = (pick(n) for n in range(5))
    alpha = gamma / curvature
    gamma_new = one_one - 2.0 * (alpha * one_two) + alpha * (alpha * two_two)
    beta = gamma_new / gamma
    new_residual[...] = res_ref[...] - alpha * data_ref[...]
    step = dir_ref[...]
    new_image[...] = model_ref[...] + alpha[None] * step
    new_dir[...] = (grad_ref[0] - alpha[None] * grad_ref[1]) + beta[None] * step


def shift(cells, axis, by):
    count = lax.axis_size(axis)
    pairs = [(i, i + by) for i in range(count) if 0 <= i + by < count]
    return lax.ppermute(cells, axis, pairs)


def body(
    model_image,
    data_residual,
    direction,
    old_gradient,
    aperture,
    travel_times,
    amplitude,
    trace_counts,
):
    bins_x, bins_y, samples = data_residual.shape
    entries, depths = travel_times.shape[2], travel_times.shape[3]
    highs = samples // LANES
    wide_x, wide_y = bins_x + 2 * RADIUS, bins_y + 2 * RADIUS
    columns = wide_x * wide_y
    span = SIDE * wide_y
    geo = (bins_y, entries, highs, wide_y)
    rows_per = bins_y * highs

    from_prev = shift(direction[bins_x - RADIUS :], "gx", 1)
    from_next = shift(direction[:RADIUS], "gx", -1)

    times = travel_times.reshape(bins_x * bins_y, entries, depths)
    res_rows = to_rows(data_residual)
    weight = amplitude * trace_counts.astype(F32)[:, :, None]
    weight_t = weight.transpose(0, 2, 1)
    off = (aperture // SIDE) * wide_y + aperture % SIDE
    window = off + jnp.arange(bins_y, dtype=jnp.int32)[None, :, None]
    column = window + wide_y * jnp.arange(bins_x, dtype=jnp.int32)[:, None, None]
    place = window.reshape(bins_x, 1, bins_y * entries)

    def first(row0, count, prev):
        return pl.pallas_call(
            functools.partial(first_kernel, geo, row0),
            grid=(count,),
            in_specs=[
                pl.BlockSpec((rows_per, LANES), lambda i: (i + row0, 0)),
                pl.BlockSpec((bins_y, entries, depths), lambda i: (i + row0, 0, 0)),
                pl.BlockSpec((1, entries, bins_y), lambda i: (i + row0, 0, 0)),
                pl.BlockSpec((1, 1, bins_y * entries), lambda i: (i + row0, 0, 0)),
                pl.BlockSpec((columns, depths), lambda i: (0, 0)),
            ],
            out_specs=pl.BlockSpec((columns, depths), lambda i: (0, 0)),
            out_shape=jax.ShapeDtypeStruct((columns, depths), F32),
            scratch_shapes=[pltpu.VMEM((bins_y * entries, depths), F32)],
            compiler_params=params(),
            cost_estimate=pl.CostEstimate(
                flops=4 * 10**9, bytes_accessed=4 * 10**6, transcendentals=0
            ),
            name="sample_residual",
        )(res_rows, times, weight_t, place, prev)

    s1 = first(0, bins_x // 2, jnp.zeros((columns, depths), F32))
    ext = jnp.concatenate([from_prev, direction, from_next], axis=0)
    left = shift(ext[:, bins_y - RADIUS :], "gy", 1)
    right = shift(ext[:, :RADIUS], "gy", -1)
    s1 = first(bins_x // 2, bins_x - bins_x // 2, s1)

    unroll = 4
    whole3 = lambda i: (0, 0, 0)
    whole4 = lambda i: (0, 0, 0, 0)
    strip = (2, wide_x, RADIUS, depths)
    middle = (2, wide_x, bins_y, depths)
    data_rows, curv, out_left, out_mid, out_right = pl.pallas_call(
        functools.partial(main_kernel, geo, unroll),
        grid=(bins_x,),
        in_specs=[
            pl.BlockSpec((1, bins_y, entries), lambda i: (i, 0, 0), memory_space=pltpu.SMEM),
            pl.BlockSpec((1, bins_y, entries), lambda i: (i, 0, 0), memory_space=pltpu.SMEM),
            pl.BlockSpec((bins_y, entries, depths), lambda i: (i, 0, 0)),
            pl.BlockSpec((1, entries, bins_y), lambda i: (i, 0, 0)),
            pl.BlockSpec((1, 1, bins_y * entries), lambda i: (i, 0, 0)),
            pl.BlockSpec((wide_x, bins_y, depths), whole3),
            pl.BlockSpec((wide_x, RADIUS, depths), whole3),
            pl.BlockSpec((wide_x, RADIUS, depths), whole3),
            pl.BlockSpec((columns, depths), lambda i: (0, 0)),
        ],
        out_specs=[
            pl.BlockSpec((rows_per, LANES), lambda i: (i, 0)),
            pl.BlockSpec((highs, LANES), lambda i: (0, 0)),
            pl.BlockSpec(strip, whole4),
            pl.BlockSpec(middle, whole4),
            pl.BlockSpec(strip, whole4),
        ],
        out_shape=[
            jax.ShapeDtypeStruct((bins_x * rows_per, LANES), F32),
            jax.ShapeDtypeStruct((highs, LANES), F32),
            jax.ShapeDtypeStruct(strip, F32),
            jax.ShapeDtypeStruct(middle, F32),
            jax.ShapeDtypeStruct(strip, F32),
        ],
        scratch_shapes=[
            pltpu.VMEM((columns, depths), F32),
            pltpu.VMEM((columns, depths), F32),
            pltpu.VMEM((bins_y * entries, depths), F32),
            pltpu.VMEM((unroll, 4, entries, LANES), F32),
        ],
        compiler_params=params(),
        cost_estimate=pl.CostEstimate(
            flops=20 * 10**9, bytes_accessed=8 * 10**6, transcendentals=0
        ),
        name="demigrate_and_sample",
    )(column, weight, times, weight_t, place, ext, left, right, s1)

    from_low = shift(out_right, "gy", 1)
    from_high = shift(out_left, "gy", -1)
    edge = jax.ShapeDtypeStruct((2, RADIUS, bins_y, depths), F32)
    out_head, inner, out_tail = pl.pallas_call(
        fold_y_kernel,
        out_shape=[edge, jax.ShapeDtypeStruct((2, bins_x, bins_y, depths), F32), edge],
        compiler_params=params(),
        name="fold_y",
    )(out_mid, from_low, from_high)
    from_low = shift(out_tail, "gx", 1)
    from_high = shift(out_head, "gx", -1)
    grads, stats = pl.pallas_call(
        fold_x_kernel,
        out_shape=[
            jax.ShapeDtypeStruct((2, bins_x, bins_y, depths), F32),
            jax.ShapeDtypeStruct((1, LANES), F32),
        ],
        compiler_params=params(),
        name="fold_x",
    )(inner, from_low, from_high, old_gradient, curv)
    stats = lax.all_gather(stats, ("gx", "gy"), axis=0, tiled=True)

    steps = 8
    rows_step = bins_x * rows_per // steps
    x_step = bins_x // steps
    cells = pl.BlockSpec((x_step, bins_y, depths), lambda i: (i, 0, 0))
    rows = pl.BlockSpec((rows_step, LANES), lambda i: (i, 0))
    image_shape = jax.ShapeDtypeStruct(direction.shape, F32)
    new_image, new_rows, new_direction = pl.pallas_call(
        last_kernel,
        grid=(steps,),
        in_specs=[
            pl.BlockSpec(stats.shape, lambda i: (0, 0)),
            rows,
            rows,
            cells,
            cells,
            pl.BlockSpec((2, x_step, bins_y, depths), lambda i: (0, i, 0, 0)),
        ],
        out_specs=[cells, rows, cells],
        out_shape=[image_shape, jax.ShapeDtypeStruct(res_rows.shape, F32), image_shape],
        compiler_params=params(),
        name="update",
    )(stats, res_rows, data_rows, model_image, direction, grads)
    return (new_image, from_rows(new_rows, data_residual.shape), new_direction)


def solution(mesh):
    in_specs = (
        P("gx", "gy", None),
        P("gx", "gy", None),
        P("gx", "gy", None),
        P("gx", "gy", None),
        P("gx", "gy", None),
        P("gx", "gy", None, None),
        P("gx", "gy", None),
        P("gx", "gy"),
    )
    out_specs = (P("gx", "gy", None), P("gx", "gy", None), P("gx", "gy", None))
    return jax.shard_map(body, mesh=mesh, in_specs=in_specs, out_specs=out_specs, check_vma=False)
```

```python
import functools

import jax
import jax.numpy as jnp
from jax import lax
from jax.experimental import pallas as pl
from jax.experimental.pallas import tpu as pltpu
from jax.sharding import PartitionSpec as P

RADIUS = 8
SIDE = 2 * RADIUS + 1
LANES = 128
SUB = 8
F32 = jnp.float32
BF16 = jnp.bfloat16
VMEM_LIMIT = 48 * 1024 * 1024


def params(**extra):
    return pltpu.CompilerParams(vmem_limit_bytes=VMEM_LIMIT, **extra)


def to_rows(traces):
    bins_x, bins_y, samples = traces.shape
    parts = traces.reshape(bins_x, bins_y // SUB, SUB, samples // LANES, LANES)
    return parts.transpose(0, 1, 3, 2, 4).reshape(-1, LANES)


def from_rows(rows, shape):
    bins_x, bins_y, samples = shape
    parts = rows.reshape(bins_x, bins_y // SUB, samples // LANES, SUB, LANES)
    return parts.transpose(0, 1, 3, 2, 4).reshape(shape)


def trace_row(b, highs):
    return (b // SUB) * (SUB * highs) + b % SUB


def sample_row(res_ref, times_ref, wt_ref, vals, bins_y, entries, highs):
    for b in range(bins_y):
        first = trace_row(b, highs)
        for part in range(0, entries, SUB):
            times = times_ref[b, pl.ds(part, SUB), :]
            high = jnp.right_shift(times, LANES.bit_length() - 1)
            low = jnp.bitwise_and(times, LANES - 1)
            acc = jnp.zeros(times.shape, F32)
            for h in range(highs):
                table = res_ref[pl.ds(first + SUB * h, SUB, stride=0), :]
                got = jnp.take_along_axis(table, low, axis=1, mode="promise_in_bounds")
                acc = jnp.where(high == h, got, acc)
            scale = wt_ref[0][part : part + SUB, b : b + 1]
            vals[pl.ds(b * entries + part, SUB), :] = acc * scale


def spread_row(vals, place_ref, s_ref, row, wide_y, span):
    value = vals[...]
    upper = value.astype(BF16)
    lower = (value - upper.astype(F32)).astype(BF16)
    both = jnp.concatenate([upper, lower], axis=1)
    place = place_ref[0]
    step = 32
    for m in range(0, span, step):
        iota = lax.broadcasted_iota(jnp.int32, (step, place.shape[1]), 0) + m
        table = jnp.where(iota == place, 1.0, 0.0).astype(BF16)
        part = jnp.dot(table, both, preferred_element_type=F32)
        at = pl.ds(pl.multiple_of(row * wide_y + m, SUB), step)
        s_ref[at, :] += part[:, :LANES] + part[:, LANES:]


def first_kernel(geo, row0, res_ref, times_ref, wt_ref, place_ref, prev_ref, s_ref, vals):
    bins_y, entries, highs, wide_y = geo
    step = pl.program_id(0)

    @pl.when(step == 0)
    def _():
        s_ref[...] = prev_ref[...]

    sample_row(res_ref, times_ref, wt_ref, vals, bins_y, entries, highs)
    spread_row(vals, place_ref, s_ref, step + row0, wide_y, SIDE * wide_y)


def main_kernel(
    geo,
    unroll,
    col_ref,
    weight_ref,
    times_ref,
    wt_ref,
    place_ref,
    mid_ref,
    left_ref,
    right_ref,
    s1_ref,
    data_ref,
    curv_ref,
    out_left,
    out_mid,
    out_right,
    image,
    s_ref,
    vals,
    work,
):
    bins_y, entries, highs, wide_y = geo
    step = pl.program_id(0)
    wide_x = mid_ref.shape[0]

    @pl.when(step == 0)
    def _():
        s_ref[...] = jnp.zeros_like(s_ref)
        curv_ref[...] = jnp.zeros_like(curv_ref)
        for x in range(wide_x):
            image[pl.ds(x * wide_y, RADIUS), :] = left_ref[x]
            image[pl.ds(x * wide_y + RADIUS, bins_y), :] = mid_ref[x]
            image[pl.ds(x * wide_y + RADIUS + bins_y, RADIUS), :] = right_ref[x]

    half = LANES // 2
    half_bits = half.bit_length() - 1
    iota16 = lax.broadcasted_iota(jnp.int32, (16, LANES), 0)
    iota_lo = [(iota16 + k).astype(F32).astype(BF16) for k in range(0, half, 16)]
    iota_hi = [(iota16 + k).astype(F32).astype(BF16) for k in range(0, 2 * highs, 16)]
    zero = jnp.zeros((), BF16)
    one = jnp.ones((), BF16)

    def one_bin(b, slot):
        for e in range(entries):
            column = col_ref[0, b, e]
            work[slot, 0, pl.ds(e, 1), :] = image[pl.ds(column, 1), :] * weight_ref[0, b, e]
        value = work[slot, 0]
        upper = value.astype(BF16).astype(F32)
        work[slot, 0] = upper
        work[slot, 1] = value - upper
        times = times_ref[b]
        work[slot, 2] = jnp.bitwise_and(times, half - 1).astype(F32)
        middle = jnp.bitwise_and(jnp.right_shift(times, half_bits), 1)
        work[slot, 3] = (jnp.right_shift(times, half_bits + 1) + middle * highs).astype(F32)
        lefts = []
        rights = []
        for e in range(entries):

            def wide(k):
                return work[slot, k, pl.ds(e, 16, stride=0), :].astype(BF16)

            place = wide(3)
            hits = [place == iota for iota in iota_hi]
            parts = [jnp.where(hit, wide(k), zero) for k in range(2) for hit in hits]
            lefts.append(jnp.concatenate(parts, axis=0))
            low = wide(2)
            rights.append(
                jnp.concatenate([jnp.where(low == iota, one, zero) for iota in iota_lo], axis=0)
            )
        out = lax.dot_general(
            jnp.concatenate(lefts, axis=1),
            jnp.concatenate(rights, axis=1),
            (((1,), (1,)), ((), ())),
            preferred_element_type=F32,
        )
        out = out[: 2 * highs] + out[2 * highs :]
        trace = jnp.concatenate([out[:highs], out[highs:]], axis=1)
        data_ref[pl.ds(trace_row(b, highs), highs, stride=SUB), :] = trace
        return trace * trace

    def some_bins(k, total):
        for u in range(unroll):
            total = total + one_bin(k * unroll + u, u)
        return total

    total = lax.fori_loop(0, bins_y // unroll, some_bins, jnp.zeros((highs, LANES), F32))
    curv_ref[...] += total
    sample_row(data_ref, times_ref, wt_ref, vals, bins_y, entries, highs)
    spread_row(vals, place_ref, s_ref, step, wide_y, SIDE * wide_y)

    @pl.when(step == pl.num_programs(0) - 1)
    def _():
        for k, ref in enumerate((s1_ref, s_ref)):
            for x in range(wide_x):
                out_left[k, x] = ref[pl.ds(x * wide_y, RADIUS), :]
                out_mid[k, x] = ref[pl.ds(x * wide_y + RADIUS, bins_y), :]
                out_right[k, x] = ref[pl.ds(x * wide_y + RADIUS + bins_y, RADIUS), :]


def fold_y_kernel(mid_ref, low_ref, high_ref, out_head, out_mid, out_tail):
    wide_x, bins_y = mid_ref.shape[1], mid_ref.shape[2]
    bins_x = wide_x - 2 * RADIUS
    for k in range(2):
        for x in range(wide_x):
            if x < RADIUS:
                ref, at = out_head, x
            elif x < RADIUS + bins_x:
                ref, at = out_mid, x - RADIUS
            else:
                ref, at = out_tail, x - RADIUS - bins_x
            ref[k, at, pl.ds(0, RADIUS), :] = mid_ref[k, x, pl.ds(0, RADIUS), :] + low_ref[k, x]
            high = pl.ds(bins_y - RADIUS, RADIUS)
            ref[k, at, high, :] = mid_ref[k, x, high, :] + high_ref[k, x]


def fold_x_kernel(mid_ref, low_ref, high_ref, grad_ref, curv_ref, out_ref, stats_ref):
    bins_x = mid_ref.shape[1]
    sums = [jnp.zeros((1, LANES), F32) for _ in range(5)]
    for x in range(bins_x):
        pair = []
        for k in range(2):
            cells = mid_ref[k, x]
            if x < RADIUS:
                cells = cells + low_ref[k, x]
            else:
                cells = cells + high_ref[k, x - RADIUS]
            out_ref[k, x] = cells
            pair.append(cells)
        old = grad_ref[x]
        terms = (old * old, None, pair[0] * pair[0], pair[0] * pair[1], pair[1] * pair[1])
        for n, term in enumerate(terms):
            if term is not None:
                sums[n] = sums[n] + jnp.sum(term, axis=0, keepdims=True)
    sums[1] = jnp.sum(curv_ref[...], axis=0, keepdims=True)
    lane = lax.broadcasted_iota(jnp.int32, (1, LANES), 1)
    stats = jnp.zeros((1, LANES), F32)
    for n, term in enumerate(sums):
        stats = jnp.where(lane == n, jnp.sum(term, axis=1, keepdims=True), stats)
    stats_ref[...] = stats


def last_kernel(
    stats_ref, res_ref, data_ref, model_ref, dir_ref, grad_ref, new_image, new_residual, new_dir
):
    stats = jnp.sum(stats_ref[...], axis=0, keepdims=True)
    lane = lax.broadcasted_iota(jnp.int32, stats.shape, 1)

    def pick(n):
        return jnp.sum(jnp.where(lane == n, stats, 0.0), axis=1, keepdims=True)

    gamma, curvature, one_one, one_two, two_two = (pick(n) for n in range(5))
    alpha = gamma / curvature
    gamma_new = one_one - 2.0 * (alpha * one_two) + alpha * (alpha * two_two)
    beta = gamma_new / gamma
    new_residual[...] = res_ref[...] - alpha * data_ref[...]
    step = dir_ref[...]
    new_image[...] = model_ref[...] + alpha[None] * step
    new_dir[...] = (grad_ref[0] - alpha[None] * grad_ref[1]) + beta[None] * step


def shift(cells, axis, by):
    count = lax.axis_size(axis)
    pairs = [(i, i + by) for i in range(count) if 0 <= i + by < count]
    return lax.ppermute(cells, axis, pairs)


def body(
    model_image,
    data_residual,
    direction,
    old_gradient,
    aperture,
    travel_times,
    amplitude,
    trace_counts,
):
    bins_x, bins_y, samples = data_residual.shape
    entries, depths = travel_times.shape[2], travel_times.shape[3]
    highs = samples // LANES
    wide_x, wide_y = bins_x + 2 * RADIUS, bins_y + 2 * RADIUS
    columns = wide_x * wide_y
    span = SIDE * wide_y
    geo = (bins_y, entries, highs, wide_y)
    rows_per = bins_y * highs

    from_prev = shift(direction[bins_x - RADIUS :], "gx", 1)
    from_next = shift(direction[:RADIUS], "gx", -1)

    times = travel_times.reshape(bins_x * bins_y, entries, depths)
    res_rows = to_rows(data_residual)
    weight = amplitude * trace_counts.astype(F32)[:, :, None]
    weight_t = weight.transpose(0, 2, 1)
    off = (aperture // SIDE) * wide_y + aperture % SIDE
    window = off + jnp.arange(bins_y, dtype=jnp.int32)[None, :, None]
    column = window + wide_y * jnp.arange(bins_x, dtype=jnp.int32)[:, None, None]
    place = window.reshape(bins_x, 1, bins_y * entries)

    def first(row0, count, prev):
        return pl.pallas_call(
            functools.partial(first_kernel, geo, row0),
            grid=(count,),
            in_specs=[
                pl.BlockSpec((rows_per, LANES), lambda i: (i + row0, 0)),
                pl.BlockSpec((bins_y, entries, depths), lambda i: (i + row0, 0, 0)),
                pl.BlockSpec((1, entries, bins_y), lambda i: (i + row0, 0, 0)),
                pl.BlockSpec((1, 1, bins_y * entries), lambda i: (i + row0, 0, 0)),
                pl.BlockSpec((columns, depths), lambda i: (0, 0)),
            ],
            out_specs=pl.BlockSpec((columns, depths), lambda i: (0, 0)),
            out_shape=jax.ShapeDtypeStruct((columns, depths), F32),
            scratch_shapes=[pltpu.VMEM((bins_y * entries, depths), F32)],
            compiler_params=params(),
            cost_estimate=pl.CostEstimate(
                flops=4 * 10**9, bytes_accessed=4 * 10**6, transcendentals=0
            ),
            name="sample_residual",
        )(res_rows, times, weight_t, place, prev)

    s1 = first(0, bins_x // 2, jnp.zeros((columns, depths), F32))
    ext = jnp.concatenate([from_prev, direction, from_next], axis=0)
    left = shift(ext[:, bins_y - RADIUS :], "gy", 1)
    right = shift(ext[:, :RADIUS], "gy", -1)
    s1 = first(bins_x // 2, bins_x - bins_x // 2, s1)

    unroll = 4
    whole3 = lambda i: (0, 0, 0)
    whole4 = lambda i: (0, 0, 0, 0)
    strip = (2, wide_x, RADIUS, depths)
    middle = (2, wide_x, bins_y, depths)
    data_rows, curv, out_left, out_mid, out_right = pl.pallas_call(
        functools.partial(main_kernel, geo, unroll),
        grid=(bins_x,),
        in_specs=[
            pl.BlockSpec((1, bins_y, entries), lambda i: (i, 0, 0), memory_space=pltpu.SMEM),
            pl.BlockSpec((1, bins_y, entries), lambda i: (i, 0, 0), memory_space=pltpu.SMEM),
            pl.BlockSpec((bins_y, entries, depths), lambda i: (i, 0, 0)),
            pl.BlockSpec((1, entries, bins_y), lambda i: (i, 0, 0)),
            pl.BlockSpec((1, 1, bins_y * entries), lambda i: (i, 0, 0)),
            pl.BlockSpec((wide_x, bins_y, depths), whole3),
            pl.BlockSpec((wide_x, RADIUS, depths), whole3),
            pl.BlockSpec((wide_x, RADIUS, depths), whole3),
            pl.BlockSpec((columns, depths), lambda i: (0, 0)),
        ],
        out_specs=[
            pl.BlockSpec((rows_per, LANES), lambda i: (i, 0)),
            pl.BlockSpec((highs, LANES), lambda i: (0, 0)),
            pl.BlockSpec(strip, whole4),
            pl.BlockSpec(middle, whole4),
            pl.BlockSpec(strip, whole4),
        ],
        out_shape=[
            jax.ShapeDtypeStruct((bins_x * rows_per, LANES), F32),
            jax.ShapeDtypeStruct((highs, LANES), F32),
            jax.ShapeDtypeStruct(strip, F32),
            jax.ShapeDtypeStruct(middle, F32),
            jax.ShapeDtypeStruct(strip, F32),
        ],
        scratch_shapes=[
            pltpu.VMEM((columns, depths), F32),
            pltpu.VMEM((columns, depths), F32),
            pltpu.VMEM((bins_y * entries, depths), F32),
            pltpu.VMEM((unroll, 4, entries, LANES), F32),
        ],
        compiler_params=params(),
        cost_estimate=pl.CostEstimate(
            flops=20 * 10**9, bytes_accessed=8 * 10**6, transcendentals=0
        ),
        name="demigrate_and_sample",
    )(column, weight, times, weight_t, place, ext, left, right, s1)

    from_low = shift(out_right, "gy", 1)
    from_high = shift(out_left, "gy", -1)
    edge = jax.ShapeDtypeStruct((2, RADIUS, bins_y, depths), F32)
    out_head, inner, out_tail = pl.pallas_call(
        fold_y_kernel,
        out_shape=[edge, jax.ShapeDtypeStruct((2, bins_x, bins_y, depths), F32), edge],
        compiler_params=params(),
        name="fold_y",
    )(out_mid, from_low, from_high)
    from_low = shift(out_tail, "gx", 1)
    from_high = shift(out_head, "gx", -1)
    grads, stats = pl.pallas_call(
        fold_x_kernel,
        out_shape=[
            jax.ShapeDtypeStruct((2, bins_x, bins_y, depths), F32),
            jax.ShapeDtypeStruct((1, LANES), F32),
        ],
        compiler_params=params(),
        name="fold_x",
    )(inner, from_low, from_high, old_gradient, curv)
    devices = lax.axis_size("gx") * lax.axis_size("gy")
    stats = jnp.broadcast_to(stats[:, None], (devices, 1, LANES))
    stats = lax.all_to_all(stats, ("gx", "gy"), 0, 0, tiled=True).reshape(devices, LANES)

    steps = 8
    rows_step = bins_x * rows_per // steps
    x_step = bins_x // steps
    cells = pl.BlockSpec((x_step, bins_y, depths), lambda i: (i, 0, 0))
    rows = pl.BlockSpec((rows_step, LANES), lambda i: (i, 0))
    image_shape = jax.ShapeDtypeStruct(direction.shape, F32)
    new_image, new_rows, new_direction = pl.pallas_call(
        last_kernel,
        grid=(steps,),
        in_specs=[
            pl.BlockSpec(stats.shape, lambda i: (0, 0)),
            rows,
            rows,
            cells,
            cells,
            pl.BlockSpec((2, x_step, bins_y, depths), lambda i: (0, i, 0, 0)),
        ],
        out_specs=[cells, rows, cells],
        out_shape=[image_shape, jax.ShapeDtypeStruct(res_rows.shape, F32), image_shape],
        compiler_params=params(),
        name="update",
    )(stats, res_rows, data_rows, model_image, direction, grads)
    return (new_image, from_rows(new_rows, data_residual.shape), new_direction)


def solution(mesh):
    in_specs = (
        P("gx", "gy", None),
        P("gx", "gy", None),
        P("gx", "gy", None),
        P("gx", "gy", None),
        P("gx", "gy", None),
        P("gx", "gy", None, None),
        P("gx", "gy", None),
        P("gx", "gy"),
    )
    out_specs = (P("gx", "gy", None), P("gx", "gy", None), P("gx", "gy", None))
    return jax.shard_map(body, mesh=mesh, in_specs=in_specs, out_specs=out_specs, check_vma=False)
```

```python
import functools

import jax
import jax.numpy as jnp
from jax import lax
from jax.experimental import pallas as pl
from jax.experimental.pallas import tpu as pltpu
from jax.sharding import PartitionSpec as P

RADIUS = 8
SIDE = 2 * RADIUS + 1
LANES = 128
SUB = 8
F32 = jnp.float32
BF16 = jnp.bfloat16
VMEM_LIMIT = 51 * 1024 * 1024
SMALL_LIMIT = 24 * 1024 * 1024


def params(limit=VMEM_LIMIT):
    return pltpu.CompilerParams(vmem_limit_bytes=limit)


def to_rows(traces):
    bins_x, bins_y, samples = traces.shape
    parts = traces.reshape(bins_x, bins_y // SUB, SUB, samples // LANES, LANES)
    return parts.transpose(0, 1, 3, 2, 4).reshape(-1, LANES)


def from_rows(rows, shape):
    bins_x, bins_y, samples = shape
    parts = rows.reshape(bins_x, bins_y // SUB, samples // LANES, SUB, LANES)
    return parts.transpose(0, 1, 3, 2, 4).reshape(shape)


def trace_row(b, highs):
    return (b // SUB) * (SUB * highs) + b % SUB


def fill_weights(amp_ref, counts_ref, scales, bins_y, entries, row):
    weight = amp_ref[0].T * counts_ref[pl.ds(row, 1), :].astype(F32)
    for b in range(bins_y):
        column = jnp.broadcast_to(weight[:, b : b + 1], (entries, LANES))
        scales[pl.ds(b * entries, entries), :] = column


def sample_row(res_ref, times_ref, scales, vals, bins_y, entries, highs):
    for b in range(bins_y):
        first = trace_row(b, highs)
        for part in range(0, entries, SUB):
            times = times_ref[b, pl.ds(part, SUB), :]
            high = jnp.right_shift(times, LANES.bit_length() - 1)
            low = jnp.bitwise_and(times, LANES - 1)
            acc = jnp.zeros(times.shape, F32)
            for h in range(highs):
                table = res_ref[pl.ds(first + SUB * h, SUB, stride=0), :]
                got = jnp.take_along_axis(table, low, axis=1, mode="promise_in_bounds")
                acc = jnp.where(high == h, got, acc)
            at = pl.ds(b * entries + part, SUB)
            vals[at, :] = acc * scales[at, :]


def spread_row(vals, place_ref, s_ref, row, wide_y, span):
    value = vals[...]
    upper = value.astype(BF16)
    lower = (value - upper.astype(F32)).astype(BF16)
    both = jnp.concatenate([upper, lower], axis=1)
    place = place_ref[0]
    iota = lax.broadcasted_iota(jnp.int32, (span, place.shape[1]), 0)
    table = jnp.where(iota == place, 1.0, 0.0).astype(BF16)
    part = jnp.dot(table, both, preferred_element_type=F32)
    s_ref[pl.ds(pl.multiple_of(row * wide_y, SUB), span), :] += part[:, :LANES] + part[:, LANES:]


def first_kernel(
    geo, row0, res_ref, times_ref, amp_ref, counts_ref, place_ref, prev_ref, s_ref, vals, scales
):
    bins_y, entries, highs, wide_y = geo
    step = pl.program_id(0)

    @pl.when(step == 0)
    def _():
        s_ref[...] = prev_ref[...]

    fill_weights(amp_ref, counts_ref, scales, bins_y, entries, step + row0)
    sample_row(res_ref, times_ref, scales, vals, bins_y, entries, highs)
    spread_row(vals, place_ref, s_ref, step + row0, wide_y, SIDE * wide_y)


def main_kernel(
    geo,
    unroll,
    col_ref,
    times_ref,
    amp_ref,
    counts_ref,
    place_ref,
    mid_ref,
    left_ref,
    right_ref,
    s1_ref,
    data_ref,
    curv_ref,
    out_left,
    out_mid,
    out_right,
    image,
    s_ref,
    vals,
    scales,
    work,
):
    bins_y, entries, highs, wide_y = geo
    step = pl.program_id(0)
    wide_x = mid_ref.shape[0]

    @pl.when(step == 0)
    def _():
        s_ref[...] = jnp.zeros_like(s_ref)
        curv_ref[...] = jnp.zeros_like(curv_ref)
        for x in range(wide_x):
            image[pl.ds(x * wide_y, RADIUS), :] = left_ref[x]
            image[pl.ds(x * wide_y + RADIUS, bins_y), :] = mid_ref[x]
            image[pl.ds(x * wide_y + RADIUS + bins_y, RADIUS), :] = right_ref[x]

    fill_weights(amp_ref, counts_ref, scales, bins_y, entries, step)
    half = LANES // 2
    half_bits = half.bit_length() - 1
    iota16 = lax.broadcasted_iota(jnp.int32, (16, LANES), 0)
    iota_lo = [(iota16 + k).astype(F32).astype(BF16) for k in range(0, half, 16)]
    iota_hi = [(iota16 + k).astype(F32).astype(BF16) for k in range(0, 2 * highs, 16)]
    zero = jnp.zeros((), BF16)
    one = jnp.ones((), BF16)

    def one_bin(b, slot):
        for e in range(entries):
            column = col_ref[0, b, e]
            work[slot, 0, pl.ds(e, 1), :] = image[pl.ds(column, 1), :]
        value = work[slot, 0] * scales[pl.ds(pl.multiple_of(b * entries, SUB), entries), :]
        upper = value.astype(BF16).astype(F32)
        work[slot, 0] = upper
        work[slot, 1] = value - upper
        times = times_ref[b]
        work[slot, 2] = jnp.bitwise_and(times, half - 1).astype(F32)
        middle = jnp.bitwise_and(jnp.right_shift(times, half_bits), 1)
        work[slot, 3] = (jnp.right_shift(times, half_bits + 1) + middle * highs).astype(F32)
        lefts = []
        rights = []
        for e in range(entries):

            def wide(k):
                return work[slot, k, pl.ds(e, 16, stride=0), :].astype(BF16)

            place = wide(3)
            hits = [place == iota for iota in iota_hi]
            parts = [jnp.where(hit, wide(k), zero) for k in range(2) for hit in hits]
            lefts.append(jnp.concatenate(parts, axis=0))
            low = wide(2)
            rights.append(
                jnp.concatenate([jnp.where(low == iota, one, zero) for iota in iota_lo], axis=0)
            )
        out = lax.dot_general(
            jnp.concatenate(lefts, axis=1),
            jnp.concatenate(rights, axis=1),
            (((1,), (1,)), ((), ())),
            preferred_element_type=F32,
        )
        out = out[: 2 * highs] + out[2 * highs :]
        trace = jnp.concatenate([out[:highs], out[highs:]], axis=1)
        data_ref[pl.ds(trace_row(b, highs), highs, stride=SUB), :] = trace
        return trace * trace

    def some_bins(k, total):
        for u in range(unroll):
            total = total + one_bin(k * unroll + u, u)
        return total

    total = lax.fori_loop(0, bins_y // unroll, some_bins, jnp.zeros((highs, LANES), F32))
    curv_ref[...] += total
    sample_row(data_ref, times_ref, scales, vals, bins_y, entries, highs)
    spread_row(vals, place_ref, s_ref, step, wide_y, SIDE * wide_y)

    @pl.when(step == pl.num_programs(0) - 1)
    def _():
        for k, ref in enumerate((s1_ref, s_ref)):
            for x in range(wide_x):
                out_left[k, x] = ref[pl.ds(x * wide_y, RADIUS), :]
                out_mid[k, x] = ref[pl.ds(x * wide_y + RADIUS, bins_y), :]
                out_right[k, x] = ref[pl.ds(x * wide_y + RADIUS + bins_y, RADIUS), :]


def fold_y_kernel(mid_ref, low_ref, high_ref, out_head, out_mid, out_tail):
    wide_x, bins_y = mid_ref.shape[1], mid_ref.shape[2]
    bins_x = wide_x - 2 * RADIUS
    for k in range(2):
        for x in range(wide_x):
            if x < RADIUS:
                ref, at = out_head, x
            elif x < RADIUS + bins_x:
                ref, at = out_mid, x - RADIUS
            else:
                ref, at = out_tail, x - RADIUS - bins_x
            ref[k, at, pl.ds(0, RADIUS), :] = mid_ref[k, x, pl.ds(0, RADIUS), :] + low_ref[k, x]
            high = pl.ds(bins_y - RADIUS, RADIUS)
            ref[k, at, high, :] = mid_ref[k, x, high, :] + high_ref[k, x]


def fold_x_kernel(mid_ref, low_ref, high_ref, grad_ref, curv_ref, out_ref, stats_ref):
    bins_x = mid_ref.shape[1]
    sums = [jnp.zeros((1, LANES), F32) for _ in range(5)]
    for x in range(bins_x):
        pair = []
        for k in range(2):
            cells = mid_ref[k, x]
            if x < RADIUS:
                cells = cells + low_ref[k, x]
            else:
                cells = cells + high_ref[k, x - RADIUS]
            out_ref[k, x] = cells
            pair.append(cells)
        old = grad_ref[x]
        terms = (old * old, None, pair[0] * pair[0], pair[0] * pair[1], pair[1] * pair[1])
        for n, term in enumerate(terms):
            if term is not None:
                sums[n] = sums[n] + jnp.sum(term, axis=0, keepdims=True)
    sums[1] = jnp.sum(curv_ref[...], axis=0, keepdims=True)
    lane = lax.broadcasted_iota(jnp.int32, (1, LANES), 1)
    stats = jnp.zeros((1, LANES), F32)
    for n, term in enumerate(sums):
        stats = jnp.where(lane == n, jnp.sum(term, axis=1, keepdims=True), stats)
    stats_ref[...] = jnp.broadcast_to(stats[None], stats_ref.shape)


def last_kernel(
    stats_ref, res_ref, data_ref, model_ref, dir_ref, grad_ref, new_image, new_residual, new_dir
):
    stats = jnp.sum(stats_ref[...], axis=0)
    lane = lax.broadcasted_iota(jnp.int32, stats.shape, 1)

    def pick(n):
        return jnp.sum(jnp.where(lane == n, stats, 0.0), axis=1, keepdims=True)

    gamma, curvature, one_one, one_two, two_two = (pick(n) for n in range(5))
    alpha = gamma / curvature
    gamma_new = one_one - 2.0 * (alpha * one_two) + alpha * (alpha * two_two)
    beta = gamma_new / gamma
    new_residual[...] = res_ref[...] - alpha * data_ref[...]
    step = dir_ref[...]
    new_image[...] = model_ref[...] + alpha[None] * step
    new_dir[...] = (grad_ref[0] - alpha[None] * grad_ref[1]) + beta[None] * step


def shift(cells, axis, by):
    count = lax.axis_size(axis)
    pairs = [(i, i + by) for i in range(count) if 0 <= i + by < count]
    return lax.ppermute(cells, axis, pairs)


def body(
    model_image,
    data_residual,
    direction,
    old_gradient,
    aperture,
    travel_times,
    amplitude,
    trace_counts,
):
    bins_x, bins_y, samples = data_residual.shape
    entries, depths = travel_times.shape[2], travel_times.shape[3]
    highs = samples // LANES
    wide_x, wide_y = bins_x + 2 * RADIUS, bins_y + 2 * RADIUS
    columns = wide_x * wide_y
    span = SIDE * wide_y
    geo = (bins_y, entries, highs, wide_y)
    rows_per = bins_y * highs

    from_prev = shift(direction[bins_x - RADIUS :], "gx", 1)
    from_next = shift(direction[:RADIUS], "gx", -1)

    times = travel_times.reshape(bins_x * bins_y, entries, depths)
    res_rows = to_rows(data_residual)
    off = (aperture // SIDE) * wide_y + aperture % SIDE
    window = off + jnp.arange(bins_y, dtype=jnp.int32)[None, :, None]
    column = window + wide_y * jnp.arange(bins_x, dtype=jnp.int32)[:, None, None]
    place = window.reshape(bins_x, 1, bins_y * entries)

    def first(row0, count, prev):
        return pl.pallas_call(
            functools.partial(first_kernel, geo, row0),
            grid=(count,),
            in_specs=[
                pl.BlockSpec((rows_per, LANES), lambda i: (i + row0, 0)),
                pl.BlockSpec((bins_y, entries, depths), lambda i: (i + row0, 0, 0)),
                pl.BlockSpec((1, bins_y, entries), lambda i: (i + row0, 0, 0)),
                pl.BlockSpec((bins_x, bins_y), lambda i: (0, 0)),
                pl.BlockSpec((1, 1, bins_y * entries), lambda i: (i + row0, 0, 0)),
                pl.BlockSpec((columns, depths), lambda i: (0, 0)),
            ],
            out_specs=pl.BlockSpec((columns, depths), lambda i: (0, 0)),
            out_shape=jax.ShapeDtypeStruct((columns, depths), F32),
            scratch_shapes=[pltpu.VMEM((bins_y * entries, depths), F32)] * 2,
            compiler_params=params(),
            cost_estimate=pl.CostEstimate(
                flops=4 * 10**9, bytes_accessed=4 * 10**6, transcendentals=0
            ),
            name="sample_residual",
        )(res_rows, times, amplitude, trace_counts, place, prev)

    s1 = first(0, bins_x // 2, jnp.zeros((columns, depths), F32))
    ext = jnp.concatenate([from_prev, direction, from_next], axis=0)
    tail, head, s1 = lax.optimization_barrier((ext[:, bins_y - RADIUS :], ext[:, :RADIUS], s1))
    left = shift(tail, "gy", 1)
    right = shift(head, "gy", -1)
    s1 = first(bins_x // 2, bins_x - bins_x // 2, s1)

    unroll = 4
    whole3 = lambda i: (0, 0, 0)
    whole4 = lambda i: (0, 0, 0, 0)
    strip = (2, wide_x, RADIUS, depths)
    middle = (2, wide_x, bins_y, depths)
    data_rows, curv, out_left, out_mid, out_right = pl.pallas_call(
        functools.partial(main_kernel, geo, unroll),
        grid=(bins_x,),
        in_specs=[
            pl.BlockSpec((1, bins_y, entries), lambda i: (i, 0, 0), memory_space=pltpu.SMEM),
            pl.BlockSpec((bins_y, entries, depths), lambda i: (i, 0, 0)),
            pl.BlockSpec((1, bins_y, entries), lambda i: (i, 0, 0)),
            pl.BlockSpec((bins_x, bins_y), lambda i: (0, 0)),
            pl.BlockSpec((1, 1, bins_y * entries), lambda i: (i, 0, 0)),
            pl.BlockSpec((wide_x, bins_y, depths), whole3),
            pl.BlockSpec((wide_x, RADIUS, depths), whole3),
            pl.BlockSpec((wide_x, RADIUS, depths), whole3),
            pl.BlockSpec((columns, depths), lambda i: (0, 0)),
        ],
        out_specs=[
            pl.BlockSpec((rows_per, LANES), lambda i: (i, 0)),
            pl.BlockSpec((highs, LANES), lambda i: (0, 0)),
            pl.BlockSpec(strip, whole4),
            pl.BlockSpec(middle, whole4),
            pl.BlockSpec(strip, whole4),
        ],
        out_shape=[
            jax.ShapeDtypeStruct((bins_x * rows_per, LANES), F32),
            jax.ShapeDtypeStruct((highs, LANES), F32),
            jax.ShapeDtypeStruct(strip, F32),
            jax.ShapeDtypeStruct(middle, F32),
            jax.ShapeDtypeStruct(strip, F32),
        ],
        scratch_shapes=[
            pltpu.VMEM((columns, depths), F32),
            pltpu.VMEM((columns, depths), F32),
            pltpu.VMEM((bins_y * entries, depths), F32),
            pltpu.VMEM((bins_y * entries, depths), F32),
            pltpu.VMEM((unroll, 4, entries, LANES), F32),
        ],
        compiler_params=params(),
        cost_estimate=pl.CostEstimate(
            flops=20 * 10**9, bytes_accessed=8 * 10**6, transcendentals=0
        ),
        name="demigrate_and_sample",
    )(column, times, amplitude, trace_counts, place, ext, left, right, s1)

    from_low = shift(out_right, "gy", 1)
    from_high = shift(out_left, "gy", -1)
    edge = jax.ShapeDtypeStruct((2, RADIUS, bins_y, depths), F32)
    out_head, inner, out_tail = pl.pallas_call(
        fold_y_kernel,
        out_shape=[edge, jax.ShapeDtypeStruct((2, bins_x, bins_y, depths), F32), edge],
        compiler_params=params(SMALL_LIMIT),
        name="fold_y",
    )(out_mid, from_low, from_high)
    from_low = shift(out_tail, "gx", 1)
    from_high = shift(out_head, "gx", -1)
    devices = lax.axis_size("gx") * lax.axis_size("gy")
    grads, stats = pl.pallas_call(
        fold_x_kernel,
        out_shape=[
            jax.ShapeDtypeStruct((2, bins_x, bins_y, depths), F32),
            jax.ShapeDtypeStruct((devices, 1, LANES), F32),
        ],
        compiler_params=params(SMALL_LIMIT),
        name="fold_x",
    )(inner, from_low, from_high, old_gradient, curv)
    stats = lax.all_to_all(stats, ("gx", "gy"), 0, 0, tiled=True)

    steps = 8
    rows_step = bins_x * rows_per // steps
    x_step = bins_x // steps
    cells = pl.BlockSpec((x_step, bins_y, depths), lambda i: (i, 0, 0))
    rows = pl.BlockSpec((rows_step, LANES), lambda i: (i, 0))
    image_shape = jax.ShapeDtypeStruct(direction.shape, F32)
    new_image, new_rows, new_direction = pl.pallas_call(
        last_kernel,
        grid=(steps,),
        in_specs=[
            pl.BlockSpec(stats.shape, lambda i: (0, 0, 0)),
            rows,
            rows,
            cells,
            cells,
            pl.BlockSpec((2, x_step, bins_y, depths), lambda i: (0, i, 0, 0)),
        ],
        out_specs=[cells, rows, cells],
        out_shape=[image_shape, jax.ShapeDtypeStruct(res_rows.shape, F32), image_shape],
        compiler_params=params(SMALL_LIMIT),
        name="update",
    )(stats, res_rows, data_rows, model_image, direction, grads)
    return (new_image, from_rows(new_rows, data_residual.shape), new_direction)


def solution(mesh):
    in_specs = (
        P("gx", "gy", None),
        P("gx", "gy", None),
        P("gx", "gy", None),
        P("gx", "gy", None),
        P("gx", "gy", None),
        P("gx", "gy", None, None),
        P("gx", "gy", None),
        P("gx", "gy"),
    )
    out_specs = (P("gx", "gy", None), P("gx", "gy", None), P("gx", "gy", None))
    return jax.shard_map(body, mesh=mesh, in_specs=in_specs, out_specs=out_specs, check_vma=False)
```

```python
import functools

import jax
import jax.numpy as jnp
from jax import lax
from jax.experimental import pallas as pl
from jax.experimental.pallas import tpu as pltpu
from jax.sharding import PartitionSpec as P

RADIUS = 8
SIDE = 2 * RADIUS + 1
LANES = 128
SUB = 8
F32 = jnp.float32
BF16 = jnp.bfloat16
VMEM_LIMIT = 51 * 1024 * 1024
SMALL_LIMIT = 24 * 1024 * 1024


def params(limit=VMEM_LIMIT):
    return pltpu.CompilerParams(vmem_limit_bytes=limit)


def to_rows(traces):
    bins_x, bins_y, samples = traces.shape
    parts = traces.reshape(bins_x, bins_y // SUB, SUB, samples // LANES, LANES)
    return parts.transpose(0, 1, 3, 2, 4).reshape(-1, LANES)


def from_rows(rows, shape):
    bins_x, bins_y, samples = shape
    parts = rows.reshape(bins_x, bins_y // SUB, samples // LANES, SUB, LANES)
    return parts.transpose(0, 1, 3, 2, 4).reshape(shape)


def trace_row(b, highs):
    return (b // SUB) * (SUB * highs) + b % SUB


def fill_weights(amp_ref, counts, scales):
    bins, entries = amp_ref.shape[1], amp_ref.shape[2]
    weight = amp_ref[0].T * counts.astype(F32)
    for b in range(bins):
        column = jnp.broadcast_to(weight[:, b : b + 1], (entries, LANES))
        scales[pl.ds(b * entries, entries), :] = column


def sample_bin(source, first, highs, times_ref, b, scales, vals):
    entries = times_ref.shape[1]
    for part in range(0, entries, SUB):
        times = times_ref[b, pl.ds(part, SUB), :]
        high = jnp.right_shift(times, LANES.bit_length() - 1)
        low = jnp.bitwise_and(times, LANES - 1)
        acc = jnp.zeros(times.shape, F32)
        for h in range(highs):
            table = source[pl.ds(first + SUB * h, SUB, stride=0), :]
            got = jnp.take_along_axis(table, low, axis=1, mode="promise_in_bounds")
            acc = jnp.where(high == h, got, acc)
        at = b * entries + part
        at = pl.ds(at if isinstance(at, int) else pl.multiple_of(at, SUB), SUB)
        vals[at, :] = acc * scales[at, :]


def spread_bins(vals, place_ref, s_ref, row, wide_y):
    span = SIDE * wide_y
    value = vals[...]
    upper = value.astype(BF16)
    lower = (value - upper.astype(F32)).astype(BF16)
    both = jnp.concatenate([upper, lower], axis=1)
    place = place_ref[0]
    iota = lax.broadcasted_iota(jnp.int32, (span, place.shape[1]), 0)
    table = jnp.where(iota == place, 1.0, 0.0).astype(BF16)
    part = jnp.dot(table, both, preferred_element_type=F32)
    s_ref[pl.ds(pl.multiple_of(row * wide_y, SUB), span), :] += part[:, :LANES] + part[:, LANES:]


def first_kernel(
    geo, row0, res_ref, times_ref, amp_ref, counts_ref, place_ref, prev_ref, s_ref, vals, scales
):
    bins_y, entries, highs, wide_y = geo
    step = pl.program_id(0)

    @pl.when(step == 0)
    def _():
        s_ref[...] = prev_ref[...]

    fill_weights(amp_ref, counts_ref[pl.ds(step + row0, 1), :], scales)
    for b in range(bins_y):
        sample_bin(res_ref, trace_row(b, highs), highs, times_ref, b, scales, vals)
    spread_bins(vals, place_ref, s_ref, step + row0, wide_y)


def scatter_bin(geo, b, image, col_ref, times_ref, scales, work):
    bins_y, entries, highs, wide_y = geo
    half = LANES // 2
    half_bits = half.bit_length() - 1
    iota16 = lax.broadcasted_iota(jnp.int32, (16, LANES), 0)
    iota_lo = [(iota16 + k).astype(F32).astype(BF16) for k in range(0, half, 16)]
    iota_hi = [(iota16 + k).astype(F32).astype(BF16) for k in range(0, 2 * highs, 16)]
    zero = jnp.zeros((), BF16)
    one = jnp.ones((), BF16)
    for e in range(entries):
        column = col_ref[0, b, e]
        work[0, pl.ds(e, 1), :] = image[pl.ds(column, 1), :]
    value = work[0, pl.ds(0, entries), :]
    value = value * scales[pl.ds(pl.multiple_of(b * entries, SUB), entries), :]
    upper = value.astype(BF16).astype(F32)
    times = times_ref[b]
    middle = jnp.bitwise_and(jnp.right_shift(times, half_bits), 1)
    rows = pl.ds(0, entries)
    work[0, rows, :] = upper
    work[1, rows, :] = value - upper
    work[2, rows, :] = jnp.bitwise_and(times, half - 1).astype(F32)
    work[3, rows, :] = (jnp.right_shift(times, half_bits + 1) + middle * highs).astype(F32)
    lefts = []
    rights = []
    for e in range(entries):

        def wide(k):
            row = work[k, pl.ds(e, SUB, stride=0), :]
            return jnp.concatenate([row, row], axis=0).astype(BF16)

        place = wide(3)
        hits = [place == iota for iota in iota_hi]
        parts = [jnp.where(hit, wide(k), zero) for k in range(2) for hit in hits]
        lefts.append(jnp.concatenate(parts, axis=0))
        low = wide(2)
        rights.append(
            jnp.concatenate([jnp.where(low == iota, one, zero) for iota in iota_lo], axis=0)
        )
    out = lax.dot_general(
        jnp.concatenate(lefts, axis=1),
        jnp.concatenate(rights, axis=1),
        (((1,), (1,)), ((), ())),
        preferred_element_type=F32,
    )
    out = out[: 2 * highs] + out[2 * highs :]
    return jnp.concatenate([out[:highs], out[highs:]], axis=1)


def main_kernel(
    geo,
    unroll,
    row0,
    col_ref,
    times_ref,
    old_times_ref,
    res_times_ref,
    amp_ref,
    res_amp_ref,
    counts_ref,
    res_counts_ref,
    old_place_ref,
    last_place_ref,
    res_place_ref,
    res_ref,
    mid_ref,
    left_ref,
    right_ref,
    s1_in_ref,
    data_ref,
    curv_ref,
    out_left,
    out_mid,
    out_right,
    image,
    s1_ref,
    s2_ref,
    vals,
    res_vals,
    scales,
    old_scales,
    res_scales,
    old_data,
    *works,
):
    bins_y, entries, highs, wide_y = geo
    step = pl.program_id(0)
    wide_x = mid_ref.shape[0]
    groups = bins_y // unroll
    res_bins = res_times_ref.shape[0]
    res_unroll = res_bins // groups

    @pl.when(step == 0)
    def _():
        s1_ref[...] = s1_in_ref[...]
        s2_ref[...] = jnp.zeros_like(s2_ref)
        curv_ref[...] = jnp.zeros_like(curv_ref)
        old_data[...] = jnp.zeros_like(old_data)
        scales[...] = jnp.zeros_like(scales)
        for x in range(wide_x):
            image[pl.ds(x * wide_y, RADIUS), :] = left_ref[x]
            image[pl.ds(x * wide_y + RADIUS, bins_y), :] = mid_ref[x]
            image[pl.ds(x * wide_y + RADIUS + bins_y, RADIUS), :] = right_ref[x]

    old_scales[...] = scales[...]
    fill_weights(amp_ref, counts_ref[pl.ds(step, 1), :], scales)
    fill_weights(res_amp_ref, res_counts_ref[0], res_scales)

    def some_bins(k, total):
        for u in range(unroll):
            b = k * unroll + u
            trace = scatter_bin(geo, b, image, col_ref, times_ref, scales, works[u])
            data_ref[pl.ds(trace_row(b, highs), highs, stride=SUB), :] = trace
            total = total + trace * trace
            first = trace_row(b, highs)
            sample_bin(old_data, first, highs, old_times_ref, b, old_scales, vals)
            if u < res_unroll:
                r = k * res_unroll + u
                first = trace_row(r, highs)
                sample_bin(res_ref, first, highs, res_times_ref, r, res_scales, res_vals)
        return total

    curv_ref[...] += lax.fori_loop(0, groups, some_bins, jnp.zeros((highs, LANES), F32))
    spread_bins(vals, old_place_ref, s2_ref, jnp.maximum(step - 1, 0), wide_y)
    spread_bins(res_vals, res_place_ref, s1_ref, row0 + (step * res_bins) // bins_y, wide_y)
    old_data[...] = data_ref[...]

    @pl.when(step == pl.num_programs(0) - 1)
    def _():
        for b in range(bins_y):
            sample_bin(old_data, trace_row(b, highs), highs, times_ref, b, scales, vals)
        spread_bins(vals, last_place_ref, s2_ref, step, wide_y)
        for k, ref in enumerate((s1_ref, s2_ref)):
            for x in range(wide_x):
                out_left[k, x] = ref[pl.ds(x * wide_y, RADIUS), :]
                out_mid[k, x] = ref[pl.ds(x * wide_y + RADIUS, bins_y), :]
                out_right[k, x] = ref[pl.ds(x * wide_y + RADIUS + bins_y, RADIUS), :]


def fold_y_kernel(mid_ref, low_ref, high_ref, out_head, out_mid, out_tail):
    wide_x, bins_y = mid_ref.shape[1], mid_ref.shape[2]
    bins_x = wide_x - 2 * RADIUS
    for k in range(2):
        for x in range(wide_x):
            if x < RADIUS:
                ref, at = out_head, x
            elif x < RADIUS + bins_x:
                ref, at = out_mid, x - RADIUS
            else:
                ref, at = out_tail, x - RADIUS - bins_x
            ref[k, at, pl.ds(0, RADIUS), :] = mid_ref[k, x, pl.ds(0, RADIUS), :] + low_ref[k, x]
            high = pl.ds(bins_y - RADIUS, RADIUS)
            ref[k, at, high, :] = mid_ref[k, x, high, :] + high_ref[k, x]


def fold_x_kernel(mid_ref, low_ref, high_ref, grad_ref, curv_ref, out_ref, stats_ref):
    bins_x = mid_ref.shape[1]
    sums = [jnp.zeros((1, LANES), F32) for _ in range(5)]
    for x in range(bins_x):
        pair = []
        for k in range(2):
            cells = mid_ref[k, x]
            if x < RADIUS:
                cells = cells + low_ref[k, x]
            else:
                cells = cells + high_ref[k, x - RADIUS]
            out_ref[k, x] = cells
            pair.append(cells)
        old = grad_ref[x]
        terms = (old * old, None, pair[0] * pair[0], pair[0] * pair[1], pair[1] * pair[1])
        for n, term in enumerate(terms):
            if term is not None:
                sums[n] = sums[n] + jnp.sum(term, axis=0, keepdims=True)
    sums[1] = jnp.sum(curv_ref[...], axis=0, keepdims=True)
    lane = lax.broadcasted_iota(jnp.int32, (1, LANES), 1)
    stats = jnp.zeros((1, LANES), F32)
    for n, term in enumerate(sums):
        stats = jnp.where(lane == n, jnp.sum(term, axis=1, keepdims=True), stats)
    stats_ref[...] = jnp.broadcast_to(stats[None], stats_ref.shape)


def last_kernel(
    stats_ref, res_ref, data_ref, model_ref, dir_ref, grad_ref, new_image, new_residual, new_dir
):
    stats = jnp.sum(stats_ref[...], axis=0)
    lane = lax.broadcasted_iota(jnp.int32, stats.shape, 1)

    def pick(n):
        return jnp.sum(jnp.where(lane == n, stats, 0.0), axis=1, keepdims=True)

    gamma, curvature, one_one, one_two, two_two = (pick(n) for n in range(5))
    alpha = gamma / curvature
    gamma_new = one_one - 2.0 * (alpha * one_two) + alpha * (alpha * two_two)
    beta = gamma_new / gamma
    new_residual[...] = res_ref[...] - alpha * data_ref[...]
    step = dir_ref[...]
    new_image[...] = model_ref[...] + alpha[None] * step
    new_dir[...] = (grad_ref[0] - alpha[None] * grad_ref[1]) + beta[None] * step


def shift(cells, axis, by):
    count = lax.axis_size(axis)
    pairs = [(i, i + by) for i in range(count) if 0 <= i + by < count]
    return lax.ppermute(cells, axis, pairs)


def body(
    model_image,
    data_residual,
    direction,
    old_gradient,
    aperture,
    travel_times,
    amplitude,
    trace_counts,
):
    bins_x, bins_y, samples = data_residual.shape
    entries, depths = travel_times.shape[2], travel_times.shape[3]
    highs = samples // LANES
    wide_x, wide_y = bins_x + 2 * RADIUS, bins_y + 2 * RADIUS
    columns = wide_x * wide_y
    span = SIDE * wide_y
    geo = (bins_y, entries, highs, wide_y)
    rows_per = bins_y * highs

    from_prev = shift(direction[bins_x - RADIUS :], "gx", 1)
    from_next = shift(direction[:RADIUS], "gx", -1)

    times = travel_times.reshape(bins_x * bins_y, entries, depths)
    res_rows = to_rows(data_residual)
    off = (aperture // SIDE) * wide_y + aperture % SIDE
    window = off + jnp.arange(bins_y, dtype=jnp.int32)[None, :, None]
    column = window + wide_y * jnp.arange(bins_x, dtype=jnp.int32)[:, None, None]
    place = window.reshape(bins_x, 1, bins_y * entries)

    def first(row0, count, prev):
        return pl.pallas_call(
            functools.partial(first_kernel, geo, row0),
            grid=(count,),
            in_specs=[
                pl.BlockSpec((rows_per, LANES), lambda i: (i + row0, 0)),
                pl.BlockSpec((bins_y, entries, depths), lambda i: (i + row0, 0, 0)),
                pl.BlockSpec((1, bins_y, entries), lambda i: (i + row0, 0, 0)),
                pl.BlockSpec((bins_x, bins_y), lambda i: (0, 0)),
                pl.BlockSpec((1, 1, bins_y * entries), lambda i: (i + row0, 0, 0)),
                pl.BlockSpec((columns, depths), lambda i: (0, 0)),
            ],
            out_specs=pl.BlockSpec((columns, depths), lambda i: (0, 0)),
            out_shape=jax.ShapeDtypeStruct((columns, depths), F32),
            scratch_shapes=[pltpu.VMEM((bins_y * entries, depths), F32)] * 2,
            compiler_params=params(),
            cost_estimate=pl.CostEstimate(
                flops=4 * 10**9, bytes_accessed=4 * 10**6, transcendentals=0
            ),
            name="sample_residual",
        )(res_rows, times, amplitude, trace_counts, place, prev)

    early = bins_x // 4
    row0 = 2 * early
    s1 = first(0, early, jnp.zeros((columns, depths), F32))
    ext = jnp.concatenate([from_prev, direction, from_next], axis=0)
    tail, head, s1 = lax.optimization_barrier((ext[:, bins_y - RADIUS :], ext[:, :RADIUS], s1))
    left = shift(tail, "gy", 1)
    right = shift(head, "gy", -1)
    s1 = first(early, early, s1)

    unroll = 4
    cut = bins_x // (bins_x - row0)
    res_bins = bins_y // cut
    counts_cut = trace_counts.reshape(bins_x * cut, 1, res_bins)
    whole3 = lambda i: (0, 0, 0)
    whole4 = lambda i: (0, 0, 0, 0)
    before = lambda i: (jnp.maximum(i - 1, 0), 0, 0)
    this = lambda i: (i, 0, 0)
    late = lambda i: (row0 * cut + i, 0, 0)
    strip = (2, wide_x, RADIUS, depths)
    middle = (2, wide_x, bins_y, depths)
    vals_shape = pltpu.VMEM((bins_y * entries, depths), F32)
    res_shape = pltpu.VMEM((res_bins * entries, depths), F32)
    columns_shape = pltpu.VMEM((columns, depths), F32)
    data_rows, curv, out_left, out_mid, out_right = pl.pallas_call(
        functools.partial(main_kernel, geo, unroll, row0),
        grid=(bins_x,),
        in_specs=[
            pl.BlockSpec((1, bins_y, entries), this, memory_space=pltpu.SMEM),
            pl.BlockSpec((bins_y, entries, depths), this),
            pl.BlockSpec((bins_y, entries, depths), before),
            pl.BlockSpec((res_bins, entries, depths), late),
            pl.BlockSpec((1, bins_y, entries), this),
            pl.BlockSpec((1, res_bins, entries), late),
            pl.BlockSpec((bins_x, bins_y), lambda i: (0, 0)),
            pl.BlockSpec((1, 1, res_bins), late),
            pl.BlockSpec((1, 1, bins_y * entries), before),
            pl.BlockSpec((1, 1, bins_y * entries), lambda i: (bins_x - 1, 0, 0)),
            pl.BlockSpec((1, 1, res_bins * entries), late),
            pl.BlockSpec((res_bins * highs, LANES), lambda i: (row0 * cut + i, 0)),
            pl.BlockSpec((wide_x, bins_y, depths), whole3),
            pl.BlockSpec((wide_x, RADIUS, depths), whole3),
            pl.BlockSpec((wide_x, RADIUS, depths), whole3),
            pl.BlockSpec((columns, depths), lambda i: (0, 0)),
        ],
        out_specs=[
            pl.BlockSpec((rows_per, LANES), lambda i: (i, 0)),
            pl.BlockSpec((highs, LANES), lambda i: (0, 0)),
            pl.BlockSpec(strip, whole4),
            pl.BlockSpec(middle, whole4),
            pl.BlockSpec(strip, whole4),
        ],
        out_shape=[
            jax.ShapeDtypeStruct((bins_x * rows_per, LANES), F32),
            jax.ShapeDtypeStruct((highs, LANES), F32),
            jax.ShapeDtypeStruct(strip, F32),
            jax.ShapeDtypeStruct(middle, F32),
            jax.ShapeDtypeStruct(strip, F32),
        ],
        scratch_shapes=[columns_shape, columns_shape, columns_shape]
        + [vals_shape, res_shape, vals_shape, vals_shape, res_shape]
        + [pltpu.VMEM((rows_per, LANES), F32)]
        + [pltpu.VMEM((4, entries + SUB, LANES), F32)] * unroll,
        compiler_params=params(),
        cost_estimate=pl.CostEstimate(
            flops=20 * 10**9, bytes_accessed=8 * 10**6, transcendentals=0
        ),
        name="demigrate_and_sample",
    )(
        column,
        times,
        times,
        times,
        amplitude,
        amplitude.reshape(bins_x * cut, res_bins, entries),
        trace_counts,
        counts_cut,
        place,
        place,
        place.reshape(bins_x * cut, 1, res_bins * entries),
        res_rows,
        ext,
        left,
        right,
        s1,
    )

    from_low = shift(out_right, "gy", 1)
    from_high = shift(out_left, "gy", -1)
    edge = jax.ShapeDtypeStruct((2, RADIUS, bins_y, depths), F32)
    out_head, inner, out_tail = pl.pallas_call(
        fold_y_kernel,
        out_shape=[edge, jax.ShapeDtypeStruct((2, bins_x, bins_y, depths), F32), edge],
        compiler_params=params(SMALL_LIMIT),
        name="fold_y",
    )(out_mid, from_low, from_high)
    from_low = shift(out_tail, "gx", 1)
    from_high = shift(out_head, "gx", -1)
    devices = lax.axis_size("gx") * lax.axis_size("gy")
    grads, stats = pl.pallas_call(
        fold_x_kernel,
        out_shape=[
            jax.ShapeDtypeStruct((2, bins_x, bins_y, depths), F32),
            jax.ShapeDtypeStruct((devices, 1, LANES), F32),
        ],
        compiler_params=params(SMALL_LIMIT),
        name="fold_x",
    )(inner, from_low, from_high, old_gradient, curv)
    stats = lax.all_to_all(stats, ("gx", "gy"), 0, 0, tiled=True)

    steps = 8
    rows_step = bins_x * rows_per // steps
    x_step = bins_x // steps
    cells = pl.BlockSpec((x_step, bins_y, depths), lambda i: (i, 0, 0))
    rows = pl.BlockSpec((rows_step, LANES), lambda i: (i, 0))
    image_shape = jax.ShapeDtypeStruct(direction.shape, F32)
    new_image, new_rows, new_direction = pl.pallas_call(
        last_kernel,
        grid=(steps,),
        in_specs=[
            pl.BlockSpec(stats.shape, lambda i: (0, 0, 0)),
            rows,
            rows,
            cells,
            cells,
            pl.BlockSpec((2, x_step, bins_y, depths), lambda i: (0, i, 0, 0)),
        ],
        out_specs=[cells, rows, cells],
        out_shape=[image_shape, jax.ShapeDtypeStruct(res_rows.shape, F32), image_shape],
        compiler_params=params(),
        name="update",
    )(stats, res_rows, data_rows, model_image, direction, grads)
    return (new_image, from_rows(new_rows, data_residual.shape), new_direction)


def solution(mesh):
    in_specs = (
        P("gx", "gy", None),
        P("gx", "gy", None),
        P("gx", "gy", None),
        P("gx", "gy", None),
        P("gx", "gy", None),
        P("gx", "gy", None, None),
        P("gx", "gy", None),
        P("gx", "gy"),
    )
    out_specs = (P("gx", "gy", None), P("gx", "gy", None), P("gx", "gy", None))
    return jax.shard_map(body, mesh=mesh, in_specs=in_specs, out_specs=out_specs, check_vma=False)
```

```python
import functools

import jax
import jax.numpy as jnp
from jax import lax
from jax.experimental import pallas as pl
from jax.experimental.pallas import tpu as pltpu
from jax.sharding import PartitionSpec as P

RADIUS = 8
SIDE = 2 * RADIUS + 1
LANES = 128
SUB = 8
F32 = jnp.float32
BF16 = jnp.bfloat16
VMEM_LIMIT = 51 * 1024 * 1024
MAIN_LIMIT = 44 * 1024 * 1024
SMALL_LIMIT = 24 * 1024 * 1024


def params(limit=VMEM_LIMIT):
    return pltpu.CompilerParams(vmem_limit_bytes=limit)


def to_rows(traces):
    bins_x, bins_y, samples = traces.shape
    parts = traces.reshape(bins_x, bins_y // SUB, SUB, samples // LANES, LANES)
    return parts.transpose(0, 1, 3, 2, 4).reshape(-1, LANES)


def from_rows(rows, shape):
    bins_x, bins_y, samples = shape
    parts = rows.reshape(bins_x, bins_y // SUB, samples // LANES, SUB, LANES)
    return parts.transpose(0, 1, 3, 2, 4).reshape(shape)


def trace_row(b, highs):
    return (b // SUB) * (SUB * highs) + b % SUB


def fill_weights(amp_ref, counts, scales):
    bins, entries = amp_ref.shape[1], amp_ref.shape[2]
    weight = amp_ref[0].T * counts.astype(F32)
    for b in range(bins):
        column = jnp.broadcast_to(weight[:, b : b + 1], (entries, LANES))
        scales[pl.ds(b * entries, entries), :] = column


def sample_bin(source, first, highs, times_ref, b, scales, vals):
    entries = times_ref.shape[1]
    for part in range(0, entries, SUB):
        times = times_ref[b, pl.ds(part, SUB), :]
        high = jnp.right_shift(times, LANES.bit_length() - 1)
        low = jnp.bitwise_and(times, LANES - 1)
        acc = jnp.zeros(times.shape, F32)
        for h in range(highs):
            table = source[pl.ds(first + SUB * h, SUB, stride=0), :]
            got = jnp.take_along_axis(table, low, axis=1, mode="promise_in_bounds")
            acc = jnp.where(high == h, got, acc)
        at = b * entries + part
        at = pl.ds(at if isinstance(at, int) else pl.multiple_of(at, SUB), SUB)
        vals[at, :] = acc * scales[at, :]


def spread_bins(vals, place_ref, s_ref, row, wide_y):
    span = SIDE * wide_y
    value = vals[...]
    upper = value.astype(BF16)
    lower = (value - upper.astype(F32)).astype(BF16)
    both = jnp.concatenate([upper, lower], axis=1)
    place = place_ref[0]
    iota = lax.broadcasted_iota(jnp.int32, (span, place.shape[1]), 0)
    table = jnp.where(iota == place, 1.0, 0.0).astype(BF16)
    part = jnp.dot(table, both, preferred_element_type=F32)
    s_ref[pl.ds(pl.multiple_of(row * wide_y, SUB), span), :] += part[:, :LANES] + part[:, LANES:]


def first_kernel(
    geo, row0, res_ref, times_ref, amp_ref, counts_ref, place_ref, prev_ref, s_ref, vals, scales
):
    bins_y, entries, highs, wide_y = geo
    step = pl.program_id(0)

    @pl.when(step == 0)
    def _():
        s_ref[...] = prev_ref[...]

    fill_weights(amp_ref, counts_ref[pl.ds(step + row0, 1), :], scales)
    for b in range(bins_y):
        sample_bin(res_ref, trace_row(b, highs), highs, times_ref, b, scales, vals)
    spread_bins(vals, place_ref, s_ref, step + row0, wide_y)


def scatter_bin(geo, b, image, col_ref, times_ref, scales, work):
    bins_y, entries, highs, wide_y = geo
    half = LANES // 2
    half_bits = half.bit_length() - 1
    iota16 = lax.broadcasted_iota(jnp.int32, (16, LANES), 0)
    iota_lo = [(iota16 + k).astype(F32).astype(BF16) for k in range(0, half, 16)]
    iota_hi = [(iota16 + k).astype(F32).astype(BF16) for k in range(0, 2 * highs, 16)]
    zero = jnp.zeros((), BF16)
    one = jnp.ones((), BF16)
    for e in range(entries):
        column = col_ref[0, b, e]
        work[0, pl.ds(e, 1), :] = image[pl.ds(column, 1), :]
    value = work[0, pl.ds(0, entries), :]
    value = value * scales[pl.ds(pl.multiple_of(b * entries, SUB), entries), :]
    upper = value.astype(BF16).astype(F32)
    times = times_ref[b]
    middle = jnp.bitwise_and(jnp.right_shift(times, half_bits), 1)
    rows = pl.ds(0, entries)
    work[0, rows, :] = upper
    work[1, rows, :] = value - upper
    work[2, rows, :] = jnp.bitwise_and(times, half - 1).astype(F32)
    work[3, rows, :] = (jnp.right_shift(times, half_bits + 1) + middle * highs).astype(F32)
    lefts = []
    rights = []
    for e in range(entries):

        def wide(k):
            row = work[k, pl.ds(e, SUB, stride=0), :]
            return jnp.concatenate([row, row], axis=0).astype(BF16)

        place = wide(3)
        hits = [place == iota for iota in iota_hi]
        parts = [jnp.where(hit, wide(k), zero) for k in range(2) for hit in hits]
        lefts.append(jnp.concatenate(parts, axis=0))
        low = wide(2)
        rights.append(
            jnp.concatenate([jnp.where(low == iota, one, zero) for iota in iota_lo], axis=0)
        )
    out = lax.dot_general(
        jnp.concatenate(lefts, axis=1),
        jnp.concatenate(rights, axis=1),
        (((1,), (1,)), ((), ())),
        preferred_element_type=F32,
    )
    out = out[: 2 * highs] + out[2 * highs :]
    return jnp.concatenate([out[:highs], out[highs:]], axis=1)


def main_kernel(
    geo,
    unroll,
    row0,
    col_ref,
    times_ref,
    old_times_ref,
    res_times_ref,
    amp_ref,
    res_amp_ref,
    counts_ref,
    res_counts_ref,
    old_place_ref,
    last_place_ref,
    res_place_ref,
    res_ref,
    mid_ref,
    left_ref,
    right_ref,
    s1_in_ref,
    data_ref,
    curv_ref,
    out_left,
    out_mid,
    out_right,
    image,
    s1_ref,
    s2_ref,
    vals,
    res_vals,
    scales,
    old_scales,
    res_scales,
    old_data,
    *works,
):
    bins_y, entries, highs, wide_y = geo
    step = pl.program_id(0)
    wide_x = mid_ref.shape[0]
    groups = bins_y // unroll
    res_bins = res_times_ref.shape[0]
    res_unroll = res_bins // groups

    @pl.when(step == 0)
    def _():
        s1_ref[...] = s1_in_ref[...]
        s2_ref[...] = jnp.zeros_like(s2_ref)
        curv_ref[...] = jnp.zeros_like(curv_ref)
        old_data[...] = jnp.zeros_like(old_data)
        scales[...] = jnp.zeros_like(scales)
        for x in range(wide_x):
            image[pl.ds(x * wide_y, RADIUS), :] = left_ref[x]
            image[pl.ds(x * wide_y + RADIUS, bins_y), :] = mid_ref[x]
            image[pl.ds(x * wide_y + RADIUS + bins_y, RADIUS), :] = right_ref[x]

    old_scales[...] = scales[...]
    fill_weights(amp_ref, counts_ref[pl.ds(step, 1), :], scales)
    fill_weights(res_amp_ref, res_counts_ref[0], res_scales)

    def some_bins(k, total):
        for u in range(unroll):
            b = k * unroll + u
            trace = scatter_bin(geo, b, image, col_ref, times_ref, scales, works[u])
            data_ref[pl.ds(trace_row(b, highs), highs, stride=SUB), :] = trace
            total = total + trace * trace
            first = trace_row(b, highs)
            sample_bin(old_data, first, highs, old_times_ref, b, old_scales, vals)
            if u < res_unroll:
                r = k * res_unroll + u
                first = trace_row(r, highs)
                sample_bin(res_ref, first, highs, res_times_ref, r, res_scales, res_vals)
        return total

    curv_ref[...] += lax.fori_loop(0, groups, some_bins, jnp.zeros((highs, LANES), F32))
    spread_bins(vals, old_place_ref, s2_ref, jnp.maximum(step - 1, 0), wide_y)
    spread_bins(res_vals, res_place_ref, s1_ref, row0 + (step * res_bins) // bins_y, wide_y)
    old_data[...] = data_ref[...]

    @pl.when(step == pl.num_programs(0) - 1)
    def _():
        for b in range(bins_y):
            sample_bin(old_data, trace_row(b, highs), highs, times_ref, b, scales, vals)
        spread_bins(vals, last_place_ref, s2_ref, step, wide_y)
        for k, ref in enumerate((s1_ref, s2_ref)):
            for x in range(wide_x):
                out_left[k, x] = ref[pl.ds(x * wide_y, RADIUS), :]
                out_mid[k, x] = ref[pl.ds(x * wide_y + RADIUS, bins_y), :]
                out_right[k, x] = ref[pl.ds(x * wide_y + RADIUS + bins_y, RADIUS), :]


def fold_y_kernel(mid_ref, low_ref, high_ref, out_head, out_mid, out_tail):
    wide_x, bins_y = mid_ref.shape[1], mid_ref.shape[2]
    bins_x = wide_x - 2 * RADIUS
    for k in range(2):
        for x in range(wide_x):
            if x < RADIUS:
                ref, at = out_head, x
            elif x < RADIUS + bins_x:
                ref, at = out_mid, x - RADIUS
            else:
                ref, at = out_tail, x - RADIUS - bins_x
            ref[k, at, pl.ds(0, RADIUS), :] = mid_ref[k, x, pl.ds(0, RADIUS), :] + low_ref[k, x]
            high = pl.ds(bins_y - RADIUS, RADIUS)
            ref[k, at, high, :] = mid_ref[k, x, high, :] + high_ref[k, x]


def fold_x_kernel(mid_ref, low_ref, high_ref, grad_ref, curv_ref, out_ref, stats_ref):
    bins_x = mid_ref.shape[1]
    sums = [jnp.zeros((1, LANES), F32) for _ in range(5)]
    for x in range(bins_x):
        pair = []
        for k in range(2):
            cells = mid_ref[k, x]
            if x < RADIUS:
                cells = cells + low_ref[k, x]
            else:
                cells = cells + high_ref[k, x - RADIUS]
            out_ref[k, x] = cells
            pair.append(cells)
        old = grad_ref[x]
        terms = (old * old, None, pair[0] * pair[0], pair[0] * pair[1], pair[1] * pair[1])
        for n, term in enumerate(terms):
            if term is not None:
                sums[n] = sums[n] + jnp.sum(term, axis=0, keepdims=True)
    sums[1] = jnp.sum(curv_ref[...], axis=0, keepdims=True)
    lane = lax.broadcasted_iota(jnp.int32, (1, LANES), 1)
    stats = jnp.zeros((1, LANES), F32)
    for n, term in enumerate(sums):
        stats = jnp.where(lane == n, jnp.sum(term, axis=1, keepdims=True), stats)
    stats_ref[...] = jnp.broadcast_to(stats[None], stats_ref.shape)


def last_kernel(
    stats_ref, res_ref, data_ref, model_ref, dir_ref, grad_ref, new_image, new_residual, new_dir
):
    stats = jnp.sum(stats_ref[...], axis=0)
    lane = lax.broadcasted_iota(jnp.int32, stats.shape, 1)

    def pick(n):
        return jnp.sum(jnp.where(lane == n, stats, 0.0), axis=1, keepdims=True)

    gamma, curvature, one_one, one_two, two_two = (pick(n) for n in range(5))
    alpha = gamma / curvature
    gamma_new = one_one - 2.0 * (alpha * one_two) + alpha * (alpha * two_two)
    beta = gamma_new / gamma
    new_residual[...] = res_ref[...] - alpha * data_ref[...]
    step = dir_ref[...]
    new_image[...] = model_ref[...] + alpha[None] * step
    new_dir[...] = (grad_ref[0] - alpha[None] * grad_ref[1]) + beta[None] * step


def shift(cells, axis, by):
    count = lax.axis_size(axis)
    pairs = [(i, i + by) for i in range(count) if 0 <= i + by < count]
    return lax.ppermute(cells, axis, pairs)


def body(
    model_image,
    data_residual,
    direction,
    old_gradient,
    aperture,
    travel_times,
    amplitude,
    trace_counts,
):
    bins_x, bins_y, samples = data_residual.shape
    entries, depths = travel_times.shape[2], travel_times.shape[3]
    highs = samples // LANES
    wide_x, wide_y = bins_x + 2 * RADIUS, bins_y + 2 * RADIUS
    columns = wide_x * wide_y
    span = SIDE * wide_y
    geo = (bins_y, entries, highs, wide_y)
    rows_per = bins_y * highs

    from_prev = shift(direction, "gx", 1)[bins_x - RADIUS :]
    from_next = shift(direction, "gx", -1)[:RADIUS]

    times = travel_times.reshape(bins_x * bins_y, entries, depths)
    res_rows = to_rows(data_residual)
    off = (aperture // SIDE) * wide_y + aperture % SIDE
    window = off + jnp.arange(bins_y, dtype=jnp.int32)[None, :, None]
    column = window + wide_y * jnp.arange(bins_x, dtype=jnp.int32)[:, None, None]
    place = window.reshape(bins_x, 1, bins_y * entries)

    def first(row0, count, prev):
        return pl.pallas_call(
            functools.partial(first_kernel, geo, row0),
            grid=(count,),
            in_specs=[
                pl.BlockSpec((rows_per, LANES), lambda i: (i + row0, 0)),
                pl.BlockSpec((bins_y, entries, depths), lambda i: (i + row0, 0, 0)),
                pl.BlockSpec((1, bins_y, entries), lambda i: (i + row0, 0, 0)),
                pl.BlockSpec((bins_x, bins_y), lambda i: (0, 0)),
                pl.BlockSpec((1, 1, bins_y * entries), lambda i: (i + row0, 0, 0)),
                pl.BlockSpec((columns, depths), lambda i: (0, 0)),
            ],
            out_specs=pl.BlockSpec((columns, depths), lambda i: (0, 0)),
            out_shape=jax.ShapeDtypeStruct((columns, depths), F32),
            scratch_shapes=[pltpu.VMEM((bins_y * entries, depths), F32)] * 2,
            compiler_params=params(),
            cost_estimate=pl.CostEstimate(
                flops=4 * 10**9, bytes_accessed=4 * 10**6, transcendentals=0
            ),
            name="sample_residual",
        )(res_rows, times, amplitude, trace_counts, place, prev)

    early = bins_x // 4
    row0 = 2 * early
    s1 = first(0, early, jnp.zeros((columns, depths), F32))
    ext = jnp.concatenate([from_prev, direction, from_next], axis=0)
    tail, head, s1 = lax.optimization_barrier((ext[:, bins_y - RADIUS :], ext[:, :RADIUS], s1))
    left = shift(tail, "gy", 1)
    right = shift(head, "gy", -1)
    s1 = first(early, early, s1)

    unroll = 8
    cut = bins_x // (bins_x - row0)
    res_bins = bins_y // cut
    counts_cut = trace_counts.reshape(bins_x * cut, 1, res_bins)
    whole3 = lambda i: (0, 0, 0)
    whole4 = lambda i: (0, 0, 0, 0)
    before = lambda i: (jnp.maximum(i - 1, 0), 0, 0)
    this = lambda i: (i, 0, 0)
    late = lambda i: (row0 * cut + i, 0, 0)
    strip = (2, wide_x, RADIUS, depths)
    middle = (2, wide_x, bins_y, depths)
    vals_shape = pltpu.VMEM((bins_y * entries, depths), F32)
    res_shape = pltpu.VMEM((res_bins * entries, depths), F32)
    columns_shape = pltpu.VMEM((columns, depths), F32)
    data_rows, curv, out_left, out_mid, out_right = pl.pallas_call(
        functools.partial(main_kernel, geo, unroll, row0),
        grid=(bins_x,),
        in_specs=[
            pl.BlockSpec((1, bins_y, entries), this, memory_space=pltpu.SMEM),
            pl.BlockSpec((bins_y, entries, depths), this),
            pl.BlockSpec((bins_y, entries, depths), before),
            pl.BlockSpec((res_bins, entries, depths), late),
            pl.BlockSpec((1, bins_y, entries), this),
            pl.BlockSpec((1, res_bins, entries), late),
            pl.BlockSpec((bins_x, bins_y), lambda i: (0, 0)),
            pl.BlockSpec((1, 1, res_bins), late),
            pl.BlockSpec((1, 1, bins_y * entries), before),
            pl.BlockSpec((1, 1, bins_y * entries), lambda i: (bins_x - 1, 0, 0)),
            pl.BlockSpec((1, 1, res_bins * entries), late),
            pl.BlockSpec((res_bins * highs, LANES), lambda i: (row0 * cut + i, 0)),
            pl.BlockSpec((wide_x, bins_y, depths), whole3),
            pl.BlockSpec((wide_x, RADIUS, depths), whole3),
            pl.BlockSpec((wide_x, RADIUS, depths), whole3),
            pl.BlockSpec((columns, depths), lambda i: (0, 0)),
        ],
        out_specs=[
            pl.BlockSpec((rows_per, LANES), lambda i: (i, 0)),
            pl.BlockSpec((highs, LANES), lambda i: (0, 0)),
            pl.BlockSpec(strip, whole4),
            pl.BlockSpec(middle, whole4),
            pl.BlockSpec(strip, whole4),
        ],
        out_shape=[
            jax.ShapeDtypeStruct((bins_x * rows_per, LANES), F32),
            jax.ShapeDtypeStruct((highs, LANES), F32),
            jax.ShapeDtypeStruct(strip, F32),
            jax.ShapeDtypeStruct(middle, F32),
            jax.ShapeDtypeStruct(strip, F32),
        ],
        scratch_shapes=[columns_shape, columns_shape, columns_shape]
        + [vals_shape, res_shape, vals_shape, vals_shape, res_shape]
        + [pltpu.VMEM((rows_per, LANES), F32)]
        + [pltpu.VMEM((4, entries + SUB, LANES), F32)] * unroll,
        compiler_params=params(MAIN_LIMIT),
        cost_estimate=pl.CostEstimate(
            flops=20 * 10**9, bytes_accessed=8 * 10**6, transcendentals=0
        ),
        name="demigrate_and_sample",
    )(
        column,
        times,
        times,
        times,
        amplitude,
        amplitude.reshape(bins_x * cut, res_bins, entries),
        trace_counts,
        counts_cut,
        place,
        place,
        place.reshape(bins_x * cut, 1, res_bins * entries),
        res_rows,
        ext,
        left,
        right,
        s1,
    )

    from_low = shift(out_right, "gy", 1)
    from_high = shift(out_left, "gy", -1)
    edge = jax.ShapeDtypeStruct((2, RADIUS, bins_y, depths), F32)
    out_head, inner, out_tail = pl.pallas_call(
        fold_y_kernel,
        out_shape=[edge, jax.ShapeDtypeStruct((2, bins_x, bins_y, depths), F32), edge],
        compiler_params=params(SMALL_LIMIT),
        name="fold_y",
    )(out_mid, from_low, from_high)
    from_low = shift(out_tail, "gx", 1)
    from_high = shift(out_head, "gx", -1)
    devices = lax.axis_size("gx") * lax.axis_size("gy")
    grads, stats = pl.pallas_call(
        fold_x_kernel,
        out_shape=[
            jax.ShapeDtypeStruct((2, bins_x, bins_y, depths), F32),
            jax.ShapeDtypeStruct((devices, 1, LANES), F32),
        ],
        compiler_params=params(SMALL_LIMIT),
        name="fold_x",
    )(inner, from_low, from_high, old_gradient, curv)
    stats = lax.all_to_all(stats, ("gx", "gy"), 0, 0, tiled=True)

    steps = 8
    rows_step = bins_x * rows_per // steps
    x_step = bins_x // steps
    cells = pl.BlockSpec((x_step, bins_y, depths), lambda i: (i, 0, 0))
    rows = pl.BlockSpec((rows_step, LANES), lambda i: (i, 0))
    image_shape = jax.ShapeDtypeStruct(direction.shape, F32)
    new_image, new_rows, new_direction = pl.pallas_call(
        last_kernel,
        grid=(steps,),
        in_specs=[
            pl.BlockSpec(stats.shape, lambda i: (0, 0, 0)),
            rows,
            rows,
            cells,
            cells,
            pl.BlockSpec((2, x_step, bins_y, depths), lambda i: (0, i, 0, 0)),
        ],
        out_specs=[cells, rows, cells],
        out_shape=[image_shape, jax.ShapeDtypeStruct(res_rows.shape, F32), image_shape],
        compiler_params=params(SMALL_LIMIT),
        name="update",
    )(stats, res_rows, data_rows, model_image, direction, grads)
    return (new_image, from_rows(new_rows, data_residual.shape), new_direction)


def solution(mesh):
    in_specs = (
        P("gx", "gy", None),
        P("gx", "gy", None),
        P("gx", "gy", None),
        P("gx", "gy", None),
        P("gx", "gy", None),
        P("gx", "gy", None, None),
        P("gx", "gy", None),
        P("gx", "gy"),
    )
    out_specs = (P("gx", "gy", None), P("gx", "gy", None), P("gx", "gy", None))
    return jax.shard_map(body, mesh=mesh, in_specs=in_specs, out_specs=out_specs, check_vma=False)
```

```python
import functools

import jax
import jax.numpy as jnp
from jax import lax
from jax.experimental import pallas as pl
from jax.experimental.pallas import tpu as pltpu
from jax.sharding import PartitionSpec as P

RADIUS = 8
SIDE = 2 * RADIUS + 1
LANES = 128
SUB = 8
F32 = jnp.float32
BF16 = jnp.bfloat16
VMEM_LIMIT = 51 * 1024 * 1024
FIRST_LIMIT = 60 * 1024 * 1024
MAIN_LIMIT = 36 * 1024 * 1024
SMALL_LIMIT = 24 * 1024 * 1024


def params(limit=VMEM_LIMIT):
    return pltpu.CompilerParams(vmem_limit_bytes=limit)


def to_rows(traces):
    bins_x, bins_y, samples = traces.shape
    parts = traces.reshape(bins_x, bins_y // SUB, SUB, samples // LANES, LANES)
    return parts.transpose(0, 1, 3, 2, 4).reshape(-1, LANES)


def from_rows(rows, shape):
    bins_x, bins_y, samples = shape
    parts = rows.reshape(bins_x, bins_y // SUB, samples // LANES, SUB, LANES)
    return parts.transpose(0, 1, 3, 2, 4).reshape(shape)


def trace_row(b, highs):
    return (b // SUB) * (SUB * highs) + b % SUB


def fill_weights(amplitude, counts, scales):
    bins, entries = amplitude.shape
    weight = amplitude.T * counts.astype(F32)
    for b in range(bins):
        column = jnp.broadcast_to(weight[:, b : b + 1], (entries, LANES))
        scales[pl.ds(b * entries, entries), :] = column


def sample_bin(source, first, highs, times_ref, bin_at, b, scales, vals):
    entries = times_ref.shape[1]
    for part in range(0, entries, SUB):
        times = times_ref[bin_at, pl.ds(part, SUB), :]
        high = jnp.right_shift(times, LANES.bit_length() - 1)
        low = jnp.bitwise_and(times, LANES - 1)
        acc = jnp.zeros(times.shape, F32)
        for h in range(highs):
            table = source[pl.ds(first + SUB * h, SUB, stride=0), :]
            got = jnp.take_along_axis(table, low, axis=1, mode="promise_in_bounds")
            acc = jnp.where(high == h, got, acc)
        at = b * entries + part
        at = pl.ds(at if isinstance(at, int) else pl.multiple_of(at, SUB), SUB)
        vals[at, :] = acc * scales[at, :]


def column_offset(entry, wide_y):
    return entry + jnp.right_shift(entry * 241, 12) * (wide_y - SIDE)


def place_row(aperture, wide_y, first_bin=0):
    offset = column_offset(aperture, wide_y)
    return jnp.concatenate(
        [offset[b : b + 1, :] + (b + first_bin) for b in range(offset.shape[0])], axis=1
    )


def spread_bins(vals, place, s_ref, row, wide_y):
    span = SIDE * wide_y
    value = vals[...]
    upper = value.astype(BF16)
    lower = (value - upper.astype(F32)).astype(BF16)
    both = jnp.concatenate([upper, lower], axis=1)
    iota = lax.broadcasted_iota(jnp.int32, (span, place.shape[1]), 0)
    table = jnp.where(iota == place, 1.0, 0.0).astype(BF16)
    part = jnp.dot(table, both, preferred_element_type=F32)
    s_ref[pl.ds(pl.multiple_of(row * wide_y, SUB), span), :] += part[:, :LANES] + part[:, LANES:]


def first_kernel(
    geo, row0, res_ref, times_ref, amp_ref, counts_ref, aper_ref, *refs
):
    bins_y, entries, highs, wide_y = geo
    step = pl.program_id(0)
    s_ref, vals, scales = refs[-3:]

    @pl.when(step == 0)
    def _():
        s_ref[...] = refs[0][...] if len(refs) > 3 else jnp.zeros_like(s_ref)

    fill_weights(amp_ref[0], counts_ref[pl.ds(step + row0, 1), :], scales)
    for b in range(bins_y):
        sample_bin(res_ref, trace_row(b, highs), highs, times_ref, b, b, scales, vals)
    spread_bins(vals, place_row(aper_ref[0], wide_y), s_ref, step + row0, wide_y)


def scatter_bin(geo, row, b, image, entry_ref, times_ref, scales, work):
    bins_y, entries, highs, wide_y = geo
    half = LANES // 2
    half_bits = half.bit_length() - 1
    iota16 = lax.broadcasted_iota(jnp.int32, (16, LANES), 0)
    iota_lo = [(iota16 + k).astype(F32).astype(BF16) for k in range(0, half, 16)]
    iota_hi = [(iota16 + k).astype(F32).astype(BF16) for k in range(0, 2 * highs, 16)]
    zero = jnp.zeros((), BF16)
    one = jnp.ones((), BF16)
    for e in range(entries):
        column = column_offset(entry_ref[row, b, e], wide_y) + (row * wide_y + b)
        work[0, pl.ds(e, 1), :] = image[pl.ds(column, 1), :]
    value = work[0, pl.ds(0, entries), :]
    value = value * scales[pl.ds(b * entries, entries), :]
    upper = value.astype(BF16).astype(F32)
    times = times_ref[row * bins_y + b]
    middle = jnp.bitwise_and(jnp.right_shift(times, half_bits), 1)
    rows = pl.ds(0, entries)
    work[0, rows, :] = upper
    work[1, rows, :] = value - upper
    work[2, rows, :] = jnp.bitwise_and(times, half - 1).astype(F32)
    work[3, rows, :] = (jnp.right_shift(times, half_bits + 1) + middle * highs).astype(F32)
    lefts = []
    rights = []
    for e in range(entries):

        def wide(k):
            row = work[k, pl.ds(e, SUB, stride=0), :]
            return jnp.concatenate([row, row], axis=0).astype(BF16)

        place = wide(3)
        hits = [place == iota for iota in iota_hi]
        parts = [jnp.where(hit, wide(k), zero) for k in range(2) for hit in hits]
        lefts.append(jnp.concatenate(parts, axis=0))
        low = wide(2)
        rights.append(
            jnp.concatenate([jnp.where(low == iota, one, zero) for iota in iota_lo], axis=0)
        )
    out = lax.dot_general(
        jnp.concatenate(lefts, axis=1),
        jnp.concatenate(rights, axis=1),
        (((1,), (1,)), ((), ())),
        preferred_element_type=F32,
    )
    out = out[: 2 * highs] + out[2 * highs :]
    return jnp.concatenate([out[:highs], out[highs:]], axis=1)


def main_kernel(
    geo,
    row0,
    entry_ref,
    times_ref,
    amp_ref,
    counts_ref,
    parts_ref,
    aper_ref,
    res_ref,
    mid_ref,
    left_ref,
    right_ref,
    s1_in_ref,
    data_ref,
    curv_ref,
    out_left,
    out_mid,
    out_right,
    image,
    s1_ref,
    s2_ref,
    vals,
    res_vals,
    scales,
    old_scales,
    res_scales,
    old_data,
    *works,
):
    bins_y, entries, highs, wide_y = geo
    bins_x = amp_ref.shape[0]
    wide_x = mid_ref.shape[0]
    rows_per = bins_y * highs
    cut = bins_x // (bins_x - row0)
    res_bins = bins_y // cut

    s1_ref[...] = s1_in_ref[...]
    s2_ref[...] = jnp.zeros_like(s2_ref)
    old_data[...] = jnp.zeros_like(old_data)
    scales[...] = jnp.zeros_like(scales)
    for x in range(wide_x):
        image[pl.ds(x * wide_y, RADIUS), :] = left_ref[x]
        image[pl.ds(x * wide_y + RADIUS, bins_y), :] = mid_ref[x]
        image[pl.ds(x * wide_y + RADIUS + bins_y, RADIUS), :] = right_ref[x]

    def one_row(step, total):
        before = jnp.maximum(step - 1, 0)
        res_row = row0 + step // cut
        res_part = (step % cut) * res_bins
        res_first = pl.multiple_of(res_row * rows_per + res_part * highs, SUB)
        old_scales[...] = scales[...]
        fill_weights(amp_ref[step], counts_ref[pl.ds(step, 1), :], scales)
        fill_weights(
            amp_ref[res_row, pl.ds(pl.multiple_of(res_part, SUB), res_bins), :],
            parts_ref[pl.ds(row0 * cut + step, 1), :],
            res_scales,
        )
        for b in range(bins_y):
            trace = scatter_bin(
                geo, step, b, image, entry_ref, times_ref, scales, works[b % len(works)]
            )
            first = trace_row(b, highs)
            data_ref[pl.ds(step * rows_per + first, highs, stride=SUB), :] = trace
            total = total + trace * trace
            sample_bin(
                old_data, first, highs, times_ref, before * bins_y + b, b, old_scales, vals
            )
            if b % cut == 0:
                r = b // cut
                first = res_first + trace_row(r, highs)
                at = res_row * bins_y + res_part + r
                sample_bin(res_ref, first, highs, times_ref, at, r, res_scales, res_vals)
        spread_bins(vals, place_row(aper_ref[before], wide_y), s2_ref, before, wide_y)
        entry = aper_ref[res_row, pl.ds(pl.multiple_of(res_part, SUB), res_bins), :]
        spread_bins(res_vals, place_row(entry, wide_y, res_part), s1_ref, res_row, wide_y)
        old_data[...] = data_ref[pl.ds(pl.multiple_of(step * rows_per, SUB), rows_per), :]
        return total

    curv_ref[...] = lax.fori_loop(0, bins_x, one_row, jnp.zeros((highs, LANES), F32))
    last = bins_x - 1
    for b in range(bins_y):
        at = last * bins_y + b
        sample_bin(old_data, trace_row(b, highs), highs, times_ref, at, b, scales, vals)
    spread_bins(vals, place_row(aper_ref[last], wide_y), s2_ref, last, wide_y)
    for k, ref in enumerate((s1_ref, s2_ref)):
        for x in range(wide_x):
            out_left[k, x] = ref[pl.ds(x * wide_y, RADIUS), :]
            out_mid[k, x] = ref[pl.ds(x * wide_y + RADIUS, bins_y), :]
            out_right[k, x] = ref[pl.ds(x * wide_y + RADIUS + bins_y, RADIUS), :]


def fold_y_kernel(mid_ref, low_ref, high_ref, out_head, out_mid, out_tail):
    wide_x, bins_y = mid_ref.shape[1], mid_ref.shape[2]
    bins_x = wide_x - 2 * RADIUS
    for k in range(2):
        for x in range(wide_x):
            if x < RADIUS:
                ref, at = out_head, x
            elif x < RADIUS + bins_x:
                ref, at = out_mid, x - RADIUS
            else:
                ref, at = out_tail, x - RADIUS - bins_x
            ref[k, at, pl.ds(0, RADIUS), :] = mid_ref[k, x, pl.ds(0, RADIUS), :] + low_ref[k, x]
            high = pl.ds(bins_y - RADIUS, RADIUS)
            ref[k, at, high, :] = mid_ref[k, x, high, :] + high_ref[k, x]


def fold_x_kernel(mid_ref, low_ref, high_ref, grad_ref, curv_ref, out_ref, stats_ref):
    bins_x = mid_ref.shape[1]
    sums = [jnp.zeros((1, LANES), F32) for _ in range(5)]
    for x in range(bins_x):
        pair = []
        for k in range(2):
            cells = mid_ref[k, x]
            if x < RADIUS:
                cells = cells + low_ref[k, x]
            else:
                cells = cells + high_ref[k, x - RADIUS]
            out_ref[k, x] = cells
            pair.append(cells)
        old = grad_ref[x]
        terms = (old * old, None, pair[0] * pair[0], pair[0] * pair[1], pair[1] * pair[1])
        for n, term in enumerate(terms):
            if term is not None:
                sums[n] = sums[n] + jnp.sum(term, axis=0, keepdims=True)
    sums[1] = jnp.sum(curv_ref[...], axis=0, keepdims=True)
    lane = lax.broadcasted_iota(jnp.int32, (1, LANES), 1)
    stats = jnp.zeros((1, LANES), F32)
    for n, term in enumerate(sums):
        stats = jnp.where(lane == n, jnp.sum(term, axis=1, keepdims=True), stats)
    stats_ref[...] = jnp.broadcast_to(stats[None], stats_ref.shape)


def last_kernel(
    stats_ref, res_ref, data_ref, model_ref, dir_ref, grad_ref, new_image, new_residual, new_dir
):
    stats = jnp.sum(stats_ref[...], axis=0)
    lane = lax.broadcasted_iota(jnp.int32, stats.shape, 1)

    def pick(n):
        return jnp.sum(jnp.where(lane == n, stats, 0.0), axis=1, keepdims=True)

    gamma, curvature, one_one, one_two, two_two = (pick(n) for n in range(5))
    alpha = gamma / curvature
    gamma_new = one_one - 2.0 * (alpha * one_two) + alpha * (alpha * two_two)
    beta = gamma_new / gamma
    new_residual[...] = res_ref[...] - alpha * data_ref[...]
    step = dir_ref[...]
    new_image[...] = model_ref[...] + alpha[None] * step
    new_dir[...] = (grad_ref[0] - alpha[None] * grad_ref[1]) + beta[None] * step


def shift(cells, axis, by):
    count = lax.axis_size(axis)
    pairs = [(i, i + by) for i in range(count) if 0 <= i + by < count]
    return lax.ppermute(cells, axis, pairs)


def body(
    model_image,
    data_residual,
    direction,
    old_gradient,
    aperture,
    travel_times,
    amplitude,
    trace_counts,
):
    bins_x, bins_y, samples = data_residual.shape
    entries, depths = travel_times.shape[2], travel_times.shape[3]
    highs = samples // LANES
    wide_x, wide_y = bins_x + 2 * RADIUS, bins_y + 2 * RADIUS
    columns = wide_x * wide_y
    span = SIDE * wide_y
    geo = (bins_y, entries, highs, wide_y)
    rows_per = bins_y * highs

    from_prev = shift(direction, "gx", 1)[bins_x - RADIUS :]
    from_next = shift(direction, "gx", -1)[:RADIUS]

    times = travel_times.reshape(bins_x * bins_y, entries, depths)
    res_rows = to_rows(data_residual)
    def first(row0, count, prev, limit):
        return pl.pallas_call(
            functools.partial(first_kernel, geo, row0),
            grid=(count,),
            in_specs=[
                pl.BlockSpec((rows_per, LANES), lambda i: (i + row0, 0)),
                pl.BlockSpec((bins_y, entries, depths), lambda i: (i + row0, 0, 0)),
                pl.BlockSpec((1, bins_y, entries), lambda i: (i + row0, 0, 0)),
                pl.BlockSpec((bins_x, bins_y), lambda i: (0, 0)),
                pl.BlockSpec((1, bins_y, entries), lambda i: (i + row0, 0, 0)),
            ]
            + [pl.BlockSpec((columns, depths), lambda i: (0, 0))] * len(prev),
            out_specs=pl.BlockSpec((columns, depths), lambda i: (0, 0)),
            out_shape=jax.ShapeDtypeStruct((columns, depths), F32),
            scratch_shapes=[pltpu.VMEM((bins_y * entries, depths), F32)] * 2,
            compiler_params=params(limit),
            cost_estimate=pl.CostEstimate(
                flops=4 * 10**9, bytes_accessed=4 * 10**6, transcendentals=0
            ),
            name="sample_residual",
        )(res_rows, times, amplitude, trace_counts, aperture, *prev)

    early = bins_x // 4
    row0 = 2 * early
    s1 = first(0, early, (), FIRST_LIMIT)
    ext = jnp.concatenate([from_prev, direction, from_next], axis=0)
    tail, head, s1 = lax.optimization_barrier((ext[:, bins_y - RADIUS :], ext[:, :RADIUS], s1))
    left = shift(tail, "gy", 1)
    right = shift(head, "gy", -1)
    s1 = first(early, early, (s1,), VMEM_LIMIT)

    cut = bins_x // (bins_x - row0)
    res_bins = bins_y // cut
    parts = trace_counts.reshape(bins_x * cut, res_bins)
    strip = jax.ShapeDtypeStruct((2, wide_x, RADIUS, depths), F32)
    vals_shape = pltpu.VMEM((bins_y * entries, depths), F32)
    res_shape = pltpu.VMEM((res_bins * entries, depths), F32)
    columns_shape = pltpu.VMEM((columns, depths), F32)
    in_vmem = pl.BlockSpec(memory_space=pltpu.VMEM)
    data_rows, curv, out_left, out_mid, out_right = pl.pallas_call(
        functools.partial(main_kernel, geo, row0),
        in_specs=[pl.BlockSpec(memory_space=pltpu.SMEM)] + [in_vmem] * 10,
        out_specs=[in_vmem] * 5,
        out_shape=[
            jax.ShapeDtypeStruct((bins_x * rows_per, LANES), F32),
            jax.ShapeDtypeStruct((highs, LANES), F32),
            strip,
            jax.ShapeDtypeStruct((2, wide_x, bins_y, depths), F32),
            strip,
        ],
        scratch_shapes=[columns_shape, columns_shape, columns_shape]
        + [vals_shape, res_shape, vals_shape, vals_shape, res_shape]
        + [pltpu.VMEM((rows_per, LANES), F32)]
        + [pltpu.VMEM((4, entries + SUB, LANES), F32)] * 8,
        compiler_params=params(MAIN_LIMIT),
        cost_estimate=pl.CostEstimate(
            flops=20 * 10**9, bytes_accessed=8 * 10**6, transcendentals=0
        ),
        name="demigrate_and_sample",
    )(
        aperture,
        times,
        amplitude,
        trace_counts,
        parts,
        aperture,
        res_rows,
        ext,
        left,
        right,
        s1,
    )

    from_low = shift(out_right, "gy", 1)
    from_high = shift(out_left, "gy", -1)
    edge = jax.ShapeDtypeStruct((2, RADIUS, bins_y, depths), F32)
    out_head, inner, out_tail = pl.pallas_call(
        fold_y_kernel,
        out_shape=[edge, jax.ShapeDtypeStruct((2, bins_x, bins_y, depths), F32), edge],
        compiler_params=params(SMALL_LIMIT),
        name="fold_y",
    )(out_mid, from_low, from_high)
    from_low = shift(out_tail, "gx", 1)
    from_high = shift(out_head, "gx", -1)
    devices = lax.axis_size("gx") * lax.axis_size("gy")
    grads, stats = pl.pallas_call(
        fold_x_kernel,
        out_shape=[
            jax.ShapeDtypeStruct((2, bins_x, bins_y, depths), F32),
            jax.ShapeDtypeStruct((devices, 1, LANES), F32),
        ],
        compiler_params=params(SMALL_LIMIT),
        name="fold_x",
    )(inner, from_low, from_high, old_gradient, curv)
    stats = lax.all_to_all(stats, ("gx", "gy"), 0, 0, tiled=True)

    steps = 4
    rows_step = bins_x * rows_per // steps
    x_step = bins_x // steps
    cells = pl.BlockSpec((x_step, bins_y, depths), lambda i: (i, 0, 0))
    rows = pl.BlockSpec((rows_step, LANES), lambda i: (i, 0))
    image_shape = jax.ShapeDtypeStruct(direction.shape, F32)
    new_image, new_rows, new_direction = pl.pallas_call(
        last_kernel,
        grid=(steps,),
        in_specs=[
            pl.BlockSpec(stats.shape, lambda i: (0, 0, 0)),
            rows,
            rows,
            cells,
            cells,
            pl.BlockSpec((2, x_step, bins_y, depths), lambda i: (0, i, 0, 0)),
        ],
        out_specs=[cells, rows, cells],
        out_shape=[image_shape, jax.ShapeDtypeStruct(res_rows.shape, F32), image_shape],
        compiler_params=params(SMALL_LIMIT),
        name="update",
    )(stats, res_rows, data_rows, model_image, direction, grads)
    return (new_image, from_rows(new_rows, data_residual.shape), new_direction)


def solution(mesh):
    in_specs = (
        P("gx", "gy", None),
        P("gx", "gy", None),
        P("gx", "gy", None),
        P("gx", "gy", None),
        P("gx", "gy", None),
        P("gx", "gy", None, None),
        P("gx", "gy", None),
        P("gx", "gy"),
    )
    out_specs = (P("gx", "gy", None), P("gx", "gy", None), P("gx", "gy", None))
    return jax.shard_map(body, mesh=mesh, in_specs=in_specs, out_specs=out_specs, check_vma=False)
```

```python
import functools

import jax
import jax.numpy as jnp
from jax import lax
from jax.experimental import pallas as pl
from jax.experimental.pallas import tpu as pltpu
from jax.sharding import PartitionSpec as P

RADIUS = 8
SIDE = 2 * RADIUS + 1
LANES = 128
SUB = 8
F32 = jnp.float32
BF16 = jnp.bfloat16
VMEM_LIMIT = 51 * 1024 * 1024
FIRST_LIMIT = 59 * 1024 * 1024
MAIN_LIMIT = 36 * 1024 * 1024
SMALL_LIMIT = 24 * 1024 * 1024


def params(limit=VMEM_LIMIT):
    return pltpu.CompilerParams(vmem_limit_bytes=limit)


def to_rows(traces):
    bins_x, bins_y, samples = traces.shape
    parts = traces.reshape(bins_x, bins_y // SUB, SUB, samples // LANES, LANES)
    return parts.transpose(0, 1, 3, 2, 4).reshape(-1, LANES)


def from_rows(rows, shape):
    bins_x, bins_y, samples = shape
    parts = rows.reshape(bins_x, bins_y // SUB, samples // LANES, SUB, LANES)
    return parts.transpose(0, 1, 3, 2, 4).reshape(shape)


def trace_row(b, highs):
    return (b // SUB) * (SUB * highs) + b % SUB


def fill_weights(amplitude, counts, scales):
    bins, entries = amplitude.shape
    weight = amplitude.T * counts.astype(F32)
    for b in range(bins):
        column = jnp.broadcast_to(weight[:, b : b + 1], (entries, LANES))
        scales[pl.ds(b * entries, entries), :] = column


def sample_bin(source, first, highs, times_ref, bin_at, b, scales, vals):
    entries = times_ref.shape[1]
    tables = [source[pl.ds(first + SUB * h, SUB, stride=0), :] for h in range(highs)]
    for part in range(0, entries, SUB):
        times = times_ref[bin_at, pl.ds(part, SUB), :]
        high = jnp.right_shift(times, LANES.bit_length() - 1)
        low = jnp.bitwise_and(times, LANES - 1)
        acc = jnp.zeros(times.shape, F32)
        for h in range(highs):
            got = jnp.take_along_axis(tables[h], low, axis=1, mode="promise_in_bounds")
            acc = jnp.where(high == h, got, acc)
        at = b * entries + part
        at = pl.ds(at if isinstance(at, int) else pl.multiple_of(at, SUB), SUB)
        vals[at, :] = acc * scales[at, :]


def column_offset(entry, wide_y):
    return entry + jnp.right_shift(entry * 241, 12) * (wide_y - SIDE)


def place_row(aperture, wide_y, first_bin=0):
    offset = column_offset(aperture, wide_y)
    return jnp.concatenate(
        [offset[b : b + 1, :] + (b + first_bin) for b in range(offset.shape[0])], axis=1
    )


def split_values(vals):
    value = vals[...]
    upper = value.astype(BF16)
    lower = (value - upper.astype(F32)).astype(BF16)
    return jnp.concatenate([upper, lower], axis=1)


def spread_bins(both, place, s_ref, row, wide_y):
    span = SIDE * wide_y
    iota = lax.broadcasted_iota(jnp.int32, (span, place.shape[1]), 0)
    table = jnp.where(iota == place, 1.0, 0.0).astype(BF16)
    part = jnp.dot(table, both, preferred_element_type=F32)
    s_ref[pl.ds(pl.multiple_of(row * wide_y, SUB), span), :] += part[:, :LANES] + part[:, LANES:]


def first_kernel(
    geo, row0, res_ref, times_ref, amp_ref, counts_ref, aper_ref, s_ref, vals, scales
):
    bins_y, entries, highs, wide_y = geo
    step = pl.program_id(0)

    @pl.when(step == 0)
    def _():
        s_ref[...] = jnp.zeros_like(s_ref)

    fill_weights(amp_ref[0], counts_ref[pl.ds(step + row0, 1), :], scales)
    for b in range(bins_y):
        sample_bin(res_ref, trace_row(b, highs), highs, times_ref, b, b, scales, vals)
    both = split_values(vals)
    spread_bins(both, place_row(aper_ref[0], wide_y), s_ref, step + row0, wide_y)


def scatter_bin(geo, row, b, image, entry_ref, times_ref, scales, work):
    bins_y, entries, highs, wide_y = geo
    half = LANES // 2
    half_bits = half.bit_length() - 1
    iota16 = lax.broadcasted_iota(jnp.int32, (16, LANES), 0)
    iota_lo = [(iota16 + k).astype(F32).astype(BF16) for k in range(0, half, 16)]
    iota_hi = [(iota16 + k).astype(F32).astype(BF16) for k in range(0, 2 * highs, 16)]
    zero = jnp.zeros((), BF16)
    one = jnp.ones((), BF16)
    for e in range(entries):
        column = column_offset(entry_ref[row, b, e], wide_y) + (row * wide_y + b)
        work[0, pl.ds(e, 1), :] = image[pl.ds(column, 1), :]
    value = work[0, pl.ds(0, entries), :]
    value = value * scales[pl.ds(b * entries, entries), :]
    upper = value.astype(BF16).astype(F32)
    times = times_ref[row * bins_y + b]
    middle = jnp.bitwise_and(jnp.right_shift(times, half_bits), 1)
    rows = pl.ds(0, entries)
    work[0, rows, :] = upper
    work[1, rows, :] = value - upper
    work[2, rows, :] = jnp.bitwise_and(times, half - 1).astype(F32)
    work[3, rows, :] = (jnp.right_shift(times, half_bits + 1) + middle * highs).astype(F32)
    lefts = []
    rights = []
    for e in range(entries):

        def wide(k):
            row = work[k, pl.ds(e, SUB, stride=0), :]
            return jnp.concatenate([row, row], axis=0).astype(BF16)

        place = wide(3)
        hits = [place == iota for iota in iota_hi]
        parts = [jnp.where(hit, wide(k), zero) for k in range(2) for hit in hits]
        lefts.append(jnp.concatenate(parts, axis=0))
        low = wide(2)
        rights.append(
            jnp.concatenate([jnp.where(low == iota, one, zero) for iota in iota_lo], axis=0)
        )
    out = lax.dot_general(
        jnp.concatenate(lefts, axis=1),
        jnp.concatenate(rights, axis=1),
        (((1,), (1,)), ((), ())),
        preferred_element_type=F32,
    )
    out = out[: 2 * highs] + out[2 * highs :]
    return jnp.concatenate([out[:highs], out[highs:]], axis=1)


def main_kernel(
    geo,
    row0,
    entry_ref,
    times_ref,
    amp_ref,
    counts_ref,
    parts_ref,
    aper_ref,
    res_ref,
    mid_ref,
    left_ref,
    right_ref,
    s1_in_ref,
    s1_more_ref,
    data_ref,
    curv_ref,
    out_left,
    out_mid,
    out_right,
    image,
    s1_ref,
    s2_ref,
    vals,
    res_vals,
    scales,
    old_scales,
    res_scales,
    old_data,
    both,
    res_both,
    *works,
):
    bins_y, entries, highs, wide_y = geo
    bins_x = amp_ref.shape[0]
    wide_x = mid_ref.shape[0]
    rows_per = bins_y * highs
    cut = bins_x // (bins_x - row0)
    res_bins = bins_y // cut

    s1_ref[...] = s1_in_ref[...] + s1_more_ref[...]
    s2_ref[...] = jnp.zeros_like(s2_ref)
    old_data[...] = jnp.zeros_like(old_data)
    scales[...] = jnp.zeros_like(scales)
    both[...] = jnp.zeros_like(both)
    res_both[...] = jnp.zeros_like(res_both)
    for x in range(wide_x):
        image[pl.ds(x * wide_y, RADIUS), :] = left_ref[x]
        image[pl.ds(x * wide_y + RADIUS, bins_y), :] = mid_ref[x]
        image[pl.ds(x * wide_y + RADIUS + bins_y, RADIUS), :] = right_ref[x]

    def residual_part(step):
        return row0 + step // cut, (step % cut) * res_bins

    def spread_image(row):
        spread_bins(both[...], place_row(aper_ref[row], wide_y), s2_ref, row, wide_y)

    def spread_residual(step):
        row, part = residual_part(step)
        entry = aper_ref[row, pl.ds(pl.multiple_of(part, SUB), res_bins), :]
        spread_bins(res_both[...], place_row(entry, wide_y, part), s1_ref, row, wide_y)

    def one_row(step, total):
        before = jnp.maximum(step - 1, 0)
        spread_image(jnp.maximum(step - 2, 0))
        spread_residual(before)
        res_row, res_part = residual_part(step)
        res_first = pl.multiple_of(res_row * rows_per + res_part * highs, SUB)
        old_scales[...] = scales[...]
        fill_weights(amp_ref[step], counts_ref[pl.ds(step, 1), :], scales)
        fill_weights(
            amp_ref[res_row, pl.ds(pl.multiple_of(res_part, SUB), res_bins), :],
            parts_ref[pl.ds(row0 * cut + step, 1), :],
            res_scales,
        )
        for b in range(bins_y):
            trace = scatter_bin(
                geo, step, b, image, entry_ref, times_ref, scales, works[b % len(works)]
            )
            first = trace_row(b, highs)
            data_ref[pl.ds(step * rows_per + first, highs, stride=SUB), :] = trace
            total = total + trace * trace
            sample_bin(
                old_data, first, highs, times_ref, before * bins_y + b, b, old_scales, vals
            )
            if b % cut == 0:
                r = b // cut
                first = res_first + trace_row(r, highs)
                at = res_row * bins_y + res_part + r
                sample_bin(res_ref, first, highs, times_ref, at, r, res_scales, res_vals)
        both[...] = split_values(vals)
        res_both[...] = split_values(res_vals)
        old_data[...] = data_ref[pl.ds(pl.multiple_of(step * rows_per, SUB), rows_per), :]
        return total

    curv_ref[...] = lax.fori_loop(0, bins_x, one_row, jnp.zeros((highs, LANES), F32))
    last = bins_x - 1
    spread_image(last - 1)
    spread_residual(last)
    for b in range(bins_y):
        at = last * bins_y + b
        sample_bin(old_data, trace_row(b, highs), highs, times_ref, at, b, scales, vals)
    both[...] = split_values(vals)
    spread_image(last)
    for k, ref in enumerate((s1_ref, s2_ref)):
        for x in range(wide_x):
            out_left[k, x] = ref[pl.ds(x * wide_y, RADIUS), :]
            out_mid[k, x] = ref[pl.ds(x * wide_y + RADIUS, bins_y), :]
            out_right[k, x] = ref[pl.ds(x * wide_y + RADIUS + bins_y, RADIUS), :]


def fold_y_kernel(mid_ref, low_ref, high_ref, out_head, out_mid, out_tail):
    wide_x, bins_y = mid_ref.shape[1], mid_ref.shape[2]
    bins_x = wide_x - 2 * RADIUS
    for k in range(2):
        for x in range(wide_x):
            if x < RADIUS:
                ref, at = out_head, x
            elif x < RADIUS + bins_x:
                ref, at = out_mid, x - RADIUS
            else:
                ref, at = out_tail, x - RADIUS - bins_x
            ref[k, at, pl.ds(0, RADIUS), :] = mid_ref[k, x, pl.ds(0, RADIUS), :] + low_ref[k, x]
            high = pl.ds(bins_y - RADIUS, RADIUS)
            ref[k, at, high, :] = mid_ref[k, x, high, :] + high_ref[k, x]


def fold_x_kernel(mid_ref, low_ref, high_ref, grad_ref, curv_ref, out_ref, stats_ref):
    bins_x = mid_ref.shape[1]
    sums = [jnp.zeros((1, LANES), F32) for _ in range(5)]
    for x in range(bins_x):
        pair = []
        for k in range(2):
            cells = mid_ref[k, x]
            if x < RADIUS:
                cells = cells + low_ref[k, x]
            else:
                cells = cells + high_ref[k, x - RADIUS]
            out_ref[k, x] = cells
            pair.append(cells)
        old = grad_ref[x]
        terms = (old * old, None, pair[0] * pair[0], pair[0] * pair[1], pair[1] * pair[1])
        for n, term in enumerate(terms):
            if term is not None:
                sums[n] = sums[n] + jnp.sum(term, axis=0, keepdims=True)
    sums[1] = jnp.sum(curv_ref[...], axis=0, keepdims=True)
    lane = lax.broadcasted_iota(jnp.int32, (1, LANES), 1)
    stats = jnp.zeros((1, LANES), F32)
    for n, term in enumerate(sums):
        stats = jnp.where(lane == n, jnp.sum(term, axis=1, keepdims=True), stats)
    stats_ref[...] = jnp.broadcast_to(stats[None], stats_ref.shape)


def last_kernel(
    stats_ref, res_ref, data_ref, model_ref, dir_ref, grad_ref, new_image, new_residual, new_dir
):
    stats = jnp.sum(stats_ref[...], axis=0)
    lane = lax.broadcasted_iota(jnp.int32, stats.shape, 1)

    def pick(n):
        return jnp.sum(jnp.where(lane == n, stats, 0.0), axis=1, keepdims=True)

    gamma, curvature, one_one, one_two, two_two = (pick(n) for n in range(5))
    alpha = gamma / curvature
    gamma_new = one_one - 2.0 * (alpha * one_two) + alpha * (alpha * two_two)
    beta = gamma_new / gamma
    new_residual[...] = res_ref[...] - alpha * data_ref[...]
    step = dir_ref[...]
    new_image[...] = model_ref[...] + alpha[None] * step
    new_dir[...] = (grad_ref[0] - alpha[None] * grad_ref[1]) + beta[None] * step


def shift(cells, axis, by):
    count = lax.axis_size(axis)
    pairs = [(i, i + by) for i in range(count) if 0 <= i + by < count]
    return lax.ppermute(cells, axis, pairs)


def body(
    model_image,
    data_residual,
    direction,
    old_gradient,
    aperture,
    travel_times,
    amplitude,
    trace_counts,
):
    bins_x, bins_y, samples = data_residual.shape
    entries, depths = travel_times.shape[2], travel_times.shape[3]
    highs = samples // LANES
    wide_x, wide_y = bins_x + 2 * RADIUS, bins_y + 2 * RADIUS
    columns = wide_x * wide_y
    span = SIDE * wide_y
    geo = (bins_y, entries, highs, wide_y)
    rows_per = bins_y * highs

    from_prev = shift(direction, "gx", 1)[bins_x - RADIUS :]
    from_next = shift(direction, "gx", -1)[:RADIUS]

    times = travel_times.reshape(bins_x * bins_y, entries, depths)
    res_rows = to_rows(data_residual)
    def first(row0, count, counts, limit):
        return pl.pallas_call(
            functools.partial(first_kernel, geo, row0),
            grid=(count,),
            in_specs=[
                pl.BlockSpec((rows_per, LANES), lambda i: (i + row0, 0)),
                pl.BlockSpec((bins_y, entries, depths), lambda i: (i + row0, 0, 0)),
                pl.BlockSpec((1, bins_y, entries), lambda i: (i + row0, 0, 0)),
                pl.BlockSpec((bins_x, bins_y), lambda i: (0, 0)),
                pl.BlockSpec((1, bins_y, entries), lambda i: (i + row0, 0, 0)),
            ],
            out_specs=pl.BlockSpec((columns, depths), lambda i: (0, 0)),
            out_shape=jax.ShapeDtypeStruct((columns, depths), F32),
            scratch_shapes=[pltpu.VMEM((bins_y * entries, depths), F32)] * 2,
            compiler_params=params(limit),
            cost_estimate=pl.CostEstimate(
                flops=4 * 10**9, bytes_accessed=4 * 10**6, transcendentals=0
            ),
            name="sample_residual",
        )(res_rows, times, amplitude, counts, aperture)

    early = bins_x // 4
    row0 = 2 * early
    s1 = first(0, early, trace_counts, FIRST_LIMIT)
    ext = jnp.concatenate([from_prev, direction, from_next], axis=0)
    tail, head, s1, counts = lax.optimization_barrier(
        (ext[:, bins_y - RADIUS :], ext[:, :RADIUS], s1, trace_counts)
    )
    left = shift(tail, "gy", 1)
    right = shift(head, "gy", -1)
    s1_more = first(early, early, counts, VMEM_LIMIT)

    cut = bins_x // (bins_x - row0)
    res_bins = bins_y // cut
    parts = trace_counts.reshape(bins_x * cut, res_bins)
    strip = jax.ShapeDtypeStruct((2, wide_x, RADIUS, depths), F32)
    vals_shape = pltpu.VMEM((bins_y * entries, depths), F32)
    res_shape = pltpu.VMEM((res_bins * entries, depths), F32)
    columns_shape = pltpu.VMEM((columns, depths), F32)
    in_vmem = pl.BlockSpec(memory_space=pltpu.VMEM)
    data_rows, curv, out_left, out_mid, out_right = pl.pallas_call(
        functools.partial(main_kernel, geo, row0),
        in_specs=[pl.BlockSpec(memory_space=pltpu.SMEM)] + [in_vmem] * 11,
        out_specs=[in_vmem] * 5,
        out_shape=[
            jax.ShapeDtypeStruct((bins_x * rows_per, LANES), F32),
            jax.ShapeDtypeStruct((highs, LANES), F32),
            strip,
            jax.ShapeDtypeStruct((2, wide_x, bins_y, depths), F32),
            strip,
        ],
        scratch_shapes=[columns_shape, columns_shape, columns_shape]
        + [vals_shape, res_shape, vals_shape, vals_shape, res_shape]
        + [pltpu.VMEM((rows_per, LANES), F32)]
        + [pltpu.VMEM((bins_y * entries, 2 * depths), BF16)]
        + [pltpu.VMEM((res_bins * entries, 2 * depths), BF16)]
        + [pltpu.VMEM((4, entries + SUB, LANES), F32)] * 8,
        compiler_params=params(MAIN_LIMIT),
        cost_estimate=pl.CostEstimate(
            flops=20 * 10**9, bytes_accessed=8 * 10**6, transcendentals=0
        ),
        name="demigrate_and_sample",
    )(
        aperture,
        times,
        amplitude,
        trace_counts,
        parts,
        aperture,
        res_rows,
        ext,
        left,
        right,
        s1,
        s1_more,
    )

    from_low = shift(out_right, "gy", 1)
    from_high = shift(out_left, "gy", -1)
    edge = jax.ShapeDtypeStruct((2, RADIUS, bins_y, depths), F32)
    out_head, inner, out_tail = pl.pallas_call(
        fold_y_kernel,
        out_shape=[edge, jax.ShapeDtypeStruct((2, bins_x, bins_y, depths), F32), edge],
        compiler_params=params(SMALL_LIMIT),
        name="fold_y",
    )(out_mid, from_low, from_high)
    from_low = shift(out_tail, "gx", 1)
    from_high = shift(out_head, "gx", -1)
    devices = lax.axis_size("gx") * lax.axis_size("gy")
    grads, stats = pl.pallas_call(
        fold_x_kernel,
        out_shape=[
            jax.ShapeDtypeStruct((2, bins_x, bins_y, depths), F32),
            jax.ShapeDtypeStruct((devices, 1, LANES), F32),
        ],
        compiler_params=params(SMALL_LIMIT),
        name="fold_x",
    )(inner, from_low, from_high, old_gradient, curv)
    stats = lax.all_to_all(stats, ("gx", "gy"), 0, 0, tiled=True)

    steps = 4
    rows_step = bins_x * rows_per // steps
    x_step = bins_x // steps
    cells = pl.BlockSpec((x_step, bins_y, depths), lambda i: (i, 0, 0))
    rows = pl.BlockSpec((rows_step, LANES), lambda i: (i, 0))
    image_shape = jax.ShapeDtypeStruct(direction.shape, F32)
    new_image, new_rows, new_direction = pl.pallas_call(
        last_kernel,
        grid=(steps,),
        in_specs=[
            pl.BlockSpec(stats.shape, lambda i: (0, 0, 0)),
            rows,
            rows,
            cells,
            cells,
            pl.BlockSpec((2, x_step, bins_y, depths), lambda i: (0, i, 0, 0)),
        ],
        out_specs=[cells, rows, cells],
        out_shape=[image_shape, jax.ShapeDtypeStruct(res_rows.shape, F32), image_shape],
        compiler_params=params(SMALL_LIMIT),
        name="update",
    )(stats, res_rows, data_rows, model_image, direction, grads)
    return (new_image, from_rows(new_rows, data_residual.shape), new_direction)


def solution(mesh):
    in_specs = (
        P("gx", "gy", None),
        P("gx", "gy", None),
        P("gx", "gy", None),
        P("gx", "gy", None),
        P("gx", "gy", None),
        P("gx", "gy", None, None),
        P("gx", "gy", None),
        P("gx", "gy"),
    )
    out_specs = (P("gx", "gy", None), P("gx", "gy", None), P("gx", "gy", None))
    return jax.shard_map(body, mesh=mesh, in_specs=in_specs, out_specs=out_specs, check_vma=False)
```

```python
import functools

import jax
import jax.numpy as jnp
from jax import lax
from jax.experimental import pallas as pl
from jax.experimental.pallas import tpu as pltpu
from jax.sharding import PartitionSpec as P

RADIUS = 8
SIDE = 2 * RADIUS + 1
LANES = 128
SUB = 8
F32 = jnp.float32
BF16 = jnp.bfloat16
VMEM_LIMIT = 51 * 1024 * 1024
FIRST_LIMIT = 59 * 1024 * 1024
MAIN_LIMIT = 36 * 1024 * 1024
SMALL_LIMIT = 24 * 1024 * 1024


def params(limit=VMEM_LIMIT):
    return pltpu.CompilerParams(vmem_limit_bytes=limit)


def to_rows(traces):
    bins_x, bins_y, samples = traces.shape
    parts = traces.reshape(bins_x, bins_y // SUB, SUB, samples // LANES, LANES)
    return parts.transpose(0, 1, 3, 2, 4).reshape(-1, LANES)


def from_rows(rows, shape):
    bins_x, bins_y, samples = shape
    parts = rows.reshape(bins_x, bins_y // SUB, samples // LANES, SUB, LANES)
    return parts.transpose(0, 1, 3, 2, 4).reshape(shape)


def trace_row(b, highs):
    return (b // SUB) * (SUB * highs) + b % SUB


def fill_weights(amplitude, counts, scales):
    bins, entries = amplitude.shape
    weight = amplitude.T * counts.astype(F32)
    for b in range(bins):
        column = jnp.broadcast_to(weight[:, b : b + 1], (entries, LANES))
        scales[pl.ds(b * entries, entries), :] = column


def sample_bin(source, first, highs, times_ref, bin_at, b, scales, vals):
    entries = times_ref.shape[1]
    tables = [source[pl.ds(first + SUB * h, SUB, stride=0), :] for h in range(highs)]
    for part in range(0, entries, SUB):
        times = times_ref[bin_at, pl.ds(part, SUB), :]
        high = jnp.right_shift(times, LANES.bit_length() - 1)
        low = jnp.bitwise_and(times, LANES - 1)
        acc = jnp.zeros(times.shape, F32)
        for h in range(highs):
            got = jnp.take_along_axis(tables[h], low, axis=1, mode="promise_in_bounds")
            acc = jnp.where(high == h, got, acc)
        at = b * entries + part
        at = pl.ds(at if isinstance(at, int) else pl.multiple_of(at, SUB), SUB)
        vals[at, :] = acc * scales[at, :]


def column_offset(entry, wide_y):
    return entry + jnp.right_shift(entry * 241, 12) * (wide_y - SIDE)


def place_row(aperture, wide_y, first_bin=0):
    offset = column_offset(aperture, wide_y)
    return jnp.concatenate(
        [offset[b : b + 1, :] + (b + first_bin) for b in range(offset.shape[0])], axis=1
    )


def split_values(vals):
    value = vals[...]
    upper = value.astype(BF16)
    lower = (value - upper.astype(F32)).astype(BF16)
    return jnp.concatenate([upper, lower], axis=1)


def spread_bins(both, place, s_ref, row, wide_y):
    span = SIDE * wide_y
    iota = lax.broadcasted_iota(jnp.int32, (span, place.shape[1]), 0)
    table = jnp.where(iota == place, 1.0, 0.0).astype(BF16)
    part = jnp.dot(table, both, preferred_element_type=F32)
    s_ref[pl.ds(pl.multiple_of(row * wide_y, SUB), span), :] += part[:, :LANES] + part[:, LANES:]


def first_kernel(
    geo, row0, res_ref, times_ref, amp_ref, counts_ref, aper_ref, s_ref, vals, scales
):
    bins_y, entries, highs, wide_y = geo
    step = pl.program_id(0)

    @pl.when(step == 0)
    def _():
        s_ref[...] = jnp.zeros_like(s_ref)

    fill_weights(amp_ref[0], counts_ref[pl.ds(step + row0, 1), :], scales)
    for b in range(bins_y):
        sample_bin(res_ref, trace_row(b, highs), highs, times_ref, b, b, scales, vals)
    both = split_values(vals)
    spread_bins(both, place_row(aper_ref[0], wide_y), s_ref, step + row0, wide_y)


def scatter_bin(geo, row, b, image, entry_ref, times_ref, scales, work, late=None):
    bins_y, entries, highs, wide_y = geo
    half = LANES // 2
    half_bits = half.bit_length() - 1
    iota16 = lax.broadcasted_iota(jnp.int32, (16, LANES), 0)
    iota_lo = [(iota16 + k).astype(F32).astype(BF16) for k in range(0, half, 16)]
    iota_hi = [(iota16 + k).astype(F32).astype(BF16) for k in range(0, 2 * highs, 16)]
    zero = jnp.zeros((), BF16)
    one = jnp.ones((), BF16)
    for e in range(entries):
        column = column_offset(entry_ref[row, b, e], wide_y) + (row * wide_y + b)
        work[0, pl.ds(e, 1), :] = image[pl.ds(column, 1), :]
    value = work[0, pl.ds(0, entries), :]
    value = value * scales[pl.ds(b * entries, entries), :]
    upper = value.astype(BF16).astype(F32)
    times = times_ref[row * bins_y + b]
    middle = jnp.bitwise_and(jnp.right_shift(times, half_bits), 1)
    rows = pl.ds(0, entries)
    work[0, rows, :] = upper
    work[1, rows, :] = value - upper
    work[2, rows, :] = jnp.bitwise_and(times, half - 1).astype(F32)
    work[3, rows, :] = (jnp.right_shift(times, half_bits + 1) + middle * highs).astype(F32)
    lefts = []
    rights = []
    for e in range(entries):

        def wide(k):
            row = work[k, pl.ds(e, SUB, stride=0), :]
            return jnp.concatenate([row, row], axis=0).astype(BF16)

        place = wide(3)
        hits = [place == iota for iota in iota_hi]
        parts = [jnp.where(hit, wide(k), zero) for k in range(2) for hit in hits]
        lefts.append(jnp.concatenate(parts, axis=0))
        low = wide(2)
        rights.append(
            jnp.concatenate([jnp.where(low == iota, one, zero) for iota in iota_lo], axis=0)
        )
    right = jnp.concatenate(rights, axis=1)
    out = lax.dot_general(
        jnp.concatenate(lefts, axis=1),
        right,
        (((1,), (1,)), ((), ())),
        preferred_element_type=F32,
    )
    out = out[: 2 * highs] + out[2 * highs :]
    if late is not None:
        upper = out.astype(BF16)
        lower = (out - upper.astype(F32)).astype(BF16)
        halves = jnp.concatenate([upper, lower], axis=0)
        iota8 = lax.broadcasted_iota(jnp.int32, (SUB, LANES), 0)
        for e in range(0, entries, 2):
            tables = jnp.concatenate(rights[e : e + 2], axis=1)
            picked = jnp.dot(halves, tables, preferred_element_type=F32)
            picked = picked[: 2 * highs] + picked[2 * highs :]
            for u in range(2):
                place = work[3, pl.ds(e + u, SUB, stride=0), :]
                kept = jnp.zeros((SUB, LANES), F32)
                for k in range(0, 2 * highs, SUB):
                    part = picked[k : k + SUB, u * LANES : (u + 1) * LANES]
                    kept = kept + jnp.where(place == (iota8 + k).astype(F32), part, 0.0)
                late[pl.ds(b * entries + e + u, 1), :] = jnp.sum(kept, axis=0, keepdims=True)
    return jnp.concatenate([out[:highs], out[highs:]], axis=1)


def main_kernel(
    geo,
    row0,
    entry_ref,
    times_ref,
    amp_ref,
    counts_ref,
    parts_ref,
    aper_ref,
    res_ref,
    mid_ref,
    left_ref,
    right_ref,
    s1_in_ref,
    s1_more_ref,
    data_ref,
    curv_ref,
    out_left,
    out_mid,
    out_right,
    image,
    s1_ref,
    s2_ref,
    vals,
    res_vals,
    scales,
    old_scales,
    res_scales,
    old_data,
    both,
    res_both,
    late,
    *works,
):
    bins_y, entries, highs, wide_y = geo
    bins_x = amp_ref.shape[0]
    wide_x = mid_ref.shape[0]
    rows_per = bins_y * highs
    cut = bins_x // (bins_x - row0)
    res_bins = bins_y // cut

    s1_ref[...] = s1_in_ref[...] + s1_more_ref[...]
    s2_ref[...] = jnp.zeros_like(s2_ref)
    old_data[...] = jnp.zeros_like(old_data)
    scales[...] = jnp.zeros_like(scales)
    both[...] = jnp.zeros_like(both)
    late[...] = jnp.zeros_like(late)
    res_both[...] = jnp.zeros_like(res_both)
    for x in range(wide_x):
        image[pl.ds(x * wide_y, RADIUS), :] = left_ref[x]
        image[pl.ds(x * wide_y + RADIUS, bins_y), :] = mid_ref[x]
        image[pl.ds(x * wide_y + RADIUS + bins_y, RADIUS), :] = right_ref[x]

    def residual_part(step):
        return row0 + step // cut, (step % cut) * res_bins

    def spread_image(row):
        spread_bins(both[...], place_row(aper_ref[row], wide_y), s2_ref, row, wide_y)

    def spread_residual(step):
        row, part = residual_part(step)
        entry = aper_ref[row, pl.ds(pl.multiple_of(part, SUB), res_bins), :]
        spread_bins(res_both[...], place_row(entry, wide_y, part), s1_ref, row, wide_y)

    def by_tables(b):
        return b % cut == cut - 1

    def take_late(weights):
        for b in range(bins_y):
            if by_tables(b):
                at = pl.ds(b * entries, entries)
                vals[at, :] = late[at, :] * weights[at, :]

    def one_row(step, total):
        before = jnp.maximum(step - 1, 0)
        spread_image(jnp.maximum(step - 2, 0))
        spread_residual(before)
        res_row, res_part = residual_part(step)
        res_first = pl.multiple_of(res_row * rows_per + res_part * highs, SUB)
        old_scales[...] = scales[...]
        take_late(old_scales)
        fill_weights(amp_ref[step], counts_ref[pl.ds(step, 1), :], scales)
        fill_weights(
            amp_ref[res_row, pl.ds(pl.multiple_of(res_part, SUB), res_bins), :],
            parts_ref[pl.ds(row0 * cut + step, 1), :],
            res_scales,
        )
        for b in range(bins_y):
            trace = scatter_bin(
                geo,
                step,
                b,
                image,
                entry_ref,
                times_ref,
                scales,
                works[b % len(works)],
                late if by_tables(b) else None,
            )
            first = trace_row(b, highs)
            data_ref[pl.ds(step * rows_per + first, highs, stride=SUB), :] = trace
            total = total + trace * trace
            if not by_tables(b):
                at = before * bins_y + b
                sample_bin(old_data, first, highs, times_ref, at, b, old_scales, vals)
            else:
                r = b // cut
                first = res_first + trace_row(r, highs)
                at = res_row * bins_y + res_part + r
                sample_bin(res_ref, first, highs, times_ref, at, r, res_scales, res_vals)
        both[...] = split_values(vals)
        res_both[...] = split_values(res_vals)
        old_data[...] = data_ref[pl.ds(pl.multiple_of(step * rows_per, SUB), rows_per), :]
        return total

    curv_ref[...] = lax.fori_loop(0, bins_x, one_row, jnp.zeros((highs, LANES), F32))
    last = bins_x - 1
    spread_image(last - 1)
    spread_residual(last)
    take_late(scales)
    for b in range(bins_y):
        at = last * bins_y + b
        if not by_tables(b):
            sample_bin(old_data, trace_row(b, highs), highs, times_ref, at, b, scales, vals)
    both[...] = split_values(vals)
    spread_image(last)
    for k, ref in enumerate((s1_ref, s2_ref)):
        for x in range(wide_x):
            out_left[k, x] = ref[pl.ds(x * wide_y, RADIUS), :]
            out_mid[k, x] = ref[pl.ds(x * wide_y + RADIUS, bins_y), :]
            out_right[k, x] = ref[pl.ds(x * wide_y + RADIUS + bins_y, RADIUS), :]


def fold_y_kernel(mid_ref, low_ref, high_ref, out_head, out_mid, out_tail):
    wide_x, bins_y = mid_ref.shape[1], mid_ref.shape[2]
    bins_x = wide_x - 2 * RADIUS
    for k in range(2):
        for x in range(wide_x):
            if x < RADIUS:
                ref, at = out_head, x
            elif x < RADIUS + bins_x:
                ref, at = out_mid, x - RADIUS
            else:
                ref, at = out_tail, x - RADIUS - bins_x
            ref[k, at, pl.ds(0, RADIUS), :] = mid_ref[k, x, pl.ds(0, RADIUS), :] + low_ref[k, x]
            high = pl.ds(bins_y - RADIUS, RADIUS)
            ref[k, at, high, :] = mid_ref[k, x, high, :] + high_ref[k, x]


def fold_x_kernel(mid_ref, low_ref, high_ref, grad_ref, curv_ref, out_ref, stats_ref):
    bins_x = mid_ref.shape[1]
    sums = [jnp.zeros((1, LANES), F32) for _ in range(5)]
    for x in range(bins_x):
        pair = []
        for k in range(2):
            cells = mid_ref[k, x]
            if x < RADIUS:
                cells = cells + low_ref[k, x]
            else:
                cells = cells + high_ref[k, x - RADIUS]
            out_ref[k, x] = cells
            pair.append(cells)
        old = grad_ref[x]
        terms = (old * old, None, pair[0] * pair[0], pair[0] * pair[1], pair[1] * pair[1])
        for n, term in enumerate(terms):
            if term is not None:
                sums[n] = sums[n] + jnp.sum(term, axis=0, keepdims=True)
    sums[1] = jnp.sum(curv_ref[...], axis=0, keepdims=True)
    lane = lax.broadcasted_iota(jnp.int32, (1, LANES), 1)
    stats = jnp.zeros((1, LANES), F32)
    for n, term in enumerate(sums):
        stats = jnp.where(lane == n, jnp.sum(term, axis=1, keepdims=True), stats)
    stats_ref[...] = jnp.broadcast_to(stats[None], stats_ref.shape)


def last_kernel(
    stats_ref, res_ref, data_ref, model_ref, dir_ref, grad_ref, new_image, new_residual, new_dir
):
    stats = jnp.sum(stats_ref[...], axis=0)
    lane = lax.broadcasted_iota(jnp.int32, stats.shape, 1)

    def pick(n):
        return jnp.sum(jnp.where(lane == n, stats, 0.0), axis=1, keepdims=True)

    gamma, curvature, one_one, one_two, two_two = (pick(n) for n in range(5))
    alpha = gamma / curvature
    gamma_new = one_one - 2.0 * (alpha * one_two) + alpha * (alpha * two_two)
    beta = gamma_new / gamma
    new_residual[...] = res_ref[...] - alpha * data_ref[...]
    step = dir_ref[...]
    new_image[...] = model_ref[...] + alpha[None] * step
    new_dir[...] = (grad_ref[0] - alpha[None] * grad_ref[1]) + beta[None] * step


def shift(cells, axis, by):
    count = lax.axis_size(axis)
    pairs = [(i, i + by) for i in range(count) if 0 <= i + by < count]
    return lax.ppermute(cells, axis, pairs)


def body(
    model_image,
    data_residual,
    direction,
    old_gradient,
    aperture,
    travel_times,
    amplitude,
    trace_counts,
):
    bins_x, bins_y, samples = data_residual.shape
    entries, depths = travel_times.shape[2], travel_times.shape[3]
    highs = samples // LANES
    wide_x, wide_y = bins_x + 2 * RADIUS, bins_y + 2 * RADIUS
    columns = wide_x * wide_y
    span = SIDE * wide_y
    geo = (bins_y, entries, highs, wide_y)
    rows_per = bins_y * highs

    from_prev = shift(direction, "gx", 1)[bins_x - RADIUS :]
    from_next = shift(direction, "gx", -1)[:RADIUS]

    times = travel_times.reshape(bins_x * bins_y, entries, depths)
    res_rows = to_rows(data_residual)
    def first(row0, count, counts, limit):
        return pl.pallas_call(
            functools.partial(first_kernel, geo, row0),
            grid=(count,),
            in_specs=[
                pl.BlockSpec((rows_per, LANES), lambda i: (i + row0, 0)),
                pl.BlockSpec((bins_y, entries, depths), lambda i: (i + row0, 0, 0)),
                pl.BlockSpec((1, bins_y, entries), lambda i: (i + row0, 0, 0)),
                pl.BlockSpec((bins_x, bins_y), lambda i: (0, 0)),
                pl.BlockSpec((1, bins_y, entries), lambda i: (i + row0, 0, 0)),
            ],
            out_specs=pl.BlockSpec((columns, depths), lambda i: (0, 0)),
            out_shape=jax.ShapeDtypeStruct((columns, depths), F32),
            scratch_shapes=[pltpu.VMEM((bins_y * entries, depths), F32)] * 2,
            compiler_params=params(limit),
            cost_estimate=pl.CostEstimate(
                flops=4 * 10**9, bytes_accessed=4 * 10**6, transcendentals=0
            ),
            name="sample_residual",
        )(res_rows, times, amplitude, counts, aperture)

    early = bins_x // 4
    row0 = 2 * early
    s1 = first(0, early, trace_counts, FIRST_LIMIT)
    ext = jnp.concatenate([from_prev, direction, from_next], axis=0)
    tail, head, s1, counts = lax.optimization_barrier(
        (ext[:, bins_y - RADIUS :], ext[:, :RADIUS], s1, trace_counts)
    )
    left = shift(tail, "gy", 1)
    right = shift(head, "gy", -1)
    s1_more = first(early, early, counts, VMEM_LIMIT)

    cut = bins_x // (bins_x - row0)
    res_bins = bins_y // cut
    parts = trace_counts.reshape(bins_x * cut, res_bins)
    strip = jax.ShapeDtypeStruct((2, wide_x, RADIUS, depths), F32)
    vals_shape = pltpu.VMEM((bins_y * entries, depths), F32)
    res_shape = pltpu.VMEM((res_bins * entries, depths), F32)
    columns_shape = pltpu.VMEM((columns, depths), F32)
    in_vmem = pl.BlockSpec(memory_space=pltpu.VMEM)
    data_rows, curv, out_left, out_mid, out_right = pl.pallas_call(
        functools.partial(main_kernel, geo, row0),
        in_specs=[pl.BlockSpec(memory_space=pltpu.SMEM)] + [in_vmem] * 11,
        out_specs=[in_vmem] * 5,
        out_shape=[
            jax.ShapeDtypeStruct((bins_x * rows_per, LANES), F32),
            jax.ShapeDtypeStruct((highs, LANES), F32),
            strip,
            jax.ShapeDtypeStruct((2, wide_x, bins_y, depths), F32),
            strip,
        ],
        scratch_shapes=[columns_shape, columns_shape, columns_shape]
        + [vals_shape, res_shape, vals_shape, vals_shape, res_shape]
        + [pltpu.VMEM((rows_per, LANES), F32)]
        + [pltpu.VMEM((bins_y * entries, 2 * depths), BF16)]
        + [pltpu.VMEM((res_bins * entries, 2 * depths), BF16)]
        + [vals_shape]
        + [pltpu.VMEM((4, entries + SUB, LANES), F32)] * 8,
        compiler_params=params(MAIN_LIMIT),
        cost_estimate=pl.CostEstimate(
            flops=20 * 10**9, bytes_accessed=8 * 10**6, transcendentals=0
        ),
        name="demigrate_and_sample",
    )(
        aperture,
        times,
        amplitude,
        trace_counts,
        parts,
        aperture,
        res_rows,
        ext,
        left,
        right,
        s1,
        s1_more,
    )

    from_low = shift(out_right, "gy", 1)
    from_high = shift(out_left, "gy", -1)
    edge = jax.ShapeDtypeStruct((2, RADIUS, bins_y, depths), F32)
    out_head, inner, out_tail = pl.pallas_call(
        fold_y_kernel,
        out_shape=[edge, jax.ShapeDtypeStruct((2, bins_x, bins_y, depths), F32), edge],
        compiler_params=params(SMALL_LIMIT),
        name="fold_y",
    )(out_mid, from_low, from_high)
    from_low = shift(out_tail, "gx", 1)
    from_high = shift(out_head, "gx", -1)
    devices = lax.axis_size("gx") * lax.axis_size("gy")
    grads, stats = pl.pallas_call(
        fold_x_kernel,
        out_shape=[
            jax.ShapeDtypeStruct((2, bins_x, bins_y, depths), F32),
            jax.ShapeDtypeStruct((devices, 1, LANES), F32),
        ],
        compiler_params=params(SMALL_LIMIT),
        name="fold_x",
    )(inner, from_low, from_high, old_gradient, curv)
    stats = lax.all_to_all(stats, ("gx", "gy"), 0, 0, tiled=True)

    steps = 4
    rows_step = bins_x * rows_per // steps
    x_step = bins_x // steps
    cells = pl.BlockSpec((x_step, bins_y, depths), lambda i: (i, 0, 0))
    rows = pl.BlockSpec((rows_step, LANES), lambda i: (i, 0))
    image_shape = jax.ShapeDtypeStruct(direction.shape, F32)
    new_image, new_rows, new_direction = pl.pallas_call(
        last_kernel,
        grid=(steps,),
        in_specs=[
            pl.BlockSpec(stats.shape, lambda i: (0, 0, 0)),
            rows,
            rows,
            cells,
            cells,
            pl.BlockSpec((2, x_step, bins_y, depths), lambda i: (0, i, 0, 0)),
        ],
        out_specs=[cells, rows, cells],
        out_shape=[image_shape, jax.ShapeDtypeStruct(res_rows.shape, F32), image_shape],
        compiler_params=params(SMALL_LIMIT),
        name="update",
    )(stats, res_rows, data_rows, model_image, direction, grads)
    return (new_image, from_rows(new_rows, data_residual.shape), new_direction)


def solution(mesh):
    in_specs = (
        P("gx", "gy", None),
        P("gx", "gy", None),
        P("gx", "gy", None),
        P("gx", "gy", None),
        P("gx", "gy", None),
        P("gx", "gy", None, None),
        P("gx", "gy", None),
        P("gx", "gy"),
    )
    out_specs = (P("gx", "gy", None), P("gx", "gy", None), P("gx", "gy", None))
    return jax.shard_map(body, mesh=mesh, in_specs=in_specs, out_specs=out_specs, check_vma=False)
```

```python
import functools

import jax
import jax.numpy as jnp
from jax import lax
from jax.experimental import pallas as pl
from jax.experimental.pallas import tpu as pltpu
from jax.sharding import PartitionSpec as P

RADIUS = 8
SIDE = 2 * RADIUS + 1
LANES = 128
SUB = 8
F32 = jnp.float32
BF16 = jnp.bfloat16
VMEM_LIMIT = 51 * 1024 * 1024
FIRST_LIMIT = 59 * 1024 * 1024
MAIN_LIMIT = 36 * 1024 * 1024
SMALL_LIMIT = 24 * 1024 * 1024


def params(limit=VMEM_LIMIT):
    return pltpu.CompilerParams(vmem_limit_bytes=limit)


def to_rows(traces):
    bins_x, bins_y, samples = traces.shape
    parts = traces.reshape(bins_x, bins_y // SUB, SUB, samples // LANES, LANES)
    return parts.transpose(0, 1, 3, 2, 4).reshape(-1, LANES)


def from_rows(rows, shape):
    bins_x, bins_y, samples = shape
    parts = rows.reshape(bins_x, bins_y // SUB, samples // LANES, SUB, LANES)
    return parts.transpose(0, 1, 3, 2, 4).reshape(shape)


def trace_row(b, highs):
    return (b // SUB) * (SUB * highs) + b % SUB


def fill_weights(amplitude, counts, scales):
    bins, entries = amplitude.shape
    weight = amplitude.T * counts.astype(F32)
    for b in range(bins):
        column = jnp.broadcast_to(weight[:, b : b + 1], (entries, LANES))
        scales[pl.ds(b * entries, entries), :] = column


def sample_bin(source, first, highs, times_ref, bin_at, b, scales, vals):
    entries = times_ref.shape[1]
    tables = [source[pl.ds(first + SUB * h, SUB, stride=0), :] for h in range(highs)]
    for part in range(0, entries, SUB):
        times = times_ref[bin_at, pl.ds(part, SUB), :]
        high = jnp.right_shift(times, LANES.bit_length() - 1)
        low = jnp.bitwise_and(times, LANES - 1)
        acc = jnp.zeros(times.shape, F32)
        for h in range(highs):
            got = jnp.take_along_axis(tables[h], low, axis=1, mode="promise_in_bounds")
            acc = jnp.where(high == h, got, acc)
        at = b * entries + part
        at = pl.ds(at if isinstance(at, int) else pl.multiple_of(at, SUB), SUB)
        vals[at, :] = acc * scales[at, :]


def column_offset(entry, wide_y):
    return entry + jnp.right_shift(entry * 241, 12) * (wide_y - SIDE)


def place_row(aperture, wide_y, first_bin=0):
    offset = column_offset(aperture, wide_y)
    return jnp.concatenate(
        [offset[b : b + 1, :] + (b + first_bin) for b in range(offset.shape[0])], axis=1
    )


def split_values(vals):
    value = vals[...]
    upper = value.astype(BF16)
    lower = (value - upper.astype(F32)).astype(BF16)
    return jnp.concatenate([upper, lower], axis=1)


def spread_bins(both, place, s_ref, row, wide_y):
    span = SIDE * wide_y
    iota = lax.broadcasted_iota(jnp.int32, (span, place.shape[1]), 0)
    table = jnp.where(iota == place, 1.0, 0.0).astype(BF16)
    part = jnp.dot(table, both, preferred_element_type=F32)
    s_ref[pl.ds(pl.multiple_of(row * wide_y, SUB), span), :] += part[:, :LANES] + part[:, LANES:]


def first_kernel(
    geo, row0, res_ref, times_ref, amp_ref, counts_ref, aper_ref, s_ref, vals, scales
):
    bins_y, entries, highs, wide_y = geo
    step = pl.program_id(0)

    @pl.when(step == 0)
    def _():
        s_ref[...] = jnp.zeros_like(s_ref)

    fill_weights(amp_ref[0], counts_ref[pl.ds(step + row0, 1), :], scales)
    for b in range(bins_y):
        sample_bin(res_ref, trace_row(b, highs), highs, times_ref, b, b, scales, vals)
    both = split_values(vals)
    spread_bins(both, place_row(aper_ref[0], wide_y), s_ref, step + row0, wide_y)


def scatter_bin(geo, row, b, image, entry_ref, times_ref, scales, work):
    bins_y, entries, highs, wide_y = geo
    half = LANES // 2
    half_bits = half.bit_length() - 1
    iota16 = lax.broadcasted_iota(jnp.int32, (16, LANES), 0)
    iota_lo = [(iota16 + k).astype(F32).astype(BF16) for k in range(0, half, 16)]
    iota_hi = [(iota16 + k).astype(F32).astype(BF16) for k in range(0, 2 * highs, 16)]
    zero = jnp.zeros((), BF16)
    one = jnp.ones((), BF16)
    for e in range(entries):
        column = column_offset(entry_ref[row, b, e], wide_y) + (row * wide_y + b)
        work[0, pl.ds(e, 1), :] = image[pl.ds(column, 1), :]
    value = work[0, pl.ds(0, entries), :]
    value = value * scales[pl.ds(b * entries, entries), :]
    upper = value.astype(BF16).astype(F32)
    times = times_ref[row * bins_y + b]
    middle = jnp.bitwise_and(jnp.right_shift(times, half_bits), 1)
    rows = pl.ds(0, entries)
    work[0, rows, :] = upper
    work[1, rows, :] = value - upper
    work[2, rows, :] = jnp.bitwise_and(times, half - 1).astype(F32)
    work[3, rows, :] = (jnp.right_shift(times, half_bits + 1) + middle * highs).astype(F32)
    lefts = []
    rights = []
    for e in range(entries):

        def wide(k):
            row = work[k, pl.ds(e, SUB, stride=0), :]
            return jnp.concatenate([row, row], axis=0).astype(BF16)

        place = wide(3)
        hits = [place == iota for iota in iota_hi]
        parts = [jnp.where(hit, wide(k), zero) for k in range(2) for hit in hits]
        lefts.append(jnp.concatenate(parts, axis=0))
        low = wide(2)
        rights.append(
            jnp.concatenate([jnp.where(low == iota, one, zero) for iota in iota_lo], axis=0)
        )
    out = lax.dot_general(
        jnp.concatenate(lefts, axis=1),
        jnp.concatenate(rights, axis=1),
        (((1,), (1,)), ((), ())),
        preferred_element_type=F32,
    )
    out = out[: 2 * highs] + out[2 * highs :]
    return jnp.concatenate([out[:highs], out[highs:]], axis=1)


def main_kernel(
    geo,
    row0,
    entry_ref,
    times_ref,
    amp_ref,
    counts_ref,
    parts_ref,
    aper_ref,
    res_ref,
    mid_ref,
    left_ref,
    right_ref,
    s1_in_ref,
    s1_more_ref,
    data_ref,
    curv_ref,
    out_left,
    out_mid,
    out_right,
    image,
    s1_ref,
    s2_ref,
    vals,
    res_vals,
    scales,
    old_scales,
    res_scales,
    old_data,
    both,
    res_both,
    *works,
):
    bins_y, entries, highs, wide_y = geo
    bins_x = amp_ref.shape[0]
    wide_x = mid_ref.shape[0]
    rows_per = bins_y * highs
    cut = bins_x // (bins_x - row0)
    res_bins = bins_y // cut

    s1_ref[...] = s1_in_ref[...] + s1_more_ref[...]
    s2_ref[...] = jnp.zeros_like(s2_ref)
    old_data[...] = jnp.zeros_like(old_data)
    scales[...] = jnp.zeros_like(scales)
    both[...] = jnp.zeros_like(both)
    res_both[...] = jnp.zeros_like(res_both)
    for x in range(wide_x):
        image[pl.ds(x * wide_y, RADIUS), :] = left_ref[x]
        image[pl.ds(x * wide_y + RADIUS, bins_y), :] = mid_ref[x]
        image[pl.ds(x * wide_y + RADIUS + bins_y, RADIUS), :] = right_ref[x]

    def residual_part(step):
        return row0 + step // cut, (step % cut) * res_bins

    def spread_image(row):
        spread_bins(both[...], place_row(aper_ref[row], wide_y), s2_ref, row, wide_y)

    def spread_residual(step):
        row, part = residual_part(step)
        entry = aper_ref[row, pl.ds(pl.multiple_of(part, SUB), res_bins), :]
        spread_bins(res_both[...], place_row(entry, wide_y, part), s1_ref, row, wide_y)

    def one_row(step, total):
        before = jnp.maximum(step - 1, 0)
        spread_image(jnp.maximum(step - 2, 0))
        spread_residual(before)
        res_row, res_part = residual_part(step)
        res_first = pl.multiple_of(res_row * rows_per + res_part * highs, SUB)
        old_scales[...] = scales[...]
        fill_weights(amp_ref[step], counts_ref[pl.ds(step, 1), :], scales)
        fill_weights(
            amp_ref[res_row, pl.ds(pl.multiple_of(res_part, SUB), res_bins), :],
            parts_ref[pl.ds(row0 * cut + step, 1), :],
            res_scales,
        )
        for b in range(bins_y):
            trace = scatter_bin(
                geo, step, b, image, entry_ref, times_ref, scales, works[b % len(works)]
            )
            first = trace_row(b, highs)
            data_ref[pl.ds(step * rows_per + first, highs, stride=SUB), :] = trace
            total = total + trace * trace
            sample_bin(
                old_data, first, highs, times_ref, before * bins_y + b, b, old_scales, vals
            )
            if b % cut == 0:
                r = b // cut
                first = res_first + trace_row(r, highs)
                at = res_row * bins_y + res_part + r
                sample_bin(res_ref, first, highs, times_ref, at, r, res_scales, res_vals)
        both[...] = split_values(vals)
        res_both[...] = split_values(res_vals)
        old_data[...] = data_ref[pl.ds(pl.multiple_of(step * rows_per, SUB), rows_per), :]
        return total

    curv_ref[...] = lax.fori_loop(0, bins_x, one_row, jnp.zeros((highs, LANES), F32))
    last = bins_x - 1
    spread_image(last - 1)
    spread_residual(last)
    for b in range(bins_y):
        at = last * bins_y + b
        sample_bin(old_data, trace_row(b, highs), highs, times_ref, at, b, scales, vals)
    both[...] = split_values(vals)
    spread_image(last)
    for k, ref in enumerate((s1_ref, s2_ref)):
        for x in range(wide_x):
            out_left[k, x] = ref[pl.ds(x * wide_y, RADIUS), :]
            out_mid[k, x] = ref[pl.ds(x * wide_y + RADIUS, bins_y), :]
            out_right[k, x] = ref[pl.ds(x * wide_y + RADIUS + bins_y, RADIUS), :]


def fold_y_kernel(mid_ref, low_ref, high_ref, out_head, out_mid, out_tail):
    wide_x, bins_y = mid_ref.shape[1], mid_ref.shape[2]
    bins_x = wide_x - 2 * RADIUS
    for k in range(2):
        for x in range(wide_x):
            if x < RADIUS:
                ref, at = out_head, x
            elif x < RADIUS + bins_x:
                ref, at = out_mid, x - RADIUS
            else:
                ref, at = out_tail, x - RADIUS - bins_x
            ref[k, at, pl.ds(0, RADIUS), :] = mid_ref[k, x, pl.ds(0, RADIUS), :] + low_ref[k, x]
            high = pl.ds(bins_y - RADIUS, RADIUS)
            ref[k, at, high, :] = mid_ref[k, x, high, :] + high_ref[k, x]


def fold_x_kernel(mid_ref, low_ref, high_ref, grad_ref, curv_ref, out_ref, stats_ref):
    bins_x = mid_ref.shape[1]
    sums = [jnp.zeros((1, LANES), F32) for _ in range(5)]
    for x in range(bins_x):
        pair = []
        for k in range(2):
            cells = mid_ref[k, x]
            if x < RADIUS:
                cells = cells + low_ref[k, x]
            else:
                cells = cells + high_ref[k, x - RADIUS]
            out_ref[k, x] = cells
            pair.append(cells)
        old = grad_ref[x]
        terms = (old * old, None, pair[0] * pair[0], pair[0] * pair[1], pair[1] * pair[1])
        for n, term in enumerate(terms):
            if term is not None:
                sums[n] = sums[n] + jnp.sum(term, axis=0, keepdims=True)
    sums[1] = jnp.sum(curv_ref[...], axis=0, keepdims=True)
    lane = lax.broadcasted_iota(jnp.int32, (1, LANES), 1)
    stats = jnp.zeros((1, LANES), F32)
    for n, term in enumerate(sums):
        stats = jnp.where(lane == n, jnp.sum(term, axis=1, keepdims=True), stats)
    stats_ref[...] = jnp.broadcast_to(stats[None], stats_ref.shape)


def last_kernel(
    stats_ref, res_ref, data_ref, model_ref, dir_ref, grad_ref, new_image, new_residual, new_dir
):
    stats = jnp.sum(stats_ref[...], axis=0)
    lane = lax.broadcasted_iota(jnp.int32, stats.shape, 1)

    def pick(n):
        return jnp.sum(jnp.where(lane == n, stats, 0.0), axis=1, keepdims=True)

    gamma, curvature, one_one, one_two, two_two = (pick(n) for n in range(5))
    alpha = gamma / curvature
    gamma_new = one_one - 2.0 * (alpha * one_two) + alpha * (alpha * two_two)
    beta = gamma_new / gamma
    new_residual[...] = res_ref[...] - alpha * data_ref[...]
    step = dir_ref[...]
    new_image[...] = model_ref[...] + alpha[None] * step
    new_dir[...] = (grad_ref[0] - alpha[None] * grad_ref[1]) + beta[None] * step


def shift(cells, axis, by):
    count = lax.axis_size(axis)
    pairs = [(i, i + by) for i in range(count) if 0 <= i + by < count]
    return lax.ppermute(cells, axis, pairs)


def body(
    model_image,
    data_residual,
    direction,
    old_gradient,
    aperture,
    travel_times,
    amplitude,
    trace_counts,
):
    bins_x, bins_y, samples = data_residual.shape
    entries, depths = travel_times.shape[2], travel_times.shape[3]
    highs = samples // LANES
    wide_x, wide_y = bins_x + 2 * RADIUS, bins_y + 2 * RADIUS
    columns = wide_x * wide_y
    span = SIDE * wide_y
    geo = (bins_y, entries, highs, wide_y)
    rows_per = bins_y * highs

    from_prev = shift(direction, "gx", 1)[bins_x - RADIUS :]
    from_next = shift(direction, "gx", -1)[:RADIUS]

    times = travel_times.reshape(bins_x * bins_y, entries, depths)
    res_rows = to_rows(data_residual)
    def first(row0, count, counts, limit):
        return pl.pallas_call(
            functools.partial(first_kernel, geo, row0),
            grid=(count,),
            in_specs=[
                pl.BlockSpec((rows_per, LANES), lambda i: (i + row0, 0)),
                pl.BlockSpec((bins_y, entries, depths), lambda i: (i + row0, 0, 0)),
                pl.BlockSpec((1, bins_y, entries), lambda i: (i + row0, 0, 0)),
                pl.BlockSpec((bins_x, bins_y), lambda i: (0, 0)),
                pl.BlockSpec((1, bins_y, entries), lambda i: (i + row0, 0, 0)),
            ],
            out_specs=pl.BlockSpec((columns, depths), lambda i: (0, 0)),
            out_shape=jax.ShapeDtypeStruct((columns, depths), F32),
            scratch_shapes=[pltpu.VMEM((bins_y * entries, depths), F32)] * 2,
            compiler_params=params(limit),
            cost_estimate=pl.CostEstimate(
                flops=4 * 10**9, bytes_accessed=4 * 10**6, transcendentals=0
            ),
            name="sample_residual",
        )(res_rows, times, amplitude, counts, aperture)

    early = bins_x // 4
    row0 = 2 * early
    s1 = first(0, early, trace_counts, FIRST_LIMIT)
    ext = jnp.concatenate([from_prev, direction, from_next], axis=0)
    tail, head, s1, counts = lax.optimization_barrier(
        (ext[:, bins_y - RADIUS :], ext[:, :RADIUS], s1, trace_counts)
    )
    left = shift(tail, "gy", 1)
    right = shift(head, "gy", -1)
    s1_more = first(early, early, counts, VMEM_LIMIT)

    cut = bins_x // (bins_x - row0)
    res_bins = bins_y // cut
    parts = trace_counts.reshape(bins_x * cut, res_bins)
    strip = jax.ShapeDtypeStruct((2, wide_x, RADIUS, depths), F32)
    vals_shape = pltpu.VMEM((bins_y * entries, depths), F32)
    res_shape = pltpu.VMEM((res_bins * entries, depths), F32)
    columns_shape = pltpu.VMEM((columns, depths), F32)
    in_vmem = pl.BlockSpec(memory_space=pltpu.VMEM)
    data_rows, curv, out_left, out_mid, out_right = pl.pallas_call(
        functools.partial(main_kernel, geo, row0),
        in_specs=[pl.BlockSpec(memory_space=pltpu.SMEM)] + [in_vmem] * 11,
        out_specs=[in_vmem] * 5,
        out_shape=[
            jax.ShapeDtypeStruct((bins_x * rows_per, LANES), F32),
            jax.ShapeDtypeStruct((highs, LANES), F32),
            strip,
            jax.ShapeDtypeStruct((2, wide_x, bins_y, depths), F32),
            strip,
        ],
        scratch_shapes=[columns_shape, columns_shape, columns_shape]
        + [vals_shape, res_shape, vals_shape, vals_shape, res_shape]
        + [pltpu.VMEM((rows_per, LANES), F32)]
        + [pltpu.VMEM((bins_y * entries, 2 * depths), BF16)]
        + [pltpu.VMEM((res_bins * entries, 2 * depths), BF16)]
        + [pltpu.VMEM((4, entries + SUB, LANES), F32)] * 8,
        compiler_params=params(MAIN_LIMIT),
        cost_estimate=pl.CostEstimate(
            flops=20 * 10**9, bytes_accessed=8 * 10**6, transcendentals=0
        ),
        name="demigrate_and_sample",
    )(
        aperture,
        times,
        amplitude,
        trace_counts,
        parts,
        aperture,
        res_rows,
        ext,
        left,
        right,
        s1,
        s1_more,
    )

    from_low = shift(out_right, "gy", 1)
    from_high = shift(out_left, "gy", -1)
    edge = jax.ShapeDtypeStruct((2, RADIUS, bins_y, depths), F32)
    out_head, inner, out_tail = pl.pallas_call(
        fold_y_kernel,
        out_shape=[edge, jax.ShapeDtypeStruct((2, bins_x, bins_y, depths), F32), edge],
        compiler_params=params(SMALL_LIMIT),
        name="fold_y",
    )(out_mid, from_low, from_high)
    from_low = shift(out_tail, "gx", 1)
    from_high = shift(out_head, "gx", -1)
    devices_x, devices_y = lax.axis_size("gx"), lax.axis_size("gy")
    grads, stats = pl.pallas_call(
        fold_x_kernel,
        out_shape=[
            jax.ShapeDtypeStruct((2, bins_x, bins_y, depths), F32),
            jax.ShapeDtypeStruct((devices_y, 1, LANES), F32),
        ],
        compiler_params=params(SMALL_LIMIT),
        name="fold_x",
    )(inner, from_low, from_high, old_gradient, curv)
    stats = lax.all_to_all(stats, "gy", 0, 0, tiled=True)
    stats = jnp.broadcast_to(jnp.sum(stats, axis=0, keepdims=True), (devices_x, 1, LANES))
    stats = lax.all_to_all(stats, "gx", 0, 0, tiled=True)

    steps = 4
    rows_step = bins_x * rows_per // steps
    x_step = bins_x // steps
    cells = pl.BlockSpec((x_step, bins_y, depths), lambda i: (i, 0, 0))
    rows = pl.BlockSpec((rows_step, LANES), lambda i: (i, 0))
    image_shape = jax.ShapeDtypeStruct(direction.shape, F32)
    new_image, new_rows, new_direction = pl.pallas_call(
        last_kernel,
        grid=(steps,),
        in_specs=[
            pl.BlockSpec(stats.shape, lambda i: (0, 0, 0)),
            rows,
            rows,
            cells,
            cells,
            pl.BlockSpec((2, x_step, bins_y, depths), lambda i: (0, i, 0, 0)),
        ],
        out_specs=[cells, rows, cells],
        out_shape=[image_shape, jax.ShapeDtypeStruct(res_rows.shape, F32), image_shape],
        compiler_params=params(SMALL_LIMIT),
        name="update",
    )(stats, res_rows, data_rows, model_image, direction, grads)
    return (new_image, from_rows(new_rows, data_residual.shape), new_direction)


def solution(mesh):
    in_specs = (
        P("gx", "gy", None),
        P("gx", "gy", None),
        P("gx", "gy", None),
        P("gx", "gy", None),
        P("gx", "gy", None),
        P("gx", "gy", None, None),
        P("gx", "gy", None),
        P("gx", "gy"),
    )
    out_specs = (P("gx", "gy", None), P("gx", "gy", None), P("gx", "gy", None))
    return jax.shard_map(body, mesh=mesh, in_specs=in_specs, out_specs=out_specs, check_vma=False)
```

```python
import functools

import jax
import jax.numpy as jnp
from jax import lax
from jax.experimental import pallas as pl
from jax.experimental.pallas import tpu as pltpu
from jax.sharding import PartitionSpec as P

RADIUS = 8
SIDE = 2 * RADIUS + 1
LANES = 128
SUB = 8
F32 = jnp.float32
BF16 = jnp.bfloat16
VMEM_LIMIT = 51 * 1024 * 1024
FIRST_LIMIT = 59 * 1024 * 1024
MAIN_LIMIT = 36 * 1024 * 1024
SMALL_LIMIT = 24 * 1024 * 1024


def params(limit=VMEM_LIMIT):
    return pltpu.CompilerParams(vmem_limit_bytes=limit)


def to_rows(traces):
    bins_x, bins_y, samples = traces.shape
    parts = traces.reshape(bins_x, bins_y // SUB, SUB, samples // LANES, LANES)
    return parts.transpose(0, 1, 3, 2, 4).reshape(-1, LANES)


def from_rows(rows, shape):
    bins_x, bins_y, samples = shape
    parts = rows.reshape(bins_x, bins_y // SUB, samples // LANES, SUB, LANES)
    return parts.transpose(0, 1, 3, 2, 4).reshape(shape)


def trace_row(b, highs):
    return (b // SUB) * (SUB * highs) + b % SUB


def fill_weights(amplitude, counts, scales):
    bins, entries = amplitude.shape
    weight = amplitude.T * counts.astype(F32)
    for b in range(bins):
        column = jnp.broadcast_to(weight[:, b : b + 1], (entries, LANES))
        scales[pl.ds(b * entries, entries), :] = column


def sample_bin(source, first, highs, times_ref, bin_at, b, scales, vals):
    entries = times_ref.shape[1]
    tables = [source[pl.ds(first + SUB * h, SUB, stride=0), :] for h in range(highs)]
    for part in range(0, entries, SUB):
        times = times_ref[bin_at, pl.ds(part, SUB), :]
        high = jnp.right_shift(times, LANES.bit_length() - 1)
        low = jnp.bitwise_and(times, LANES - 1)
        acc = jnp.zeros(times.shape, F32)
        for h in range(highs):
            got = jnp.take_along_axis(tables[h], low, axis=1, mode="promise_in_bounds")
            acc = jnp.where(high == h, got, acc)
        at = b * entries + part
        at = pl.ds(at if isinstance(at, int) else pl.multiple_of(at, SUB), SUB)
        vals[at, :] = acc * scales[at, :]


def column_offset(entry, wide_y):
    return entry + jnp.right_shift(entry * 241, 12) * (wide_y - SIDE)


def place_row(aperture, wide_y, first_bin=0):
    offset = column_offset(aperture, wide_y)
    return jnp.concatenate(
        [offset[b : b + 1, :] + (b + first_bin) for b in range(offset.shape[0])], axis=1
    )


def split_values(vals):
    value = vals[...]
    upper = value.astype(BF16)
    lower = (value - upper.astype(F32)).astype(BF16)
    return jnp.concatenate([upper, lower], axis=1)


def spread_bins(both, place, s_ref, row, wide_y):
    span = SIDE * wide_y
    iota = lax.broadcasted_iota(jnp.int32, (span, place.shape[1]), 0)
    table = jnp.where(iota == place, 1.0, 0.0).astype(BF16)
    part = jnp.dot(table, both, preferred_element_type=F32)
    s_ref[pl.ds(pl.multiple_of(row * wide_y, SUB), span), :] += part[:, :LANES] + part[:, LANES:]


def first_kernel(
    geo, row0, res_ref, times_ref, amp_ref, counts_ref, aper_ref, s_ref, vals, scales, traces
):
    bins_y, entries, highs, wide_y = geo
    step = pl.program_id(0)

    @pl.when(step == 0)
    def _():
        s_ref[...] = jnp.zeros_like(s_ref)

    traces[pl.ds(0, bins_y * highs), :] = res_ref[...]
    fill_weights(amp_ref[0], counts_ref[pl.ds(step + row0, 1), :], scales)
    for b in range(bins_y):
        sample_bin(traces, trace_row(b, highs), highs, times_ref, b, b, scales, vals)
    both = split_values(vals)
    spread_bins(both, place_row(aper_ref[0], wide_y), s_ref, step + row0, wide_y)


def scatter_bin(geo, row, b, image, entry_ref, times_ref, scales, work):
    bins_y, entries, highs, wide_y = geo
    half = LANES // 2
    half_bits = half.bit_length() - 1
    iota16 = lax.broadcasted_iota(jnp.int32, (16, LANES), 0)
    iota_lo = [(iota16 + k).astype(F32).astype(BF16) for k in range(0, half, 16)]
    iota_hi = [(iota16 + k).astype(F32).astype(BF16) for k in range(0, 2 * highs, 16)]
    zero = jnp.zeros((), BF16)
    one = jnp.ones((), BF16)
    for e in range(entries):
        column = column_offset(entry_ref[row, b, e], wide_y) + (row * wide_y + b)
        work[0, pl.ds(e, 1), :] = image[pl.ds(column, 1), :]
    value = work[0, pl.ds(0, entries), :]
    value = value * scales[pl.ds(b * entries, entries), :]
    upper = value.astype(BF16).astype(F32)
    times = times_ref[row * bins_y + b]
    middle = jnp.bitwise_and(jnp.right_shift(times, half_bits), 1)
    rows = pl.ds(0, entries)
    work[0, rows, :] = upper
    work[1, rows, :] = value - upper
    work[2, rows, :] = jnp.bitwise_and(times, half - 1).astype(F32)
    work[3, rows, :] = (jnp.right_shift(times, half_bits + 1) + middle * highs).astype(F32)
    lefts = []
    rights = []
    for e in range(entries):

        def wide(k):
            row = work[k, pl.ds(e, SUB, stride=0), :]
            return jnp.concatenate([row, row], axis=0).astype(BF16)

        place = wide(3)
        hits = [place == iota for iota in iota_hi]
        parts = [jnp.where(hit, wide(k), zero) for k in range(2) for hit in hits]
        lefts.append(jnp.concatenate(parts, axis=0))
        low = wide(2)
        rights.append(
            jnp.concatenate([jnp.where(low == iota, one, zero) for iota in iota_lo], axis=0)
        )
    out = lax.dot_general(
        jnp.concatenate(lefts, axis=1),
        jnp.concatenate(rights, axis=1),
        (((1,), (1,)), ((), ())),
        preferred_element_type=F32,
    )
    out = out[: 2 * highs] + out[2 * highs :]
    return jnp.concatenate([out[:highs], out[highs:]], axis=1)


def main_kernel(
    geo,
    row0,
    entry_ref,
    times_ref,
    amp_ref,
    counts_ref,
    parts_ref,
    aper_ref,
    res_ref,
    mid_ref,
    left_ref,
    right_ref,
    s1_in_ref,
    s1_more_ref,
    data_ref,
    curv_ref,
    out_left,
    out_mid,
    out_right,
    image,
    s_ref,
    vals,
    res_vals,
    scales,
    old_scales,
    res_scales,
    old_data,
    both,
    res_both,
    traces,
    *works,
):
    bins_y, entries, highs, wide_y = geo
    bins_x = amp_ref.shape[0]
    wide_x = mid_ref.shape[0]
    rows_per = bins_y * highs
    cut = bins_x // (bins_x - row0)
    res_bins = bins_y // cut

    columns = wide_x * wide_y
    current = pl.ds(0, rows_per)
    s_ref[pl.ds(0, columns), :] = s1_in_ref[...] + s1_more_ref[...]
    s_ref[pl.ds(columns, columns), :] = jnp.zeros((columns, LANES), F32)
    odd_row = row0 - 1
    old_data[current, :] = res_ref[pl.ds(odd_row * rows_per, rows_per), :]
    fill_weights(amp_ref[odd_row], counts_ref[pl.ds(odd_row, 1), :], scales)
    both[...] = jnp.zeros_like(both)
    res_both[...] = jnp.zeros_like(res_both)
    for x in range(wide_x):
        image[pl.ds(x * wide_y, RADIUS), :] = left_ref[x]
        image[pl.ds(x * wide_y + RADIUS, bins_y), :] = mid_ref[x]
        image[pl.ds(x * wide_y + RADIUS + bins_y, RADIUS), :] = right_ref[x]

    def residual_part(step):
        return row0 + step // cut, (step % cut) * res_bins

    def spread_image(step):
        row = jnp.where(step < 1, odd_row, step - 1)
        at = jnp.where(step < 1, odd_row, step - 1 + wide_x)
        spread_bins(both[...], place_row(aper_ref[row], wide_y), s_ref, at, wide_y)

    def spread_residual(step):
        row, part = residual_part(step)
        entry = aper_ref[row, pl.ds(pl.multiple_of(part, SUB), res_bins), :]
        spread_bins(res_both[...], place_row(entry, wide_y, part), s_ref, row, wide_y)

    def one_row(step, total):
        before = jnp.where(step < 1, odd_row, step - 1)
        spread_image(step - 1)
        spread_residual(jnp.maximum(step - 1, 0))
        res_row, res_part = residual_part(step)
        res_first = pl.multiple_of(res_row * rows_per + res_part * highs, SUB)
        old_scales[...] = scales[...]
        part = res_bins * highs
        traces[pl.ds(0, part), :] = res_ref[pl.ds(res_first, part), :]
        fill_weights(amp_ref[step], counts_ref[pl.ds(step, 1), :], scales)
        fill_weights(
            amp_ref[res_row, pl.ds(pl.multiple_of(res_part, SUB), res_bins), :],
            parts_ref[pl.ds(row0 * cut + step, 1), :],
            res_scales,
        )
        for b in range(bins_y):
            trace = scatter_bin(
                geo, step, b, image, entry_ref, times_ref, scales, works[b % len(works)]
            )
            first = trace_row(b, highs)
            data_ref[pl.ds(step * rows_per + first, highs, stride=SUB), :] = trace
            total = total + trace * trace
            sample_bin(
                old_data, first, highs, times_ref, before * bins_y + b, b, old_scales, vals
            )
            if b % cut == 0:
                r = b // cut
                first = trace_row(r, highs)
                at = res_row * bins_y + res_part + r
                sample_bin(traces, first, highs, times_ref, at, r, res_scales, res_vals)
        both[...] = split_values(vals)
        res_both[...] = split_values(res_vals)
        old_data[current, :] = data_ref[pl.ds(pl.multiple_of(step * rows_per, SUB), rows_per), :]
        return total

    curv_ref[...] = lax.fori_loop(0, bins_x, one_row, jnp.zeros((highs, LANES), F32))
    last = bins_x - 1
    spread_image(last)
    spread_residual(last)
    for b in range(bins_y):
        at = last * bins_y + b
        sample_bin(old_data, trace_row(b, highs), highs, times_ref, at, b, scales, vals)
    both[...] = split_values(vals)
    spread_image(bins_x)
    for k in range(2):
        for x in range(wide_x):
            at = k * columns + x * wide_y
            out_left[k, x] = s_ref[pl.ds(at, RADIUS), :]
            out_mid[k, x] = s_ref[pl.ds(at + RADIUS, bins_y), :]
            out_right[k, x] = s_ref[pl.ds(at + RADIUS + bins_y, RADIUS), :]


def fold_y_kernel(mid_ref, low_ref, high_ref, out_head, out_mid, out_tail):
    wide_x, bins_y = mid_ref.shape[1], mid_ref.shape[2]
    bins_x = wide_x - 2 * RADIUS
    for k in range(2):
        for x in range(wide_x):
            if x < RADIUS:
                ref, at = out_head, x
            elif x < RADIUS + bins_x:
                ref, at = out_mid, x - RADIUS
            else:
                ref, at = out_tail, x - RADIUS - bins_x
            ref[k, at, pl.ds(0, RADIUS), :] = mid_ref[k, x, pl.ds(0, RADIUS), :] + low_ref[k, x]
            high = pl.ds(bins_y - RADIUS, RADIUS)
            ref[k, at, high, :] = mid_ref[k, x, high, :] + high_ref[k, x]


def fold_x_kernel(mid_ref, low_ref, high_ref, grad_ref, curv_ref, out_ref, stats_ref):
    bins_x = mid_ref.shape[1]
    sums = [jnp.zeros((1, LANES), F32) for _ in range(5)]
    for x in range(bins_x):
        pair = []
        for k in range(2):
            cells = mid_ref[k, x]
            if x < RADIUS:
                cells = cells + low_ref[k, x]
            else:
                cells = cells + high_ref[k, x - RADIUS]
            out_ref[k, x] = cells
            pair.append(cells)
        old = grad_ref[x]
        terms = (old * old, None, pair[0] * pair[0], pair[0] * pair[1], pair[1] * pair[1])
        for n, term in enumerate(terms):
            if term is not None:
                sums[n] = sums[n] + jnp.sum(term, axis=0, keepdims=True)
    sums[1] = jnp.sum(curv_ref[...], axis=0, keepdims=True)
    lane = lax.broadcasted_iota(jnp.int32, (1, LANES), 1)
    stats = jnp.zeros((1, LANES), F32)
    for n, term in enumerate(sums):
        stats = jnp.where(lane == n, jnp.sum(term, axis=1, keepdims=True), stats)
    stats_ref[...] = jnp.broadcast_to(stats[None], stats_ref.shape)


def last_kernel(
    stats_ref, res_ref, data_ref, model_ref, dir_ref, grad_ref, new_image, new_residual, new_dir
):
    stats = jnp.sum(stats_ref[...], axis=0)
    lane = lax.broadcasted_iota(jnp.int32, stats.shape, 1)

    def pick(n):
        return jnp.sum(jnp.where(lane == n, stats, 0.0), axis=1, keepdims=True)

    gamma, curvature, one_one, one_two, two_two = (pick(n) for n in range(5))
    alpha = gamma / curvature
    gamma_new = one_one - 2.0 * (alpha * one_two) + alpha * (alpha * two_two)
    beta = gamma_new / gamma
    new_residual[...] = res_ref[...] - alpha * data_ref[...]
    step = dir_ref[...]
    new_image[...] = model_ref[...] + alpha[None] * step
    new_dir[...] = (grad_ref[0] - alpha[None] * grad_ref[1]) + beta[None] * step


def shift(cells, axis, by):
    count = lax.axis_size(axis)
    pairs = [(i, i + by) for i in range(count) if 0 <= i + by < count]
    return lax.ppermute(cells, axis, pairs)


def body(
    model_image,
    data_residual,
    direction,
    old_gradient,
    aperture,
    travel_times,
    amplitude,
    trace_counts,
):
    bins_x, bins_y, samples = data_residual.shape
    entries, depths = travel_times.shape[2], travel_times.shape[3]
    highs = samples // LANES
    wide_x, wide_y = bins_x + 2 * RADIUS, bins_y + 2 * RADIUS
    columns = wide_x * wide_y
    span = SIDE * wide_y
    geo = (bins_y, entries, highs, wide_y)
    rows_per = bins_y * highs

    from_prev = shift(direction, "gx", 1)[bins_x - RADIUS :]
    from_next = shift(direction, "gx", -1)[:RADIUS]

    times = travel_times.reshape(bins_x * bins_y, entries, depths)
    res_rows = to_rows(data_residual)
    def first(row0, count, counts, limit):
        return pl.pallas_call(
            functools.partial(first_kernel, geo, row0),
            grid=(count,),
            in_specs=[
                pl.BlockSpec((rows_per, LANES), lambda i: (i + row0, 0)),
                pl.BlockSpec((bins_y, entries, depths), lambda i: (i + row0, 0, 0)),
                pl.BlockSpec((1, bins_y, entries), lambda i: (i + row0, 0, 0)),
                pl.BlockSpec((bins_x, bins_y), lambda i: (0, 0)),
                pl.BlockSpec((1, bins_y, entries), lambda i: (i + row0, 0, 0)),
            ],
            out_specs=pl.BlockSpec((columns, depths), lambda i: (0, 0)),
            out_shape=jax.ShapeDtypeStruct((columns, depths), F32),
            scratch_shapes=[pltpu.VMEM((bins_y * entries, depths), F32)] * 2
            + [pltpu.VMEM((rows_per + SUB, LANES), F32)],
            compiler_params=params(limit),
            cost_estimate=pl.CostEstimate(
                flops=4 * 10**9, bytes_accessed=4 * 10**6, transcendentals=0
            ),
            name="sample_residual",
        )(res_rows, times, amplitude, counts, aperture)

    early = bins_x // 4
    row0 = 2 * early
    s1 = first(0, early, trace_counts, FIRST_LIMIT)
    ext = jnp.concatenate([from_prev, direction, from_next], axis=0)
    tail, head, s1, counts = lax.optimization_barrier(
        (ext[:, bins_y - RADIUS :], ext[:, :RADIUS], s1, trace_counts)
    )
    left = shift(tail, "gy", 1)
    right = shift(head, "gy", -1)
    s1_more = first(early, early - 1, counts, VMEM_LIMIT)

    cut = bins_x // (bins_x - row0)
    res_bins = bins_y // cut
    parts = trace_counts.reshape(bins_x * cut, res_bins)
    strip = jax.ShapeDtypeStruct((2, wide_x, RADIUS, depths), F32)
    vals_shape = pltpu.VMEM((bins_y * entries, depths), F32)
    res_shape = pltpu.VMEM((res_bins * entries, depths), F32)
    columns_shape = pltpu.VMEM((columns, depths), F32)
    in_vmem = pl.BlockSpec(memory_space=pltpu.VMEM)
    data_rows, curv, out_left, out_mid, out_right = pl.pallas_call(
        functools.partial(main_kernel, geo, row0),
        in_specs=[pl.BlockSpec(memory_space=pltpu.SMEM)] + [in_vmem] * 11,
        out_specs=[in_vmem] * 5,
        out_shape=[
            jax.ShapeDtypeStruct((bins_x * rows_per, LANES), F32),
            jax.ShapeDtypeStruct((highs, LANES), F32),
            strip,
            jax.ShapeDtypeStruct((2, wide_x, bins_y, depths), F32),
            strip,
        ],
        scratch_shapes=[columns_shape, pltpu.VMEM((2 * columns, depths), F32)]
        + [vals_shape, res_shape, vals_shape, vals_shape, res_shape]
        + [pltpu.VMEM((rows_per + SUB, LANES), F32)]
        + [pltpu.VMEM((bins_y * entries, 2 * depths), BF16)]
        + [pltpu.VMEM((res_bins * entries, 2 * depths), BF16)]
        + [pltpu.VMEM((res_bins * highs + SUB, LANES), F32)]
        + [pltpu.VMEM((4, entries + SUB, LANES), F32)] * 8,
        compiler_params=params(MAIN_LIMIT),
        cost_estimate=pl.CostEstimate(
            flops=20 * 10**9, bytes_accessed=8 * 10**6, transcendentals=0
        ),
        name="demigrate_and_sample",
    )(
        aperture,
        times,
        amplitude,
        trace_counts,
        parts,
        aperture,
        res_rows,
        ext,
        left,
        right,
        s1,
        s1_more,
    )

    from_low = shift(out_right, "gy", 1)
    from_high = shift(out_left, "gy", -1)
    edge = jax.ShapeDtypeStruct((2, RADIUS, bins_y, depths), F32)
    out_head, inner, out_tail = pl.pallas_call(
        fold_y_kernel,
        out_shape=[edge, jax.ShapeDtypeStruct((2, bins_x, bins_y, depths), F32), edge],
        compiler_params=params(SMALL_LIMIT),
        name="fold_y",
    )(out_mid, from_low, from_high)
    from_low = shift(out_tail, "gx", 1)
    from_high = shift(out_head, "gx", -1)
    devices = lax.axis_size("gx") * lax.axis_size("gy")
    grads, stats = pl.pallas_call(
        fold_x_kernel,
        out_shape=[
            jax.ShapeDtypeStruct((2, bins_x, bins_y, depths), F32),
            jax.ShapeDtypeStruct((devices, 1, LANES), F32),
        ],
        compiler_params=params(SMALL_LIMIT),
        name="fold_x",
    )(inner, from_low, from_high, old_gradient, curv)
    stats = lax.all_to_all(stats, ("gx", "gy"), 0, 0, tiled=True)

    steps = 4
    rows_step = bins_x * rows_per // steps
    x_step = bins_x // steps
    cells = pl.BlockSpec((x_step, bins_y, depths), lambda i: (i, 0, 0))
    rows = pl.BlockSpec((rows_step, LANES), lambda i: (i, 0))
    image_shape = jax.ShapeDtypeStruct(direction.shape, F32)
    new_image, new_rows, new_direction = pl.pallas_call(
        last_kernel,
        grid=(steps,),
        in_specs=[
            pl.BlockSpec(stats.shape, lambda i: (0, 0, 0)),
            rows,
            rows,
            cells,
            cells,
            pl.BlockSpec((2, x_step, bins_y, depths), lambda i: (0, i, 0, 0)),
        ],
        out_specs=[cells, rows, cells],
        out_shape=[image_shape, jax.ShapeDtypeStruct(res_rows.shape, F32), image_shape],
        compiler_params=params(SMALL_LIMIT),
        name="update",
    )(stats, res_rows, data_rows, model_image, direction, grads)
    return (new_image, from_rows(new_rows, data_residual.shape), new_direction)


def solution(mesh):
    in_specs = (
        P("gx", "gy", None),
        P("gx", "gy", None),
        P("gx", "gy", None),
        P("gx", "gy", None),
        P("gx", "gy", None),
        P("gx", "gy", None, None),
        P("gx", "gy", None),
        P("gx", "gy"),
    )
    out_specs = (P("gx", "gy", None), P("gx", "gy", None), P("gx", "gy", None))
    return jax.shard_map(body, mesh=mesh, in_specs=in_specs, out_specs=out_specs, check_vma=False)
```

```python
import functools

import jax
import jax.numpy as jnp
from jax import lax
from jax.experimental import pallas as pl
from jax.experimental.pallas import tpu as pltpu
from jax.sharding import PartitionSpec as P

RADIUS = 8
SIDE = 2 * RADIUS + 1
LANES = 128
SUB = 8
F32 = jnp.float32
BF16 = jnp.bfloat16
VMEM_LIMIT = 51 * 1024 * 1024
FIRST_LIMIT = 59 * 1024 * 1024
MAIN_LIMIT = 36 * 1024 * 1024
SMALL_LIMIT = 24 * 1024 * 1024


def params(limit=VMEM_LIMIT):
    return pltpu.CompilerParams(vmem_limit_bytes=limit)


def to_rows(traces):
    bins_x, bins_y, samples = traces.shape
    parts = traces.reshape(bins_x, bins_y // SUB, SUB, samples // LANES, LANES)
    return parts.transpose(0, 1, 3, 2, 4).reshape(-1, LANES)


def from_rows(rows, shape):
    bins_x, bins_y, samples = shape
    parts = rows.reshape(bins_x, bins_y // SUB, samples // LANES, SUB, LANES)
    return parts.transpose(0, 1, 3, 2, 4).reshape(shape)


def trace_row(b, highs):
    return (b // SUB) * (SUB * highs) + b % SUB


def fill_weights(amplitude, counts, scales):
    bins, entries = amplitude.shape
    weight = amplitude.T * counts.astype(F32)
    for b in range(bins):
        column = jnp.broadcast_to(weight[:, b : b + 1], (entries, LANES))
        scales[pl.ds(b * entries, entries), :] = column


def sample_bin(source, first, highs, times_ref, bin_at, b, scales, vals):
    entries = times_ref.shape[1]
    tables = [source[pl.ds(first + SUB * h, SUB, stride=0), :] for h in range(highs)]
    for part in range(0, entries, SUB):
        times = times_ref[bin_at, pl.ds(part, SUB), :]
        high = jnp.right_shift(times, LANES.bit_length() - 1)
        low = jnp.bitwise_and(times, LANES - 1)
        acc = jnp.zeros(times.shape, F32)
        for h in range(highs):
            got = jnp.take_along_axis(tables[h], low, axis=1, mode="promise_in_bounds")
            acc = jnp.where(high == h, got, acc)
        at = b * entries + part
        at = pl.ds(at if isinstance(at, int) else pl.multiple_of(at, SUB), SUB)
        vals[at, :] = acc * scales[at, :]


def column_offset(entry, wide_y):
    return entry + jnp.right_shift(entry * 241, 12) * (wide_y - SIDE)


def place_row(aperture, wide_y, first_bin=0):
    offset = column_offset(aperture, wide_y)
    return jnp.concatenate(
        [offset[b : b + 1, :] + (b + first_bin) for b in range(offset.shape[0])], axis=1
    )


def split_values(vals):
    value = vals[...]
    upper = value.astype(BF16)
    lower = (value - upper.astype(F32)).astype(BF16)
    return jnp.concatenate([upper, lower], axis=1)


def spread_bins(both, place, s_ref, row, wide_y):
    span = SIDE * wide_y
    iota = lax.broadcasted_iota(jnp.int32, (span, place.shape[1]), 0)
    table = jnp.where(iota == place, 1.0, 0.0).astype(BF16)
    part = jnp.dot(table, both, preferred_element_type=F32)
    s_ref[pl.ds(pl.multiple_of(row * wide_y, SUB), span), :] += part[:, :LANES] + part[:, LANES:]


def first_kernel(
    geo,
    row0,
    res_ref,
    times_ref,
    amp_ref,
    counts_ref,
    old_aper_ref,
    aper_ref,
    s_ref,
    vals,
    scales,
    traces,
    both,
):
    bins_y, entries, highs, wide_y = geo
    step = pl.program_id(0)

    @pl.when(step == 0)
    def _():
        s_ref[...] = jnp.zeros_like(s_ref)
        both[...] = jnp.zeros_like(both)

    before = jnp.maximum(step - 1, 0) + row0
    spread_bins(both[...], place_row(old_aper_ref[0], wide_y), s_ref, before, wide_y)
    traces[pl.ds(0, bins_y * highs), :] = res_ref[...]
    fill_weights(amp_ref[0], counts_ref[pl.ds(step + row0, 1), :], scales)
    for b in range(bins_y):
        sample_bin(traces, trace_row(b, highs), highs, times_ref, b, b, scales, vals)
    both[...] = split_values(vals)

    @pl.when(step == pl.num_programs(0) - 1)
    def _():
        spread_bins(both[...], place_row(aper_ref[0], wide_y), s_ref, step + row0, wide_y)


def scatter_bin(geo, row, b, image, entry_ref, times_ref, scales, work):
    bins_y, entries, highs, wide_y = geo
    half = LANES // 2
    half_bits = half.bit_length() - 1
    iota16 = lax.broadcasted_iota(jnp.int32, (16, LANES), 0)
    iota_lo = [(iota16 + k).astype(F32).astype(BF16) for k in range(0, half, 16)]
    iota_hi = [(iota16 + k).astype(F32).astype(BF16) for k in range(0, 2 * highs, 16)]
    zero = jnp.zeros((), BF16)
    one = jnp.ones((), BF16)
    for e in range(entries):
        column = column_offset(entry_ref[row, b, e], wide_y) + (row * wide_y + b)
        work[0, pl.ds(e, 1), :] = image[pl.ds(column, 1), :]
    value = work[0, pl.ds(0, entries), :]
    value = value * scales[pl.ds(b * entries, entries), :]
    upper = value.astype(BF16).astype(F32)
    times = times_ref[row * bins_y + b]
    middle = jnp.bitwise_and(jnp.right_shift(times, half_bits), 1)
    rows = pl.ds(0, entries)
    work[0, rows, :] = upper
    work[1, rows, :] = value - upper
    work[2, rows, :] = jnp.bitwise_and(times, half - 1).astype(F32)
    work[3, rows, :] = (jnp.right_shift(times, half_bits + 1) + middle * highs).astype(F32)
    lefts = []
    rights = []
    for e in range(entries):

        def wide(k):
            row = work[k, pl.ds(e, SUB, stride=0), :]
            return jnp.concatenate([row, row], axis=0).astype(BF16)

        place = wide(3)
        hits = [place == iota for iota in iota_hi]
        parts = [jnp.where(hit, wide(k), zero) for k in range(2) for hit in hits]
        lefts.append(jnp.concatenate(parts, axis=0))
        low = wide(2)
        rights.append(
            jnp.concatenate([jnp.where(low == iota, one, zero) for iota in iota_lo], axis=0)
        )
    out = lax.dot_general(
        jnp.concatenate(lefts, axis=1),
        jnp.concatenate(rights, axis=1),
        (((1,), (1,)), ((), ())),
        preferred_element_type=F32,
    )
    out = out[: 2 * highs] + out[2 * highs :]
    return jnp.concatenate([out[:highs], out[highs:]], axis=1)


def main_kernel(
    geo,
    row0,
    entry_ref,
    times_ref,
    amp_ref,
    counts_ref,
    parts_ref,
    aper_ref,
    res_ref,
    mid_ref,
    left_ref,
    right_ref,
    s1_in_ref,
    s1_more_ref,
    data_ref,
    curv_ref,
    out_left,
    out_mid,
    out_right,
    image,
    s_ref,
    vals,
    res_vals,
    scales,
    old_scales,
    res_scales,
    old_data,
    both,
    res_both,
    traces,
    *works,
):
    bins_y, entries, highs, wide_y = geo
    bins_x = amp_ref.shape[0]
    wide_x = mid_ref.shape[0]
    rows_per = bins_y * highs
    cut = bins_x // (bins_x - row0)
    res_bins = bins_y // cut

    columns = wide_x * wide_y
    current = pl.ds(0, rows_per)
    s_ref[pl.ds(0, columns), :] = s1_in_ref[...] + s1_more_ref[...]
    s_ref[pl.ds(columns, columns), :] = jnp.zeros((columns, LANES), F32)
    odd_row = row0 - 1
    old_data[current, :] = res_ref[pl.ds(odd_row * rows_per, rows_per), :]
    fill_weights(amp_ref[odd_row], counts_ref[pl.ds(odd_row, 1), :], scales)
    both[...] = jnp.zeros_like(both)
    res_both[...] = jnp.zeros_like(res_both)
    for x in range(wide_x):
        image[pl.ds(x * wide_y, RADIUS), :] = left_ref[x]
        image[pl.ds(x * wide_y + RADIUS, bins_y), :] = mid_ref[x]
        image[pl.ds(x * wide_y + RADIUS + bins_y, RADIUS), :] = right_ref[x]

    def residual_part(step):
        return row0 + step // cut, (step % cut) * res_bins

    def spread_image(step):
        row = jnp.where(step < 1, odd_row, step - 1)
        at = jnp.where(step < 1, odd_row, step - 1 + wide_x)
        spread_bins(both[...], place_row(aper_ref[row], wide_y), s_ref, at, wide_y)

    def spread_residual(step):
        row, part = residual_part(step)
        entry = aper_ref[row, pl.ds(pl.multiple_of(part, SUB), res_bins), :]
        spread_bins(res_both[...], place_row(entry, wide_y, part), s_ref, row, wide_y)

    def one_row(step, total):
        before = jnp.where(step < 1, odd_row, step - 1)
        spread_image(step - 1)
        spread_residual(jnp.maximum(step - 1, 0))
        res_row, res_part = residual_part(step)
        res_first = pl.multiple_of(res_row * rows_per + res_part * highs, SUB)
        old_scales[...] = scales[...]
        part = res_bins * highs
        traces[pl.ds(0, part), :] = res_ref[pl.ds(res_first, part), :]
        fill_weights(amp_ref[step], counts_ref[pl.ds(step, 1), :], scales)
        fill_weights(
            amp_ref[res_row, pl.ds(pl.multiple_of(res_part, SUB), res_bins), :],
            parts_ref[pl.ds(row0 * cut + step, 1), :],
            res_scales,
        )
        for b in range(bins_y):
            trace = scatter_bin(
                geo, step, b, image, entry_ref, times_ref, scales, works[b % len(works)]
            )
            first = trace_row(b, highs)
            data_ref[pl.ds(step * rows_per + first, highs, stride=SUB), :] = trace
            total = total + trace * trace
            sample_bin(
                old_data, first, highs, times_ref, before * bins_y + b, b, old_scales, vals
            )
            if b % cut == 0:
                r = b // cut
                first = trace_row(r, highs)
                at = res_row * bins_y + res_part + r
                sample_bin(traces, first, highs, times_ref, at, r, res_scales, res_vals)
        both[...] = split_values(vals)
        res_both[...] = split_values(res_vals)
        old_data[current, :] = data_ref[pl.ds(pl.multiple_of(step * rows_per, SUB), rows_per), :]
        return total

    curv_ref[...] = lax.fori_loop(0, bins_x, one_row, jnp.zeros((highs, LANES), F32))
    last = bins_x - 1
    spread_image(last)
    spread_residual(last)
    for b in range(bins_y):
        at = last * bins_y + b
        sample_bin(old_data, trace_row(b, highs), highs, times_ref, at, b, scales, vals)
    both[...] = split_values(vals)
    spread_image(bins_x)
    for k in range(2):
        for x in range(wide_x):
            at = k * columns + x * wide_y
            out_left[k, x] = s_ref[pl.ds(at, RADIUS), :]
            out_mid[k, x] = s_ref[pl.ds(at + RADIUS, bins_y), :]
            out_right[k, x] = s_ref[pl.ds(at + RADIUS + bins_y, RADIUS), :]


def fold_y_kernel(mid_ref, low_ref, high_ref, out_head, out_mid, out_tail):
    wide_x, bins_y = mid_ref.shape[1], mid_ref.shape[2]
    bins_x = wide_x - 2 * RADIUS
    for k in range(2):
        for x in range(wide_x):
            if x < RADIUS:
                ref, at = out_head, x
            elif x < RADIUS + bins_x:
                ref, at = out_mid, x - RADIUS
            else:
                ref, at = out_tail, x - RADIUS - bins_x
            ref[k, at, pl.ds(0, RADIUS), :] = mid_ref[k, x, pl.ds(0, RADIUS), :] + low_ref[k, x]
            high = pl.ds(bins_y - RADIUS, RADIUS)
            ref[k, at, high, :] = mid_ref[k, x, high, :] + high_ref[k, x]


def fold_x_kernel(mid_ref, low_ref, high_ref, grad_ref, curv_ref, out_ref, stats_ref):
    bins_x = mid_ref.shape[1]
    sums = [jnp.zeros(mid_ref.shape[2:], F32) for _ in range(5)]
    for x in range(bins_x):
        pair = []
        for k in range(2):
            cells = mid_ref[k, x]
            if x < RADIUS:
                cells = cells + low_ref[k, x]
            else:
                cells = cells + high_ref[k, x - RADIUS]
            out_ref[k, x] = cells
            pair.append(cells)
        old = grad_ref[x]
        terms = (old * old, None, pair[0] * pair[0], pair[0] * pair[1], pair[1] * pair[1])
        for n, term in enumerate(terms):
            if term is not None:
                sums[n] = sums[n] + term
    sums[1] = curv_ref[...]
    sums = [jnp.sum(term, axis=0, keepdims=True) for term in sums]
    lane = lax.broadcasted_iota(jnp.int32, (1, LANES), 1)
    stats = jnp.zeros((1, LANES), F32)
    for n, term in enumerate(sums):
        stats = jnp.where(lane == n, jnp.sum(term, axis=1, keepdims=True), stats)
    stats_ref[...] = jnp.broadcast_to(stats[None], stats_ref.shape)


def last_kernel(
    stats_ref, res_ref, data_ref, model_ref, dir_ref, grad_ref, new_image, new_residual, new_dir
):
    stats = jnp.sum(stats_ref[...], axis=0)
    lane = lax.broadcasted_iota(jnp.int32, stats.shape, 1)

    def pick(n):
        return jnp.sum(jnp.where(lane == n, stats, 0.0), axis=1, keepdims=True)

    gamma, curvature, one_one, one_two, two_two = (pick(n) for n in range(5))
    alpha = gamma / curvature
    gamma_new = one_one - 2.0 * (alpha * one_two) + alpha * (alpha * two_two)
    beta = gamma_new / gamma
    new_residual[...] = res_ref[...] - alpha * data_ref[...]
    step = dir_ref[...]
    new_image[...] = model_ref[...] + alpha[None] * step
    new_dir[...] = (grad_ref[0] - alpha[None] * grad_ref[1]) + beta[None] * step


def shift(cells, axis, by):
    count = lax.axis_size(axis)
    pairs = [(i, i + by) for i in range(count) if 0 <= i + by < count]
    return lax.ppermute(cells, axis, pairs)


def body(
    model_image,
    data_residual,
    direction,
    old_gradient,
    aperture,
    travel_times,
    amplitude,
    trace_counts,
):
    bins_x, bins_y, samples = data_residual.shape
    entries, depths = travel_times.shape[2], travel_times.shape[3]
    highs = samples // LANES
    wide_x, wide_y = bins_x + 2 * RADIUS, bins_y + 2 * RADIUS
    columns = wide_x * wide_y
    span = SIDE * wide_y
    geo = (bins_y, entries, highs, wide_y)
    rows_per = bins_y * highs

    from_prev = shift(direction, "gx", 1)[bins_x - RADIUS :]
    from_next = shift(direction, "gx", -1)[:RADIUS]

    times = travel_times.reshape(bins_x * bins_y, entries, depths)
    res_rows = to_rows(data_residual)
    def first(row0, count, counts, limit):
        return pl.pallas_call(
            functools.partial(first_kernel, geo, row0),
            grid=(count,),
            in_specs=[
                pl.BlockSpec((rows_per, LANES), lambda i: (i + row0, 0)),
                pl.BlockSpec((bins_y, entries, depths), lambda i: (i + row0, 0, 0)),
                pl.BlockSpec((1, bins_y, entries), lambda i: (i + row0, 0, 0)),
                pl.BlockSpec((bins_x, bins_y), lambda i: (0, 0)),
                pl.BlockSpec((1, bins_y, entries), lambda i: (jnp.maximum(i - 1, 0) + row0, 0, 0)),
                pl.BlockSpec((1, bins_y, entries), lambda i: (i + row0, 0, 0)),
            ],
            out_specs=pl.BlockSpec((columns, depths), lambda i: (0, 0)),
            out_shape=jax.ShapeDtypeStruct((columns, depths), F32),
            scratch_shapes=[pltpu.VMEM((bins_y * entries, depths), F32)] * 2
            + [pltpu.VMEM((rows_per + SUB, LANES), F32)]
            + [pltpu.VMEM((bins_y * entries, 2 * depths), BF16)],
            compiler_params=params(limit),
            cost_estimate=pl.CostEstimate(
                flops=4 * 10**9, bytes_accessed=4 * 10**6, transcendentals=0
            ),
            name="sample_residual",
        )(res_rows, times, amplitude, counts, aperture, aperture)

    early = bins_x // 4
    row0 = 2 * early
    s1 = first(0, early, trace_counts, FIRST_LIMIT)
    ext = jnp.concatenate([from_prev, direction, from_next], axis=0)
    tail, head, s1, counts = lax.optimization_barrier(
        (ext[:, bins_y - RADIUS :], ext[:, :RADIUS], s1, trace_counts)
    )
    left = shift(tail, "gy", 1)
    right = shift(head, "gy", -1)
    s1_more = first(early, early - 1, counts, VMEM_LIMIT)

    cut = bins_x // (bins_x - row0)
    res_bins = bins_y // cut
    parts = trace_counts.reshape(bins_x * cut, res_bins)
    strip = jax.ShapeDtypeStruct((2, wide_x, RADIUS, depths), F32)
    vals_shape = pltpu.VMEM((bins_y * entries, depths), F32)
    res_shape = pltpu.VMEM((res_bins * entries, depths), F32)
    columns_shape = pltpu.VMEM((columns, depths), F32)
    in_vmem = pl.BlockSpec(memory_space=pltpu.VMEM)
    data_rows, curv, out_left, out_mid, out_right = pl.pallas_call(
        functools.partial(main_kernel, geo, row0),
        in_specs=[pl.BlockSpec(memory_space=pltpu.SMEM)] + [in_vmem] * 11,
        out_specs=[in_vmem] * 5,
        out_shape=[
            jax.ShapeDtypeStruct((bins_x * rows_per, LANES), F32),
            jax.ShapeDtypeStruct((highs, LANES), F32),
            strip,
            jax.ShapeDtypeStruct((2, wide_x, bins_y, depths), F32),
            strip,
        ],
        scratch_shapes=[columns_shape, pltpu.VMEM((2 * columns, depths), F32)]
        + [vals_shape, res_shape, vals_shape, vals_shape, res_shape]
        + [pltpu.VMEM((rows_per + SUB, LANES), F32)]
        + [pltpu.VMEM((bins_y * entries, 2 * depths), BF16)]
        + [pltpu.VMEM((res_bins * entries, 2 * depths), BF16)]
        + [pltpu.VMEM((res_bins * highs + SUB, LANES), F32)]
        + [pltpu.VMEM((4, entries + SUB, LANES), F32)] * 8,
        compiler_params=params(MAIN_LIMIT),
        cost_estimate=pl.CostEstimate(
            flops=20 * 10**9, bytes_accessed=8 * 10**6, transcendentals=0
        ),
        name="demigrate_and_sample",
    )(
        aperture,
        times,
        amplitude,
        trace_counts,
        parts,
        aperture,
        res_rows,
        ext,
        left,
        right,
        s1,
        s1_more,
    )

    from_low = shift(out_right, "gy", 1)
    from_high = shift(out_left, "gy", -1)
    edge = jax.ShapeDtypeStruct((2, RADIUS, bins_y, depths), F32)
    out_head, inner, out_tail = pl.pallas_call(
        fold_y_kernel,
        out_shape=[edge, jax.ShapeDtypeStruct((2, bins_x, bins_y, depths), F32), edge],
        compiler_params=params(SMALL_LIMIT),
        name="fold_y",
    )(out_mid, from_low, from_high)
    from_low = shift(out_tail, "gx", 1)
    from_high = shift(out_head, "gx", -1)
    devices = lax.axis_size("gx") * lax.axis_size("gy")
    grads, stats = pl.pallas_call(
        fold_x_kernel,
        out_shape=[
            jax.ShapeDtypeStruct((2, bins_x, bins_y, depths), F32),
            jax.ShapeDtypeStruct((devices, 1, LANES), F32),
        ],
        compiler_params=params(SMALL_LIMIT),
        name="fold_x",
    )(inner, from_low, from_high, old_gradient, curv)
    stats = lax.all_to_all(stats, ("gx", "gy"), 0, 0, tiled=True)

    steps = 4
    rows_step = bins_x * rows_per // steps
    x_step = bins_x // steps
    cells = pl.BlockSpec((x_step, bins_y, depths), lambda i: (i, 0, 0))
    rows = pl.BlockSpec((rows_step, LANES), lambda i: (i, 0))
    image_shape = jax.ShapeDtypeStruct(direction.shape, F32)
    new_image, new_rows, new_direction = pl.pallas_call(
        last_kernel,
        grid=(steps,),
        in_specs=[
            pl.BlockSpec(stats.shape, lambda i: (0, 0, 0)),
            rows,
            rows,
            cells,
            cells,
            pl.BlockSpec((2, x_step, bins_y, depths), lambda i: (0, i, 0, 0)),
        ],
        out_specs=[cells, rows, cells],
        out_shape=[image_shape, jax.ShapeDtypeStruct(res_rows.shape, F32), image_shape],
        compiler_params=params(SMALL_LIMIT),
        name="update",
    )(stats, res_rows, data_rows, model_image, direction, grads)
    return (new_image, from_rows(new_rows, data_residual.shape), new_direction)


def solution(mesh):
    in_specs = (
        P("gx", "gy", None),
        P("gx", "gy", None),
        P("gx", "gy", None),
        P("gx", "gy", None),
        P("gx", "gy", None),
        P("gx", "gy", None, None),
        P("gx", "gy", None),
        P("gx", "gy"),
    )
    out_specs = (P("gx", "gy", None), P("gx", "gy", None), P("gx", "gy", None))
    return jax.shard_map(body, mesh=mesh, in_specs=in_specs, out_specs=out_specs, check_vma=False)
```

```python
import functools

import jax
import jax.numpy as jnp
from jax import lax
from jax.experimental import pallas as pl
from jax.experimental.pallas import tpu as pltpu
from jax.sharding import PartitionSpec as P

RADIUS = 8
SIDE = 2 * RADIUS + 1
LANES = 128
SUB = 8
F32 = jnp.float32
BF16 = jnp.bfloat16
VMEM_LIMIT = 51 * 1024 * 1024
FIRST_LIMIT = 59 * 1024 * 1024
MAIN_LIMIT = 36 * 1024 * 1024
SMALL_LIMIT = 24 * 1024 * 1024


def params(limit=VMEM_LIMIT):
    return pltpu.CompilerParams(vmem_limit_bytes=limit)


def to_rows(traces):
    bins_x, bins_y, samples = traces.shape
    parts = traces.reshape(bins_x, bins_y // SUB, SUB, samples // LANES, LANES)
    return parts.transpose(0, 1, 3, 2, 4).reshape(-1, LANES)


def from_rows(rows, shape):
    bins_x, bins_y, samples = shape
    parts = rows.reshape(bins_x, bins_y // SUB, samples // LANES, SUB, LANES)
    return parts.transpose(0, 1, 3, 2, 4).reshape(shape)


def trace_row(b, highs):
    return (b // SUB) * (SUB * highs) + b % SUB


def fill_weights(amplitude, counts, scales):
    bins, entries = amplitude.shape
    weight = amplitude.T * counts.astype(F32)
    for b in range(bins):
        column = jnp.broadcast_to(weight[:, b : b + 1], (entries, LANES))
        scales[pl.ds(b * entries, entries), :] = column


def sample_bin(source, first, highs, times_ref, bin_at, b, scales, vals):
    entries = times_ref.shape[1]
    tables = [source[pl.ds(first + SUB * h, SUB, stride=0), :] for h in range(highs)]
    for part in range(0, entries, SUB):
        times = times_ref[bin_at, pl.ds(part, SUB), :]
        high = jnp.right_shift(times, LANES.bit_length() - 1)
        low = jnp.bitwise_and(times, LANES - 1)
        acc = jnp.zeros(times.shape, F32)
        for h in range(highs):
            got = jnp.take_along_axis(tables[h], low, axis=1, mode="promise_in_bounds")
            acc = jnp.where(high == h, got, acc)
        at = b * entries + part
        at = pl.ds(at if isinstance(at, int) else pl.multiple_of(at, SUB), SUB)
        vals[at, :] = acc * scales[at, :]


def column_offset(entry, wide_y):
    return entry + jnp.right_shift(entry * 241, 12) * (wide_y - SIDE)


def place_row(aperture, wide_y, first_bin=0):
    offset = column_offset(aperture, wide_y)
    return jnp.concatenate(
        [offset[b : b + 1, :] + (b + first_bin) for b in range(offset.shape[0])], axis=1
    )


def split_values(vals):
    value = vals[...]
    upper = value.astype(BF16)
    lower = (value - upper.astype(F32)).astype(BF16)
    return jnp.concatenate([upper, lower], axis=1)


def spread_bins(both, place, s_ref, row, wide_y):
    span = SIDE * wide_y
    iota = lax.broadcasted_iota(jnp.int32, (span, place.shape[1]), 0)
    table = jnp.where(iota == place, 1.0, 0.0).astype(BF16)
    part = jnp.dot(table, both, preferred_element_type=F32)
    s_ref[pl.ds(pl.multiple_of(row * wide_y, SUB), span), :] += part[:, :LANES] + part[:, LANES:]


def first_kernel(
    geo,
    row0,
    res_ref,
    times_ref,
    amp_ref,
    counts_ref,
    old_aper_ref,
    aper_ref,
    s_ref,
    vals,
    scales,
    traces,
    both,
):
    bins_y, entries, highs, wide_y = geo
    step = pl.program_id(0)

    @pl.when(step == 0)
    def _():
        s_ref[...] = jnp.zeros_like(s_ref)
        both[...] = jnp.zeros_like(both)

    before = jnp.maximum(step - 1, 0) + row0
    spread_bins(both[...], place_row(old_aper_ref[0], wide_y), s_ref, before, wide_y)
    traces[pl.ds(0, bins_y * highs), :] = res_ref[...]
    fill_weights(amp_ref[0], counts_ref[pl.ds(step + row0, 1), :], scales)
    for b in range(bins_y):
        sample_bin(traces, trace_row(b, highs), highs, times_ref, b, b, scales, vals)
    both[...] = split_values(vals)

    @pl.when(step == pl.num_programs(0) - 1)
    def _():
        spread_bins(both[...], place_row(aper_ref[0], wide_y), s_ref, step + row0, wide_y)


def scatter_bin(geo, row, b, image, entry_ref, times_ref, scales, work):
    bins_y, entries, highs, wide_y = geo
    half = LANES // 2
    half_bits = half.bit_length() - 1
    iota16 = lax.broadcasted_iota(jnp.int32, (16, LANES), 0)
    iota_lo = [(iota16 + k).astype(F32).astype(BF16) for k in range(0, half, 16)]
    iota_hi = [(iota16 + k).astype(F32).astype(BF16) for k in range(0, 2 * highs, 16)]
    zero = jnp.zeros((), BF16)
    one = jnp.ones((), BF16)
    for e in range(entries):
        column = column_offset(entry_ref[row, b, e], wide_y) + (row * wide_y + b)
        work[0, pl.ds(e, 1), :] = image[pl.ds(column, 1), :]
    value = work[0, pl.ds(0, entries), :]
    value = value * scales[pl.ds(b * entries, entries), :]
    upper = value.astype(BF16).astype(F32)
    times = times_ref[row * bins_y + b]
    middle = jnp.bitwise_and(jnp.right_shift(times, half_bits), 1)
    rows = pl.ds(0, entries)
    work[0, rows, :] = upper
    work[1, rows, :] = value - upper
    work[2, rows, :] = jnp.bitwise_and(times, half - 1).astype(F32)
    work[3, rows, :] = (jnp.right_shift(times, half_bits + 1) + middle * highs).astype(F32)
    lefts = []
    rights = []
    for e in range(entries):

        def wide(k):
            row = work[k, pl.ds(e, SUB, stride=0), :]
            return jnp.concatenate([row, row], axis=0).astype(BF16)

        place = wide(3)
        hits = [place == iota for iota in iota_hi]
        parts = [jnp.where(hit, wide(k), zero) for k in range(2) for hit in hits]
        lefts.append(jnp.concatenate(parts, axis=0))
        low = wide(2)
        rights.append(
            jnp.concatenate([jnp.where(low == iota, one, zero) for iota in iota_lo], axis=0)
        )
    out = lax.dot_general(
        jnp.concatenate(lefts, axis=1),
        jnp.concatenate(rights, axis=1),
        (((1,), (1,)), ((), ())),
        preferred_element_type=F32,
    )
    out = out[: 2 * highs] + out[2 * highs :]
    return jnp.concatenate([out[:highs], out[highs:]], axis=1)


def main_kernel(
    geo,
    row0,
    entry_ref,
    times_ref,
    amp_ref,
    counts_ref,
    parts_ref,
    aper_ref,
    res_ref,
    mid_ref,
    left_ref,
    right_ref,
    s1_in_ref,
    s1_more_ref,
    data_ref,
    curv_ref,
    out_left,
    out_mid,
    out_right,
    image,
    s_ref,
    vals,
    res_vals,
    scales,
    old_scales,
    res_scales,
    old_data,
    both,
    res_both,
    traces,
    *works,
):
    bins_y, entries, highs, wide_y = geo
    bins_x = amp_ref.shape[0]
    wide_x = mid_ref.shape[0]
    rows_per = bins_y * highs
    cut = bins_x // (bins_x - row0)
    res_bins = bins_y // cut

    columns = wide_x * wide_y
    current = pl.ds(0, rows_per)
    s_ref[pl.ds(0, columns), :] = s1_in_ref[...] + s1_more_ref[...]
    s_ref[pl.ds(columns, columns), :] = jnp.zeros((columns, LANES), F32)
    odd_row = row0 - 1
    old_data[current, :] = res_ref[pl.ds(odd_row * rows_per, rows_per), :]
    fill_weights(amp_ref[odd_row], counts_ref[pl.ds(odd_row, 1), :], scales)
    both[...] = jnp.zeros_like(both)
    res_both[...] = jnp.zeros_like(res_both)
    for x in range(wide_x):
        image[pl.ds(x * wide_y, RADIUS), :] = left_ref[x]
        image[pl.ds(x * wide_y + RADIUS, bins_y), :] = mid_ref[x]
        image[pl.ds(x * wide_y + RADIUS + bins_y, RADIUS), :] = right_ref[x]

    def residual_part(step):
        return row0 + step // cut, (step % cut) * res_bins

    def spread_image(step):
        row = jnp.where(step < 1, odd_row, step - 1)
        at = jnp.where(step < 1, odd_row, step - 1 + wide_x)
        spread_bins(both[...], place_row(aper_ref[row], wide_y), s_ref, at, wide_y)

    def spread_residual(step):
        row, part = residual_part(step)
        entry = aper_ref[row, pl.ds(pl.multiple_of(part, SUB), res_bins), :]
        spread_bins(res_both[...], place_row(entry, wide_y, part), s_ref, row, wide_y)

    def one_row(step, total):
        before = jnp.where(step < 1, odd_row, step - 1)
        spread_image(step - 1)
        spread_residual(jnp.maximum(step - 1, 0))
        res_row, res_part = residual_part(step)
        res_first = pl.multiple_of(res_row * rows_per + res_part * highs, SUB)
        old_scales[...] = scales[...]
        part = res_bins * highs
        traces[pl.ds(0, part), :] = res_ref[pl.ds(res_first, part), :]
        fill_weights(amp_ref[step], counts_ref[pl.ds(step, 1), :], scales)
        fill_weights(
            amp_ref[res_row, pl.ds(pl.multiple_of(res_part, SUB), res_bins), :],
            parts_ref[pl.ds(row0 * cut + step, 1), :],
            res_scales,
        )
        for b in range(bins_y):
            trace = scatter_bin(
                geo, step, b, image, entry_ref, times_ref, scales, works[b % len(works)]
            )
            first = trace_row(b, highs)
            data_ref[pl.ds(step * rows_per + first, highs, stride=SUB), :] = trace
            total = total + trace * trace
            sample_bin(
                old_data, first, highs, times_ref, before * bins_y + b, b, old_scales, vals
            )
            if b % cut == 0:
                r = b // cut
                first = trace_row(r, highs)
                at = res_row * bins_y + res_part + r
                sample_bin(traces, first, highs, times_ref, at, r, res_scales, res_vals)
        both[...] = split_values(vals)
        res_both[...] = split_values(res_vals)
        old_data[current, :] = data_ref[pl.ds(pl.multiple_of(step * rows_per, SUB), rows_per), :]
        return total

    curv_ref[...] = lax.fori_loop(0, bins_x, one_row, jnp.zeros((highs, LANES), F32))
    last = bins_x - 1
    spread_image(last)
    spread_residual(last)
    for b in range(bins_y):
        at = last * bins_y + b
        sample_bin(old_data, trace_row(b, highs), highs, times_ref, at, b, scales, vals)
    both[...] = split_values(vals)
    spread_image(bins_x)
    for k in range(2):
        for x in range(wide_x):
            at = k * columns + x * wide_y
            out_left[k, x] = s_ref[pl.ds(at, RADIUS), :]
            out_mid[k, x] = s_ref[pl.ds(at + RADIUS, bins_y), :]
            out_right[k, x] = s_ref[pl.ds(at + RADIUS + bins_y, RADIUS), :]


def fold_y_kernel(mid_ref, low_ref, high_ref, out_head, out_mid, out_tail):
    wide_x, bins_y = mid_ref.shape[1], mid_ref.shape[2]
    bins_x = wide_x - 2 * RADIUS
    for k in range(2):
        for x in range(wide_x):
            if x < RADIUS:
                ref, at = out_head, x
            elif x < RADIUS + bins_x:
                ref, at = out_mid, x - RADIUS
            else:
                ref, at = out_tail, x - RADIUS - bins_x
            ref[k, at, pl.ds(0, RADIUS), :] = mid_ref[k, x, pl.ds(0, RADIUS), :] + low_ref[k, x]
            high = pl.ds(bins_y - RADIUS, RADIUS)
            ref[k, at, high, :] = mid_ref[k, x, high, :] + high_ref[k, x]


def fold_x_kernel(mid_ref, low_ref, high_ref, grad_ref, curv_ref, out_ref, stats_ref):
    bins_x = mid_ref.shape[1]
    sums = [jnp.zeros(mid_ref.shape[2:], F32) for _ in range(5)]
    for x in range(bins_x):
        pair = []
        for k in range(2):
            cells = mid_ref[k, x]
            if x < RADIUS:
                cells = cells + low_ref[k, x]
            else:
                cells = cells + high_ref[k, x - RADIUS]
            out_ref[k, x] = cells
            pair.append(cells)
        old = grad_ref[x]
        terms = (old * old, None, pair[0] * pair[0], pair[0] * pair[1], pair[1] * pair[1])
        for n, term in enumerate(terms):
            if term is not None:
                sums[n] = sums[n] + term
    sums[1] = curv_ref[...]
    sums = [jnp.sum(term, axis=0, keepdims=True) for term in sums]
    lane = lax.broadcasted_iota(jnp.int32, (1, LANES), 1)
    stats = jnp.zeros((1, LANES), F32)
    for n, term in enumerate(sums):
        stats = jnp.where(lane == n, jnp.sum(term, axis=1, keepdims=True), stats)
    stats_ref[...] = jnp.broadcast_to(stats[None], stats_ref.shape)


def last_kernel(
    stats_ref, res_ref, data_ref, model_ref, dir_ref, grad_ref, new_image, new_residual, new_dir
):
    stats = jnp.sum(stats_ref[...], axis=0)
    lane = lax.broadcasted_iota(jnp.int32, stats.shape, 1)

    def pick(n):
        return jnp.sum(jnp.where(lane == n, stats, 0.0), axis=1, keepdims=True)

    gamma, curvature, one_one, one_two, two_two = (pick(n) for n in range(5))
    alpha = gamma / curvature
    gamma_new = one_one - 2.0 * (alpha * one_two) + alpha * (alpha * two_two)
    beta = gamma_new / gamma
    new_residual[...] = res_ref[...] - alpha * data_ref[...]
    step = dir_ref[...]
    new_image[...] = model_ref[...] + alpha[None] * step
    new_dir[...] = (grad_ref[0] - alpha[None] * grad_ref[1]) + beta[None] * step


def shift(cells, axis, by):
    count = lax.axis_size(axis)
    pairs = [(i, i + by) for i in range(count) if 0 <= i + by < count]
    return lax.ppermute(cells, axis, pairs)


def body(
    model_image,
    data_residual,
    direction,
    old_gradient,
    aperture,
    travel_times,
    amplitude,
    trace_counts,
):
    bins_x, bins_y, samples = data_residual.shape
    entries, depths = travel_times.shape[2], travel_times.shape[3]
    highs = samples // LANES
    wide_x, wide_y = bins_x + 2 * RADIUS, bins_y + 2 * RADIUS
    columns = wide_x * wide_y
    span = SIDE * wide_y
    geo = (bins_y, entries, highs, wide_y)
    rows_per = bins_y * highs

    from_prev = shift(direction, "gx", 1)[bins_x - RADIUS :]
    from_next = shift(direction, "gx", -1)[:RADIUS]

    times = travel_times.reshape(bins_x * bins_y, entries, depths)
    res_rows = to_rows(data_residual)
    def first(row0, count, counts, limit):
        return pl.pallas_call(
            functools.partial(first_kernel, geo, row0),
            grid=(count,),
            in_specs=[
                pl.BlockSpec((rows_per, LANES), lambda i: (i + row0, 0)),
                pl.BlockSpec((bins_y, entries, depths), lambda i: (i + row0, 0, 0)),
                pl.BlockSpec((1, bins_y, entries), lambda i: (i + row0, 0, 0)),
                pl.BlockSpec((bins_x, bins_y), lambda i: (0, 0)),
                pl.BlockSpec((1, bins_y, entries), lambda i: (jnp.maximum(i - 1, 0) + row0, 0, 0)),
                pl.BlockSpec((1, bins_y, entries), lambda i: (i + row0, 0, 0)),
            ],
            out_specs=pl.BlockSpec((columns, depths), lambda i: (0, 0)),
            out_shape=jax.ShapeDtypeStruct((columns, depths), F32),
            scratch_shapes=[pltpu.VMEM((bins_y * entries, depths), F32)] * 2
            + [pltpu.VMEM((rows_per + SUB, LANES), F32)]
            + [pltpu.VMEM((bins_y * entries, 2 * depths), BF16)],
            compiler_params=params(limit),
            cost_estimate=pl.CostEstimate(
                flops=4 * 10**9, bytes_accessed=4 * 10**6, transcendentals=0
            ),
            name="sample_residual",
        )(res_rows, times, amplitude, counts, aperture, aperture)

    early = bins_x // 4
    row0 = 2 * early
    s1 = first(0, early, trace_counts, FIRST_LIMIT)
    ext = jnp.concatenate([from_prev, direction, from_next], axis=0)
    tail, head, s1, counts = lax.optimization_barrier(
        (ext[:, bins_y - RADIUS :], ext[:, :RADIUS], s1, trace_counts)
    )
    left = shift(tail, "gy", 1)
    right = shift(head, "gy", -1)
    s1_more = first(early, early - 1, counts, VMEM_LIMIT)

    cut = bins_x // (bins_x - row0)
    res_bins = bins_y // cut
    parts = trace_counts.reshape(bins_x * cut, res_bins)
    strip = jax.ShapeDtypeStruct((2, wide_x, RADIUS, depths), F32)
    vals_shape = pltpu.VMEM((bins_y * entries, depths), F32)
    res_shape = pltpu.VMEM((res_bins * entries, depths), F32)
    columns_shape = pltpu.VMEM((columns, depths), F32)
    in_vmem = pl.BlockSpec(memory_space=pltpu.VMEM)
    data_rows, curv, out_left, out_mid, out_right = pl.pallas_call(
        functools.partial(main_kernel, geo, row0),
        in_specs=[pl.BlockSpec(memory_space=pltpu.SMEM)] + [in_vmem] * 11,
        out_specs=[in_vmem] * 5,
        out_shape=[
            jax.ShapeDtypeStruct((bins_x * rows_per, LANES), F32),
            jax.ShapeDtypeStruct((highs, LANES), F32),
            strip,
            jax.ShapeDtypeStruct((2, wide_x, bins_y, depths), F32),
            strip,
        ],
        scratch_shapes=[columns_shape, pltpu.VMEM((2 * columns, depths), F32)]
        + [vals_shape, res_shape, vals_shape, vals_shape, res_shape]
        + [pltpu.VMEM((rows_per + SUB, LANES), F32)]
        + [pltpu.VMEM((bins_y * entries, 2 * depths), BF16)]
        + [pltpu.VMEM((res_bins * entries, 2 * depths), BF16)]
        + [pltpu.VMEM((res_bins * highs + SUB, LANES), F32)]
        + [pltpu.VMEM((4, entries + SUB, LANES), F32)] * bins_y,
        compiler_params=params(MAIN_LIMIT),
        cost_estimate=pl.CostEstimate(
            flops=20 * 10**9, bytes_accessed=8 * 10**6, transcendentals=0
        ),
        name="demigrate_and_sample",
    )(
        aperture,
        times,
        amplitude,
        trace_counts,
        parts,
        aperture,
        res_rows,
        ext,
        left,
        right,
        s1,
        s1_more,
    )

    from_low = shift(out_right, "gy", 1)
    from_high = shift(out_left, "gy", -1)
    edge = jax.ShapeDtypeStruct((2, RADIUS, bins_y, depths), F32)
    out_head, inner, out_tail = pl.pallas_call(
        fold_y_kernel,
        out_shape=[edge, jax.ShapeDtypeStruct((2, bins_x, bins_y, depths), F32), edge],
        compiler_params=params(SMALL_LIMIT),
        name="fold_y",
    )(out_mid, from_low, from_high)
    from_low = shift(out_tail, "gx", 1)
    from_high = shift(out_head, "gx", -1)
    devices = lax.axis_size("gx") * lax.axis_size("gy")
    grads, stats = pl.pallas_call(
        fold_x_kernel,
        out_shape=[
            jax.ShapeDtypeStruct((2, bins_x, bins_y, depths), F32),
            jax.ShapeDtypeStruct((devices, 1, LANES), F32),
        ],
        compiler_params=params(SMALL_LIMIT),
        name="fold_x",
    )(inner, from_low, from_high, old_gradient, curv)
    stats = lax.all_to_all(stats, ("gx", "gy"), 0, 0, tiled=True)

    steps = 2
    rows_step = bins_x * rows_per // steps
    x_step = bins_x // steps
    cells = pl.BlockSpec((x_step, bins_y, depths), lambda i: (i, 0, 0))
    rows = pl.BlockSpec((rows_step, LANES), lambda i: (i, 0))
    image_shape = jax.ShapeDtypeStruct(direction.shape, F32)
    new_image, new_rows, new_direction = pl.pallas_call(
        last_kernel,
        grid=(steps,),
        in_specs=[
            pl.BlockSpec(stats.shape, lambda i: (0, 0, 0)),
            rows,
            rows,
            cells,
            cells,
            pl.BlockSpec((2, x_step, bins_y, depths), lambda i: (0, i, 0, 0)),
        ],
        out_specs=[cells, rows, cells],
        out_shape=[image_shape, jax.ShapeDtypeStruct(res_rows.shape, F32), image_shape],
        compiler_params=params(SMALL_LIMIT),
        name="update",
    )(stats, res_rows, data_rows, model_image, direction, grads)
    return (new_image, from_rows(new_rows, data_residual.shape), new_direction)


def solution(mesh):
    in_specs = (
        P("gx", "gy", None),
        P("gx", "gy", None),
        P("gx", "gy", None),
        P("gx", "gy", None),
        P("gx", "gy", None),
        P("gx", "gy", None, None),
        P("gx", "gy", None),
        P("gx", "gy"),
    )
    out_specs = (P("gx", "gy", None), P("gx", "gy", None), P("gx", "gy", None))
    return jax.shard_map(body, mesh=mesh, in_specs=in_specs, out_specs=out_specs, check_vma=False)
```
